32 devices in a mesh: groups: 2 (over x), tensor: 8 (over z, y), dp: 2 (over core).
Axes of the slice: x: 2, y: 2, z: 4, core: 2. Of those that a mesh axis runs over, the one named last changes fastest.
Arguments:
- cotangent: bfloat16 [2048, 5120], P(('groups', 'dp', 'tensor')), parts along dimension 0, may hold values from -6 to 6
- gate_activation_stored: bfloat16 [2048, 25600], P(('groups', 'dp'), 'tensor'), parts along dimension 0, may hold values from -6 to 6
- up_activation_stored: bfloat16 [2048, 25600], P(('groups', 'dp'), 'tensor'), parts along dimension 0, may hold values from -6 to 6
- gate_matrix: bfloat16 [5120, 25600], P('dp', 'tensor'), may hold values from -0.078125 to 0.078125
- up_matrix: bfloat16 [5120, 25600], P('dp', 'tensor'), may hold values from -0.078125 to 0.078125
- down_matrix: bfloat16 [5120, 25600], P('dp', 'tensor'), may hold values from -0.0390625 to 0.0390625
- adapter_input_factor: bfloat16 [6, 25600, 64], P(None, 'tensor'), may hold values from -0.0390625 to 0.0390625
- adapter_output_factor: bfloat16 [6, 64, 5120], P(None, None, 'tensor'), may hold values from -0.078125 to 0.078125
- padded_block_segment: int32 [16], P('groups'), parts along dimension 0, may hold values from 0 to 5, never falling along the last dimension, each value on 1 to 2 neighbouring positions
- segment_adapter_index: int32 [12, 1], P('groups'), parts along dimension 0, may hold values from 0 to 5
- adapter_grad_slot: int32 [6], replicated, may hold values from 0 to 5, each once
Outputs:
- input_grad: bfloat16 [2048, 5120], P(('groups', 'dp', 'tensor')), parts along dimension 0
- grad_a: bfloat16 [12, 25600, 64], P(('groups', 'dp'), 'tensor'), parts along dimension 0
- grad_b: bfloat16 [12, 64, 5120], P(('groups', 'dp'), None, 'tensor'), parts along dimension 0
The draws below stay inside these ranges and needn't reach their ends.
There are 2 independent parts, one for each index of `groups`. The reference program is written for one: setup_inputs(seed, part) draws one part's arguments, and reference() takes and returns one part's arrays. A program takes and returns all parts, laid end to end along the dimension named above; an argument that names none is the same for every part. Nothing has to cross between parts.
Inputs may be any that keep to these rules, and one draw needn't show every extreme that they name: padded_block_segment never falls; each segment holds 1 to 2 blocks. `segment_adapter_index`: every adapter is named by some segment. `adapter_grad_slot`: each slot is named once.
All inputs are finite; a program needn't handle non-finite values.
Results may differ from the reference program's by a relative error of at most 0.007.
Values may be sent and summed in bfloat16 or wider, within the bound.
No kernel may reach another device: no remote copies, remote signals or barrier semaphores. Data moves between devices by JAX's collectives and lax.ppermute only.
A program may use at most 384 MiB of HBM per device.

```python
import math
import jax
import jax.numpy as jnp
import numpy as np
from jax import lax

MODEL_WIDTH = 5120
HIDDEN_UNITS = 25600
ADAPTER_RANK = 64
BLOCK = 128
TOKENS = 1024
BLOCKS = 8
SEGS = 6
ADAPTER_COUNT = 6


def block_scale(rng, extent, cuts, smallest, high):
    def one(axis_at, parts):
        draws = jax.random.uniform(jax.random.fold_in(jax.random.fold_in(rng, 6), axis_at), (parts,), jnp.float32, smallest / len(cuts), high / len(cuts))
        return jnp.repeat(jnp.exp(draws), extent[axis_at] // parts).reshape((-1,) + (1,) * (len(extent) - axis_at - 1))

    factor_of = one(*cuts[0])
    for cut in cuts[1:]:
        factor_of = factor_of * one(*cut)
    return factor_of


def distinct(stream_key, rows, count, top, lift):
    order = jax.random.permutation(jax.random.fold_in(stream_key, 1), count)
    boost = order
    for power in range(3):
        boost = boost * boost // count
    boost = boost * lift // count
    chance = jax.random.randint(jax.random.fold_in(stream_key, 2), (rows, count), 0, 4096) + boost
    holders = jax.random.permutation(jax.random.fold_in(stream_key, 3), rows)[jnp.arange(count) % rows]
    chance = jnp.where(jnp.arange(rows)[:, None] == holders[None, :], 1 << 14, chance)
    priority = chance * count + jnp.arange(count)
    return lax.top_k(priority.astype(jnp.int32), top)[1].astype(jnp.int32)


def split_up(amount, total, limit, lean):
    portions = [(1 << 20) // math.isqrt(standing ** lean) + 1 for standing in range(2, amount + 1)]
    rest, holding = total - limit - (amount - 1), [1] * (amount - 1)
    while rest > 0:
        free = [i for i in range(amount - 1) if holding[i] < limit]
        mass, left = sum([portions[i] for i in free]), rest
        for i in free:
            more = min(limit - holding[i], max(1, left * portions[i] // mass), rest)
            holding[i] = holding[i] + more
            rest = rest - more
    return np.array([limit] + holding)


def uneven(key, number_of, total, reach, skew):
    if number_of == 2:
        one = jax.random.randint(key, (), max(1, total - reach), min(reach, total - 1) + 1)
        return jnp.stack([one, total - one])
    lengths = jnp.asarray(split_up(number_of, total, reach, skew), jnp.int32)
    couples = (number_of - 1) // 2
    giver, receiver = lengths[1:1 + 2 * couples:2], lengths[2:2 + 2 * couples:2]
    slack = jnp.minimum(giver - 1, reach - receiver)
    moved = jax.random.randint(jax.random.fold_in(key, 1), (couples,), 0, 1 << 20) % (slack + 1)
    lengths = lengths.at[1:1 + 2 * couples:2].set(giver - moved).at[2:2 + 2 * couples:2].set(receiver + moved)
    return lengths[jax.random.permutation(jax.random.fold_in(key, 2), number_of)]


def bell_draw(key, dims, deviation, most, pieces=(), dtype=jnp.bfloat16):
    level = block_scale(key, dims, pieces, -0.22, 0.18) if pieces else 1.0
    array = jax.random.normal(key, dims, jnp.float32) * deviation * level
    return jnp.minimum(jnp.maximum(array, -most), most).astype(dtype)


def setup_inputs(seed: int = 0, part: int = 0) -> dict:
    streams_of = jax.random.split(jax.random.key(seed), 12)
    own_keys = jax.random.split(jax.random.fold_in(streams_of[11], part), 12)
    cotangent = bell_draw(own_keys[0], (TOKENS, MODEL_WIDTH), 1.0, 6.0, ((0, 16),))
    gate_activation_stored = bell_draw(own_keys[1], (TOKENS, HIDDEN_UNITS), 1.5, 6.0, ((0, 2), (1, 8)))
    up_activation_stored = bell_draw(own_keys[2], (TOKENS, HIDDEN_UNITS), 1.0, 6.0, ((0, 2), (1, 8)))
    gate_matrix = bell_draw(streams_of[3], (MODEL_WIDTH, HIDDEN_UNITS), MODEL_WIDTH ** -0.5, 0.078125, ((0, 2), (1, 8)))
    up_matrix = bell_draw(streams_of[4], (MODEL_WIDTH, HIDDEN_UNITS), MODEL_WIDTH ** -0.5, 0.078125, ((0, 2), (1, 8)))
    down_matrix = bell_draw(streams_of[5], (MODEL_WIDTH, HIDDEN_UNITS), HIDDEN_UNITS ** -0.5, 0.0390625, ((0, 2), (1, 8)))
    adapter_input_factor = bell_draw(streams_of[6], (ADAPTER_COUNT, HIDDEN_UNITS, ADAPTER_RANK), HIDDEN_UNITS ** -0.5, 0.0390625, ((1, 8),))
    adapter_output_factor = bell_draw(streams_of[7], (ADAPTER_COUNT, ADAPTER_RANK, MODEL_WIDTH), MODEL_WIDTH ** -0.5, 0.078125, ((2, 8),))
    padded_block_segment = jnp.searchsorted(jnp.cumsum(uneven(own_keys[8], SEGS, BLOCKS, 2, 1)), jnp.arange(BLOCKS), side="right").astype(jnp.int32)
    segment_adapter_index = distinct(own_keys[9], SEGS, ADAPTER_COUNT, 1, 1365)
    adapter_grad_slot = jax.random.permutation(streams_of[10], ADAPTER_COUNT).astype(jnp.int32)
    return dict(cotangent=cotangent, gate_activation_stored=gate_activation_stored, up_activation_stored=up_activation_stored, gate_matrix=gate_matrix, up_matrix=up_matrix, down_matrix=down_matrix, adapter_input_factor=adapter_input_factor, adapter_output_factor=adapter_output_factor, padded_block_segment=padded_block_segment, segment_adapter_index=segment_adapter_index, adapter_grad_slot=adapter_grad_slot)


ADAPTER_SCALE = 2.0


def reference(cotangent, gate_activation_stored, up_activation_stored, gate_matrix, up_matrix, down_matrix, adapter_input_factor, adapter_output_factor, padded_block_segment, segment_adapter_index, adapter_grad_slot):
    gate = gate_activation_stored.astype(jnp.float32)
    upper = up_activation_stored.astype(jnp.float32)
    sigmoid_gate = jax.nn.sigmoid(gate)
    silu_gate = gate * sigmoid_gate
    hidden_state = (silu_gate * upper).astype(jnp.bfloat16)
    block_adapter = segment_adapter_index[:, 0][padded_block_segment]
    token_adapter = jnp.repeat(block_adapter, BLOCK)
    lowrank_input = jnp.zeros((TOKENS, ADAPTER_RANK), jnp.float32)
    lowrank_output = jnp.zeros((TOKENS, ADAPTER_RANK), jnp.float32)
    for selected_index in range(ADAPTER_COUNT):
        membership = (token_adapter == selected_index)[:, None]
        lowrank_input = lowrank_input + jnp.where(membership, jnp.dot(hidden_state, adapter_input_factor[selected_index], preferred_element_type=jnp.float32), 0.0)
        lowrank_output = lowrank_output + jnp.where(membership, jnp.dot(cotangent, adapter_output_factor[selected_index].T, preferred_element_type=jnp.float32), 0.0)
    lowrank_input = lowrank_input.astype(jnp.bfloat16)
    lowrank_output = lowrank_output.astype(jnp.bfloat16)
    hidden_gradient = jnp.dot(cotangent, down_matrix, preferred_element_type=jnp.float32)
    input_factor_grads = []
    output_factor_grads = []
    for selected_index in range(ADAPTER_COUNT):
        membership = (token_adapter == selected_index)[:, None]
        additional_term = jnp.dot(lowrank_output, adapter_input_factor[selected_index].T, preferred_element_type=jnp.float32)
        hidden_gradient = hidden_gradient + ADAPTER_SCALE * jnp.where(membership, additional_term, 0.0)
        masked_output = jnp.where(membership, lowrank_output, jnp.zeros_like(lowrank_output))
        masked_input = jnp.where(membership, lowrank_input, jnp.zeros_like(lowrank_input))
        input_factor_grads.append(ADAPTER_SCALE * jnp.dot(hidden_state.T, masked_output, preferred_element_type=jnp.float32))
        output_factor_grads.append(ADAPTER_SCALE * jnp.dot(masked_input.T, cotangent, preferred_element_type=jnp.float32))
    gate_grad = (hidden_gradient * upper * sigmoid_gate * (1.0 + gate * (1.0 - sigmoid_gate))).astype(jnp.bfloat16)
    up_grad = (hidden_gradient * silu_gate).astype(jnp.bfloat16)
    input_grad = (jnp.dot(gate_grad, gate_matrix.T, preferred_element_type=jnp.float32) + jnp.dot(up_grad, up_matrix.T, preferred_element_type=jnp.float32)).astype(jnp.bfloat16)
    stack_a = jnp.stack(input_factor_grads)
    stack_b = jnp.stack(output_factor_grads)
    grad_a = jnp.zeros_like(stack_a).at[adapter_grad_slot].set(stack_a).astype(jnp.bfloat16)
    grad_b = jnp.zeros_like(stack_b).at[adapter_grad_slot].set(stack_b).astype(jnp.bfloat16)
    return input_grad, grad_a, grad_b
```

```python
import functools

import jax
import jax.numpy as jnp
from jax import lax
from jax.experimental import pallas as pl
from jax.experimental.pallas import tpu as pltpu
from jax.sharding import PartitionSpec as P

BLOCK = 128


ADAPTER_SCALE = 2.0

F32 = jnp.float32
BF16 = jnp.bfloat16
MIB = 1024 * 1024

Y_SWAP = [(t, t ^ 1) for t in range(8)]
PAIR = [(t, t ^ 2) for t in range(8)]
FAR = [(t, t ^ 4) for t in range(8)]
MID = [(2, 4), (3, 5), (4, 2), (5, 3)]
OUTWARD = [(2, 0), (3, 1), (4, 6), (5, 7)]
INWARD = [(0, 2), (1, 3), (6, 4), (7, 5)]
CORES = [(0, 1), (1, 0)]

M_T, M_Y, M_D, M_Z, M_SLOT_ADAPTER, M_ADAPTER, M_GRAD_SLOT = 0, 1, 2, 3, 7, 11, 15


def nt_dot(a, b):
    return lax.dot_general(a, b, (((1,), (1,)), ((), ())), preferred_element_type=F32)


def tn_dot(a, b):
    return lax.dot_general(a, b, (((0,), (0,)), ((), ())), preferred_element_type=F32)


def call(
    kernel, meta, args, grid, in_specs, out_specs, out_shape, scratch=(), flops=0, nbytes=0, vmem=48, after=()
):
    first, extra = len(args), len(after)

    def run(m, *refs):
        kernel(m, *refs[:first], *refs[first + extra :])

    return pl.pallas_call(
        run,
        grid_spec=pltpu.PrefetchScalarGridSpec(
            num_scalar_prefetch=1,
            grid=grid,
            in_specs=list(in_specs) + [pl.BlockSpec(memory_space=pl.ANY)] * extra,
            out_specs=out_specs,
            scratch_shapes=list(scratch),
        ),
        out_shape=out_shape,
        compiler_params=pltpu.CompilerParams(vmem_limit_bytes=vmem * MIB),
        cost_estimate=pl.CostEstimate(flops=flops, bytes_accessed=nbytes, transcendentals=0),
    )(meta, *args, *after)


def pack_halves(p):
    h = p.shape[0] // 2
    return jnp.concatenate([p[:h], p[h:]], axis=1)


def unpack_halves(p):
    h = p.shape[1] // 2
    return jnp.concatenate([p[:, :h], p[:, h:]], axis=0)


def hidden_kernel(m, gate_ref, up_ref, a_ref, hidden_ref, low_ref):
    g = gate_ref[...].astype(F32)
    hidden = (g * jax.nn.sigmoid(g) * up_ref[...].astype(F32)).astype(BF16)
    hidden_ref[...] = hidden
    low_ref[...] = pack_halves(nt_dot(hidden, a_ref[0]))


def hidden_and_low_in(meta, gate_act, up_act, a_t):
    rows, width = gate_act.shape
    rank = a_t.shape[1]
    blocks = rows // BLOCK
    return call(
        hidden_kernel,
        meta,
        (gate_act, up_act, a_t),
        (blocks,),
        [
            pl.BlockSpec((BLOCK, width), lambda b, m: (b, 0)),
            pl.BlockSpec((BLOCK, width), lambda b, m: (b, 0)),
            pl.BlockSpec((1, rank, width), lambda b, m: (m[M_ADAPTER + b], 0, 0)),
        ],
        [
            pl.BlockSpec((BLOCK, width), lambda b, m: (b, 0)),
            pl.BlockSpec((BLOCK // 2, 2 * rank), lambda b, m: (b, 0)),
        ],
        [
            jax.ShapeDtypeStruct((rows, width), BF16),
            jax.ShapeDtypeStruct((rows // 2, 2 * rank), F32),
        ],
        flops=2 * rows * width * rank * 2,
        nbytes=8 * rows * width,
    )


def low_out_kernel(m, *refs):
    shards, b_ref, cols_ref, low_ref = refs[:8], refs[8], refs[9], refs[10]
    rows = shards[0].shape[0]
    y = m[M_Y]
    for s in range(4):
        z = m[M_Z + s]
        own, other = shards[2 * s][...], shards[2 * s + 1][...]
        first = jnp.where(y == 0, own, other)
        second = jnp.where(y == 0, other, own)
        tokens = jnp.concatenate([first, second], axis=0)
        cols_ref[pl.ds(pl.multiple_of(z * 2 * rows, 2 * rows), 2 * rows), :] = tokens
        part = nt_dot(tokens, b_ref[m[M_SLOT_ADAPTER + s]])
        low_ref[pl.ds(pl.multiple_of(z * rows, rows), rows), :] = pack_halves(part)


def low_out_parts(meta, shards, b, after):
    rows = shards[0].shape[0]
    adapters, rank, columns = b.shape
    return call(
        low_out_kernel,
        meta,
        (*shards, b),
        (1,),
        [pl.BlockSpec((rows, columns), lambda i, m: (0, m[M_T]))] * 8
        + [pl.BlockSpec((adapters, rank, columns), lambda i, m: (0, 0, 0))],
        [
            pl.BlockSpec((8 * rows, columns), lambda i, m: (0, 0)),
            pl.BlockSpec((4 * rows, 2 * rank), lambda i, m: (0, 0)),
        ],
        [
            jax.ShapeDtypeStruct((8 * rows, columns), BF16),
            jax.ShapeDtypeStruct((4 * rows, 2 * rank), F32),
        ],
        flops=2 * 8 * rows * columns * rank,
        nbytes=4 * 8 * rows * columns,
        after=after,
    )


def hidden_grad_kernel(count, m, *refs):
    mine, other = refs[:count], refs[count : 2 * count]
    down_mine, down_other, out_ref, lhs = refs[2 * count :]
    rows = mine[0].shape[0]

    @pl.when(pl.program_id(0) == 0)
    def _():
        for s in range(count):
            lhs[0, s * rows : (s + 1) * rows] = mine[s][...]
            lhs[1, s * rows : (s + 1) * rows] = other[s][...]

    total = jnp.dot(lhs[0], down_mine[...], preferred_element_type=F32)
    out_ref[...] = total + jnp.dot(lhs[1], down_other[...], preferred_element_type=F32)


def hidden_grad(meta, shards, mine, other, span, after=()):
    rows = shards[0].shape[0]
    half = mine.shape[0]
    start, width, step = span
    count = len(shards)
    total = rows * count
    return call(
        functools.partial(hidden_grad_kernel, count),
        meta,
        (*shards, *shards, mine, other),
        (width // step,),
        [pl.BlockSpec((rows, half), lambda n, m: (0, m[M_D]))] * count
        + [pl.BlockSpec((rows, half), lambda n, m: (0, 1 - m[M_D]))] * count
        + [pl.BlockSpec((half, step), lambda n, m: (0, n + start // step))] * 2,
        pl.BlockSpec((total, step), lambda n, m: (0, n)),
        jax.ShapeDtypeStruct((total, width), F32),
        scratch=[pltpu.VMEM((2, total, half), BF16)],
        flops=2 * total * 2 * half * width,
        nbytes=2 * 2 * half * width,
        after=after,
    )


def act_grad_kernel(spans, m, *refs):
    hg_refs, (gate_ref, up_ref, low_ref, a_ref, out_ref) = refs[: len(spans)], refs[len(spans) :]
    j = pl.program_id(0)
    y = m[M_Y]
    rank = low_ref.shape[1] // 2
    second = jnp.where(j == 0, y, 1 - y) == 1
    low = jnp.where(second, low_ref[:, rank:], low_ref[:, :rank])
    for hg_ref, (start, width, _) in zip(hg_refs, spans):
        at = slice(start, start + width)
        hg = hg_ref[...] + ADAPTER_SCALE * jnp.dot(low, a_ref[0, :, at], preferred_element_type=F32)
        g = gate_ref[:, at].astype(F32)
        u = up_ref[:, at].astype(F32)
        sig = jax.nn.sigmoid(g)
        out_ref[0, :, at] = (hg * u * sig * (1.0 + g * (1.0 - sig))).astype(BF16)
        out_ref[1, :, at] = (hg * (g * sig)).astype(BF16)


def act_grad(meta, slot, spans, hgs, gate_act, up_act, low, a_t, after=()):
    rank, width = a_t.shape[1:]
    rows = BLOCK // 2

    def shard_of(j, m):
        y = m[M_Y]
        return (m[M_Z + slot] * 2 + y + j * (1 - 2 * y), 0)

    return call(
        functools.partial(act_grad_kernel, spans),
        meta,
        (*hgs, gate_act, up_act, low, a_t),
        (2,),
        [pl.BlockSpec((rows, w), lambda j, m: ((slot % 2) * 2 + j, 0)) for _, w, _ in spans]
        + [
            pl.BlockSpec((rows, width), shard_of),
            pl.BlockSpec((rows, width), shard_of),
            pl.BlockSpec((rows, 2 * rank), lambda j, m: (m[M_Z + slot], 0)),
            pl.BlockSpec((1, rank, width), lambda j, m: (m[M_SLOT_ADAPTER + slot], 0, 0)),
        ],
        pl.BlockSpec((2, rows, width), lambda j, m: (0, j, 0)),
        jax.ShapeDtypeStruct((2, 2 * rows, width), BF16),
        flops=2 * 2 * rows * width * rank,
        nbytes=2 * rows * width * 12,
        after=after,
    )


def input_grad_kernel(m, mine_ref, other_ref, gate_ref, up_ref, keep_ref, send_ref, lhs):
    rows = mine_ref.shape[1] // 2

    @pl.when(pl.program_id(0) == 0)
    def _():
        for i in range(2):
            for y in range(2):
                lhs[i, (2 * y) * rows : (2 * y + 1) * rows] = mine_ref[i, y * rows : (y + 1) * rows]
                lhs[i, (2 * y + 1) * rows : (2 * y + 2) * rows] = other_ref[i, y * rows : (y + 1) * rows]

    total = nt_dot(lhs[0], gate_ref[...]) + nt_dot(lhs[1], up_ref[...])
    keep_ref[...] = total[: 2 * rows].astype(BF16)
    send_ref[...] = total[2 * rows :].astype(BF16)


def input_grad_parts(meta, mine, other, gate, up, after=()):
    rows, width = mine.shape[1:]
    half = gate.shape[0]
    step = 512
    out = jax.ShapeDtypeStruct((rows, half), BF16)
    return call(
        input_grad_kernel,
        meta,
        (mine, other, gate, up),
        (half // step,),
        [pl.BlockSpec((2, rows, width), lambda n, m: (0, 0, 0))] * 2
        + [pl.BlockSpec((step, width), lambda n, m: (n, 0))] * 2,
        [pl.BlockSpec((rows, step), lambda n, m: (0, n))] * 2,
        [out, out],
        scratch=[pltpu.VMEM((2, 2 * rows, width), BF16)],
        flops=2 * 2 * rows * 2 * width * half,
        nbytes=2 * 2 * width * half,
        after=after,
    )


def owner_kernel(blocks, m, low_ref, features_ref, keep_ref, send_ref):
    i = pl.program_id(0)
    d = m[M_D]
    owned = keep_ref.shape[0] * pl.num_programs(0)
    rows = low_ref.shape[0] // blocks
    for ref, owner in ((keep_ref, d), (send_ref, 1 - d)):
        slot = owner * owned + i
        total = jnp.zeros(ref.shape[1:], F32)
        for b in range(blocks):
            hit = jnp.where(m[M_GRAD_SLOT + b] == slot, ADAPTER_SCALE, 0.0)
            low = unpack_halves(low_ref[b * rows : (b + 1) * rows, :])
            total += hit * tn_dot(low, features_ref[b * BLOCK : (b + 1) * BLOCK, :])
        ref[0] = total.astype(BF16)


def owner_grads(meta, low, features, owned, after=()):
    tokens, width = features.shape
    half_rows, double = low.shape
    rank = double // 2
    out = jax.ShapeDtypeStruct((owned, rank, width), BF16)
    return call(
        functools.partial(owner_kernel, tokens // BLOCK),
        meta,
        (low, features),
        (owned,),
        [
            pl.BlockSpec((half_rows, double), lambda i, m: (0, 0)),
            pl.BlockSpec((tokens, width), lambda i, m: (0, 0)),
        ],
        [pl.BlockSpec((1, rank, width), lambda i, m: (i, 0, 0))] * 2,
        [out, out],
        flops=2 * tokens * rank * width * 2 * owned,
        nbytes=2 * tokens * width,
        after=after,
    )


def add_kernel(count, m, *refs):
    total = refs[0][...].astype(F32)
    for r in refs[1:count]:
        total += r[...].astype(F32)
    for r in refs[count:]:
        r[...] = total.astype(r.dtype)


def add_after(meta, xs, after, kinds=(BF16,), steps=1):
    rows, width = xs[0].shape
    spec = pl.BlockSpec((rows // steps, width), lambda i, m: (i, 0))
    out = call(
        functools.partial(add_kernel, len(xs)),
        meta,
        xs,
        (steps,),
        [spec] * len(xs),
        [spec] * len(kinds),
        [jax.ShapeDtypeStruct((rows, width), k) for k in kinds],
        nbytes=2 * rows * width * (len(xs) + 1),
        vmem=16,
        after=after,
    )
    return out if len(kinds) > 1 else out[0]


def add(*xs):
    return functools.reduce(jnp.add, [x.astype(F32) for x in xs]).astype(BF16)


def tied(x, *others):
    return lax.optimization_barrier((x, *others))[0]


def grid_body(
    cotangent,
    gate_act,
    up_act,
    gate_matrix,
    up_matrix,
    down_matrix,
    adapter_input_factor,
    adapter_output_factor,
    padded_block_segment,
    segment_adapter_index,
    adapter_grad_slot,
):
    adapters = adapter_input_factor.shape[0]
    blocks = gate_act.shape[0] // BLOCK
    d = lax.axis_index("dp")
    t = lax.axis_index("tensor")
    z, y = t // 2, t % 2
    low_side = z < 2
    slots_z = jnp.stack([z, z ^ 1, jnp.where(low_side, 2, 1), jnp.where(low_side, 3, 0)])
    segments_here = lax.dynamic_slice_in_dim(padded_block_segment, d * blocks, blocks)

    def pick(table, index):
        hit = index[:, None] == jnp.arange(table.shape[0], dtype=jnp.int32)[None, :]
        return jnp.sum(jnp.where(hit, table[None, :], 0), axis=1)

    block_adapter = pick(segment_adapter_index[:, 0], segments_here)
    meta = jnp.concatenate(
        [
            jnp.stack([t, y, d]),
            slots_z,
            pick(block_adapter, slots_z),
            block_adapter,
            pick(adapter_grad_slot, block_adapter),
        ]
    ).astype(jnp.int32)
    a_t = jnp.swapaxes(adapter_input_factor, 1, 2)
    send = functools.partial(lax.ppermute, axis_name="tensor")
    swap_cores = functools.partial(lax.ppermute, axis_name="dp", perm=CORES)
    at_end = (z == 0) | (z == 3)

    width = gate_act.shape[1]
    step = width * 2 // 5
    spans = ((0, step, step // 5), (step, step, step // 5), (2 * step, width - 2 * step, width - 2 * step))

    down_other = swap_cores(down_matrix)
    pair = send(cotangent, perm=PAIR)
    mid = send(cotangent, perm=MID)
    y0 = send(cotangent, perm=Y_SWAP)
    hidden, low_in = hidden_and_low_in(meta, gate_act, up_act, a_t)
    y1 = send(tied(pair, y0, low_in), perm=Y_SWAP)
    pair_mid = send(tied(pair, low_in), perm=MID)
    mid_out = send(tied(mid, low_in), perm=OUTWARD)
    slot2 = jnp.where(at_end, mid_out, mid)
    y2 = send(tied(slot2, y1), perm=Y_SWAP)
    far_out = send(pair_mid, perm=OUTWARD)
    hg_near, last = [], (low_in,)
    for span in spans:
        hg_near.append(hidden_grad(meta, (cotangent, y0, pair, y1), down_matrix, down_other, span, last))
        last = (hg_near[-1],)
    slot3 = jnp.where(at_end, tied(far_out, hg_near[0]), pair_mid)
    y3 = send(tied(slot3, y2), perm=Y_SWAP)

    far = (slot2, y2, slot3, y3)
    columns, low_part = low_out_parts(meta, (cotangent, y0, pair, y1, *far), adapter_output_factor, last)
    hg_far = []
    low_sum, low_out = low_part, low_part.astype(BF16)
    for perm, span in zip((Y_SWAP, PAIR, FAR), spans):
        got = send(low_out, perm=perm)
        hg_far.append(hidden_grad(meta, far, down_matrix, down_other, span, (low_out,)))
        low_sum, low_out = add_after(meta, (low_sum, got), (hg_far[-1],), (F32, BF16))

    def grads(slot, after):
        hgs = hg_far if slot >= 2 else hg_near
        return act_grad(meta, slot, spans, hgs, gate_act, up_act, low_out, a_t, after)

    def parts(mine, other, after):
        keep, give = input_grad_parts(meta, mine, other, gate_matrix, up_matrix, after)
        return keep, send(give, perm=Y_SWAP), give

    mine3 = grads(3, ())
    low_in1 = low_in.astype(BF16)
    got_in = send(low_in1, perm=Y_SWAP)
    other3 = swap_cores(mine3)
    mine2 = grads(2, (mine3,))
    other2 = swap_cores(mine2)
    low_in2, low_in2b = add_after(meta, (low_in, got_in), (mine2,), (F32, BF16))
    got_in = send(low_in2b, perm=PAIR)
    keep3, got3, give3 = parts(mine3, other3, (low_in2b,))
    mine1 = grads(1, (give3,))
    other1 = swap_cores(mine1)
    low_in3, low_in3b = add_after(meta, (low_in2, got_in), (mine1,), (F32, BF16))
    got_in = send(low_in3b, perm=FAR)
    keep2, got2, give2 = parts(mine2, other2, (low_in3b,))
    mine0 = grads(0, (give2,))
    other0 = swap_cores(mine0)
    sum3 = add_after(meta, (keep3, got3), (mine0,))
    far_in = send(sum3, perm=INWARD)
    keep1, got1, give1 = parts(mine1, other1, (sum3,))
    sum2 = add_after(meta, (keep2, got2), (give1,))
    mid_in = send(sum2, perm=INWARD)
    far_mid = send(add_after(meta, (sum3, far_in), (sum2,)), perm=MID)
    low_in4 = add_after(meta, (low_in3, got_in), (sum2,))
    keep0, got0, give0 = parts(mine0, other0, (low_in4, sum2))
    from_mid = send(add_after(meta, (sum2, mid_in), (give0,)), perm=MID)
    from_pair = send(add_after(meta, (keep1, got1, far_mid), (give0,)), perm=PAIR)
    owned = adapters // 2
    keep_a, give_a = owner_grads(meta, low_out, hidden, owned, (give0,))
    keep_b, give_b = owner_grads(meta, low_in4, columns, owned, (keep_a,))
    grad_a = jnp.swapaxes(add(keep_a, swap_cores(give_a)), 1, 2)
    grad_b = add(keep_b, swap_cores(give_b))
    final = add_after(meta, (keep0, got0, from_pair, from_mid), (keep_b,))
    own_rows = cotangent.shape[0]
    got = swap_cores(final[own_rows:])
    own = final[:own_rows]
    input_grad = jnp.where(
        d == 0, jnp.concatenate([own, got], axis=1), jnp.concatenate([got, own], axis=1)
    )
    return (input_grad, grad_a, grad_b)


def body(
    cotangent,
    gate_activation_stored,
    up_activation_stored,
    gate_matrix,
    up_matrix,
    down_matrix,
    adapter_input_factor,
    adapter_output_factor,
    padded_block_segment,
    segment_adapter_index,
    adapter_grad_slot,
):
    local_token_rows = gate_activation_stored.shape[0]
    local_hidden_units = gate_activation_stored.shape[1]
    adapter_list = adapter_input_factor.shape[0]
    local_columns = adapter_output_factor.shape[2]
    seg_count = segment_adapter_index.shape[0]
    block_count = local_token_rows // BLOCK
    dp_index = lax.axis_index("dp")
    tensor_index = lax.axis_index("tensor")
    grad_all = lax.all_gather(cotangent, "tensor", axis=0, tiled=True)
    segments_here = lax.dynamic_slice_in_dim(
        padded_block_segment, dp_index * block_count, block_count
    )
    seg_onehot = (segments_here[:, None] == jnp.arange(seg_count, dtype=jnp.int32)[None, :]).astype(
        jnp.float32
    )
    adapter_onehot = (
        segment_adapter_index[:, 0][:, None] == jnp.arange(adapter_list, dtype=jnp.int32)[None, :]
    ).astype(jnp.float32)
    block_onehot = jnp.dot(seg_onehot, adapter_onehot)
    block_selector = block_onehot.astype(jnp.bfloat16)
    gate = gate_activation_stored.astype(jnp.float32)
    upper = up_activation_stored.astype(jnp.float32)
    sigmoid_gate = jax.nn.sigmoid(gate)
    silu_gate = gate * sigmoid_gate
    hidden_state = (silu_gate * upper).astype(jnp.bfloat16)
    hidden_blocks = hidden_state.reshape(block_count, BLOCK, local_hidden_units)
    cols_mine = lax.dynamic_slice_in_dim(grad_all, tensor_index * local_columns, local_columns, 1)
    cols_blocks = cols_mine.reshape(block_count, BLOCK, local_columns)
    a_blocks = jnp.einsum(
        "yz,zuo->yuo", block_selector, adapter_input_factor, preferred_element_type=jnp.float32
    ).astype(jnp.bfloat16)
    b_blocks = jnp.einsum(
        "vl,lyt->vyt", block_selector, adapter_output_factor, preferred_element_type=jnp.float32
    ).astype(jnp.bfloat16)
    part_in = jnp.einsum(
        "btf,bfr->btr", hidden_blocks, a_blocks, preferred_element_type=jnp.float32
    )
    part_out = jnp.einsum("btc,brc->btr", cols_blocks, b_blocks, preferred_element_type=jnp.float32)
    lowrank_input, lowrank_output = lax.psum((part_in, part_out), "tensor")
    lowrank_input = lowrank_input.astype(jnp.bfloat16)
    lowrank_output = lowrank_output.astype(jnp.bfloat16)
    gate_full, up_full, down_full = (
        lax.all_gather(gate_matrix, "dp", axis=0, tiled=True),
        lax.all_gather(up_matrix, "dp", axis=0, tiled=True),
        lax.all_gather(down_matrix, "dp", axis=0, tiled=True),
    )
    hidden_gradient = jnp.dot(grad_all, down_full, preferred_element_type=jnp.float32)
    additional_term = jnp.einsum(
        "btr,bfr->btf", lowrank_output, a_blocks, preferred_element_type=jnp.float32
    )
    hidden_gradient = hidden_gradient + ADAPTER_SCALE * additional_term.reshape(
        local_token_rows, local_hidden_units
    )
    gate_grad = (
        hidden_gradient * upper * sigmoid_gate * (1.0 + gate * (1.0 - sigmoid_gate))
    ).astype(jnp.bfloat16)
    up_grad = (hidden_gradient * silu_gate).astype(jnp.bfloat16)
    outer_product_input = jnp.einsum(
        "btf,btr->bfr", hidden_blocks, lowrank_output, preferred_element_type=jnp.float32
    )
    outer_product_output = jnp.einsum(
        "btr,btc->brc", lowrank_input, cols_blocks, preferred_element_type=jnp.float32
    )
    slot_onehot = (
        jnp.arange(adapter_list, dtype=jnp.int32)[:, None] == adapter_grad_slot[None, :]
    ).astype(jnp.float32)
    slot_block_mask = jnp.dot(slot_onehot, block_onehot.T)
    input_factor_terms = ADAPTER_SCALE * jnp.einsum(
        "pc,cdw->pdw", slot_block_mask, outer_product_input
    )
    output_factor_terms = ADAPTER_SCALE * jnp.einsum(
        "fn,nlv->flv", slot_block_mask, outer_product_output
    )
    owned_a, owned_b = (
        lax.psum_scatter(input_factor_terms, "dp", scatter_dimension=0, tiled=True),
        lax.psum_scatter(output_factor_terms, "dp", scatter_dimension=0, tiled=True),
    )
    grad_a = owned_a.astype(jnp.bfloat16)
    grad_b = owned_b.astype(jnp.bfloat16)
    first = lax.dot_general(
        gate_grad, gate_full, (((1,), (1,)), ((), ())), preferred_element_type=jnp.float32
    )
    second = lax.dot_general(
        up_grad, up_full, (((1,), (1,)), ((), ())), preferred_element_type=jnp.float32
    )
    summed = lax.psum_scatter(first + second, "tensor", scatter_dimension=0, tiled=True)
    input_grad = summed.astype(jnp.bfloat16)
    return (input_grad, grad_a, grad_b)


def solution(mesh):
    return jax.shard_map(
        grid_body if mesh.shape["tensor"] == 8 and mesh.shape["dp"] == 2 else body,
        mesh=mesh,
        in_specs=(
            P(("groups", "dp", "tensor"), None),
            P(("groups", "dp"), "tensor"),
            P(("groups", "dp"), "tensor"),
            P("dp", "tensor"),
            P("dp", "tensor"),
            P("dp", "tensor"),
            P(None, "tensor", None),
            P(None, None, "tensor"),
            P("groups"),
            P("groups", None),
            P(),
        ),
        out_specs=(
            P(("groups", "dp", "tensor"), None),
            P(("groups", "dp"), "tensor", None),
            P(("groups", "dp"), None, "tensor"),
        ),
        check_vma=False,
    )
```

```python
import functools

import jax
import jax.numpy as jnp
from jax import lax
from jax.experimental import pallas as pl
from jax.experimental.pallas import tpu as pltpu
from jax.sharding import PartitionSpec as P

BLOCK = 128


ADAPTER_SCALE = 2.0

F32 = jnp.float32
BF16 = jnp.bfloat16
MIB = 1024 * 1024

Y_SWAP = [(t, t ^ 1) for t in range(8)]
PAIR = [(t, t ^ 2) for t in range(8)]
FAR = [(t, t ^ 4) for t in range(8)]
ACROSS = [(t, t ^ 6) for t in range(8)]
MID = [(2, 4), (3, 5), (4, 2), (5, 3)]
OUTWARD = [(2, 0), (3, 1), (4, 6), (5, 7)]
INWARD = [(0, 2), (1, 3), (6, 4), (7, 5)]
CORES = [(0, 1), (1, 0)]

M_T, M_Y, M_D, M_Z, M_SLOT_ADAPTER, M_ADAPTER, M_GRAD_SLOT, M_SLAB = 0, 1, 2, 3, 7, 11, 15, 19


def nt_dot(a, b):
    return lax.dot_general(a, b, (((1,), (1,)), ((), ())), preferred_element_type=F32)


def tn_dot(a, b):
    return lax.dot_general(a, b, (((0,), (0,)), ((), ())), preferred_element_type=F32)


def call(
    kernel, meta, args, grid, in_specs, out_specs, out_shape, scratch=(), vmem=48, after=(), cost=(1000, 1000)
):
    first, extra = len(args), len(after)

    def run(m, *refs):
        kernel(m, *refs[:first], *refs[first + extra :])

    return pl.pallas_call(
        run,
        grid_spec=pltpu.PrefetchScalarGridSpec(
            num_scalar_prefetch=1,
            grid=grid,
            in_specs=list(in_specs) + [pl.BlockSpec(memory_space=pl.ANY)] * extra,
            out_specs=out_specs,
            scratch_shapes=list(scratch),
        ),
        out_shape=out_shape,
        compiler_params=pltpu.CompilerParams(vmem_limit_bytes=vmem * MIB),
        cost_estimate=pl.CostEstimate(flops=cost[0], bytes_accessed=cost[1], transcendentals=0),
    )(meta, *args, *after)


def pack_halves(p):
    h = p.shape[0] // 2
    return jnp.concatenate([p[:h], p[h:]], axis=1)


def unpack_halves(p):
    h = p.shape[1] // 2
    return jnp.concatenate([p[:, :h], p[:, h:]], axis=0)


def hidden_kernel(m, gate_ref, up_ref, a_ref, hidden_ref, low_ref):
    g = gate_ref[...].astype(F32)
    hidden = (g * jax.nn.sigmoid(g) * up_ref[...].astype(F32)).astype(BF16)
    hidden_ref[...] = hidden
    low_ref[...] = pack_halves(nt_dot(hidden, a_ref[0]))


def hidden_and_low_in(meta, gate_act, up_act, a_t, after):
    rows, width = gate_act.shape
    rank = a_t.shape[1]
    blocks = rows // BLOCK
    return call(
        hidden_kernel,
        meta,
        (gate_act, up_act, a_t),
        (blocks,),
        [
            pl.BlockSpec((BLOCK, width), lambda b, m: (b, 0)),
            pl.BlockSpec((BLOCK, width), lambda b, m: (b, 0)),
            pl.BlockSpec((1, rank, width), lambda b, m: (m[M_ADAPTER + b], 0, 0)),
        ],
        [
            pl.BlockSpec((BLOCK, width), lambda b, m: (b, 0)),
            pl.BlockSpec((BLOCK // 2, 2 * rank), lambda b, m: (b, 0)),
        ],
        [
            jax.ShapeDtypeStruct((rows, width), BF16),
            jax.ShapeDtypeStruct((rows // 2, 2 * rank), F32),
        ],
        after=after,
    )


def slabs_kernel(m, *refs):
    for i in range(4):
        refs[4 + i][...] = refs[i][0]


def slabs(meta, b):
    rank, columns = b.shape[1:]

    def spec(k):
        return pl.BlockSpec((1, rank, columns), lambda i, m: (m[M_SLAB + k], 0, 0))

    return call(
        slabs_kernel,
        meta,
        (b,) * 4,
        (1,),
        [spec(k) for k in range(4)],
        [pl.BlockSpec((rank, columns), lambda i, m: (0, 0))] * 4,
        [jax.ShapeDtypeStruct((rank, columns), BF16)] * 4,
    )


def low_out_kernel(m, own_ref, other_ref, s0, s1, s2, s3, low_in_ref, full_ref, short_ref):
    rows = own_ref.shape[0]
    rank, columns = s0.shape
    y, z = m[M_Y], m[M_Z]
    total = jnp.zeros((2 * rows, rank), F32)
    for k, slab in enumerate((s0, s1, s2, s3)):
        at = pl.ds(pl.multiple_of((jnp.bitwise_xor(z, k) * 2 + y) * columns, 128), columns)
        tokens = jnp.concatenate([own_ref[:, at], other_ref[:, at]], axis=0)
        total += nt_dot(tokens, slab[...])
    own, other = total[:rows], total[rows:]
    packed = jnp.concatenate(
        [jnp.where(y == 0, own, other), jnp.where(y == 0, other, own)], axis=1
    )
    at = pl.ds(pl.multiple_of(z * rows, rows), rows)
    for ref in (full_ref, short_ref):
        ref[: 4 * rows] = jnp.zeros((4 * rows, 2 * rank), ref.dtype)
        ref[4 * rows :] = low_in_ref[...].astype(ref.dtype)
        ref[at, :] = packed.astype(ref.dtype)


def low_parts(meta, own, other, pieces, low_in, after):
    rows, full = own.shape
    rank, columns = pieces[0].shape
    out = (8 * rows, 2 * rank)
    return call(
        low_out_kernel,
        meta,
        (own, other, *pieces, low_in),
        (1,),
        [pl.BlockSpec((rows, full), lambda i, m: (0, 0))] * 2
        + [pl.BlockSpec((rank, columns), lambda i, m: (0, 0))] * 4
        + [pl.BlockSpec((4 * rows, 2 * rank), lambda i, m: (0, 0))],
        [pl.BlockSpec(out, lambda i, m: (0, 0))] * 2,
        [jax.ShapeDtypeStruct(out, F32), jax.ShapeDtypeStruct(out, BF16)],
        after=after,
    )


def columns_kernel(m, *refs):
    cols_ref = refs[8]
    rows = refs[0].shape[0]
    y = m[M_Y]
    for s in range(4):
        z = m[M_Z + s]
        own, other = refs[2 * s][...], refs[2 * s + 1][...]
        first = jnp.where(y == 0, own, other)
        second = jnp.where(y == 0, other, own)
        tokens = jnp.concatenate([first, second], axis=0)
        cols_ref[pl.ds(pl.multiple_of(z * 2 * rows, 2 * rows), 2 * rows), :] = tokens


def own_columns(meta, shards, columns, after):
    rows = shards[0].shape[0]
    return call(
        columns_kernel,
        meta,
        shards,
        (1,),
        [pl.BlockSpec((rows, columns), lambda i, m: (0, m[M_T]))] * 8,
        pl.BlockSpec((8 * rows, columns), lambda i, m: (0, 0)),
        jax.ShapeDtypeStruct((8 * rows, columns), BF16),
        after=after,
    )


def act_grad_kernel(m, *refs):
    mine, other, gates, ups = refs[:4], refs[4:8], refs[8:12], refs[12:16]
    lows, factors = refs[16:18], refs[18:20]
    down_mine, down_other = refs[20:22]
    outs, lhs = refs[22:24], refs[24]
    rows = mine[0].shape[0]
    rank = factors[0].shape[1]
    y = m[M_Y]

    @pl.when(pl.program_id(0) == 0)
    def _():
        for s in range(4):
            lhs[0, s * rows : (s + 1) * rows] = mine[s][...]
            lhs[1, s * rows : (s + 1) * rows] = other[s][...]

    total = jnp.dot(lhs[0], down_mine[...], preferred_element_type=F32)
    total += jnp.dot(lhs[1], down_other[...], preferred_element_type=F32)
    for i in range(2):
        first, second = lows[i][:, :rank], lows[i][:, rank:]
        low = jnp.concatenate(
            [jnp.where(y == 0, first, second), jnp.where(y == 0, second, first)], axis=0
        )
        term = jnp.dot(low, factors[i][0], preferred_element_type=F32)
        for j in range(2):
            at = slice(j * rows, (j + 1) * rows)
            hg = total[(2 * i + j) * rows : (2 * i + j + 1) * rows] + ADAPTER_SCALE * term[at]
            g = gates[2 * i + j][...].astype(F32)
            u = ups[2 * i + j][...].astype(F32)
            sig = jax.nn.sigmoid(g)
            outs[i][0, at] = (hg * u * sig * (1.0 + g * (1.0 - sig))).astype(BF16)
            outs[i][1, at] = (hg * (g * sig)).astype(BF16)


def act_grads(meta, slots, shards, gate_act, up_act, low, a_t, down, after=()):
    rows = shards[0].shape[0]
    rank = a_t.shape[1]
    half, width = down.shape[0] // 2, down.shape[1]
    step = width // 5

    def act_spec(slot, j):
        def index(n, m):
            y = m[M_Y]
            return (m[M_Z + slot] * 2 + (1 - y if j else y), n)

        return pl.BlockSpec((rows, step), index)

    def low_spec(slot):
        return pl.BlockSpec((rows, 2 * rank), lambda n, m: (m[M_Z + slot], 0))

    def factor_spec(slot):
        return pl.BlockSpec((1, rank, step), lambda n, m: (m[M_SLOT_ADAPTER + slot], 0, n))

    acts = [act_spec(slot, j) for slot in slots for j in range(2)]
    return call(
        act_grad_kernel,
        meta,
        (*shards, *shards, *[gate_act] * 4, *[up_act] * 4, low, low, a_t, a_t, down, down),
        (width // step,),
        [pl.BlockSpec((rows, half), lambda n, m: (0, m[M_D]))] * 4
        + [pl.BlockSpec((rows, half), lambda n, m: (0, 1 - m[M_D]))] * 4
        + acts
        + acts
        + [low_spec(slot) for slot in slots]
        + [factor_spec(slot) for slot in slots]
        + [
            pl.BlockSpec((half, step), lambda n, m: (m[M_D], n)),
            pl.BlockSpec((half, step), lambda n, m: (1 - m[M_D], n)),
        ],
        [pl.BlockSpec((2, 2 * rows, step), lambda n, m: (0, 0, n))] * 2,
        [jax.ShapeDtypeStruct((2, 2 * rows, width), BF16)] * 2,
        scratch=[pltpu.VMEM((2, 4 * rows, half), BF16)],
        after=after,
    )


def input_grad_kernel(m, mine_ref, other_ref, gate_ref, up_ref, keep_ref, send_ref, lhs):
    rows = mine_ref.shape[1] // 2

    @pl.when(pl.program_id(0) == 0)
    def _():
        for i in range(2):
            for y in range(2):
                lhs[i, (2 * y) * rows : (2 * y + 1) * rows] = mine_ref[i, y * rows : (y + 1) * rows]
                lhs[i, (2 * y + 1) * rows : (2 * y + 2) * rows] = other_ref[i, y * rows : (y + 1) * rows]

    total = nt_dot(lhs[0], gate_ref[...]) + nt_dot(lhs[1], up_ref[...])
    keep_ref[...] = total[: 2 * rows].astype(BF16)
    send_ref[...] = total[2 * rows :].astype(BF16)


def input_grad_parts(meta, mine, other, gate, up, after=()):
    rows, width = mine.shape[1:]
    half = gate.shape[0]
    step = 512
    out = jax.ShapeDtypeStruct((rows, half), BF16)
    return call(
        input_grad_kernel,
        meta,
        (mine, other, gate, up),
        (half // step,),
        [pl.BlockSpec((2, rows, width), lambda n, m: (0, 0, 0))] * 2
        + [pl.BlockSpec((step, width), lambda n, m: (n, 0))] * 2,
        [pl.BlockSpec((rows, step), lambda n, m: (0, n))] * 2,
        [out, out],
        scratch=[pltpu.VMEM((2, 2 * rows, width), BF16)],
        after=after,
    )


def owner_kernel(blocks, m, low_ref, features_ref, keep_ref, send_ref):
    i = pl.program_id(0)
    d = m[M_D]
    owned = keep_ref.shape[0] * pl.num_programs(0)
    rows = low_ref.shape[0] // blocks
    for ref, owner in ((keep_ref, d), (send_ref, 1 - d)):
        slot = owner * owned + i
        total = jnp.zeros(ref.shape[1:], F32)
        for b in range(blocks):
            hit = jnp.where(m[M_GRAD_SLOT + b] == slot, ADAPTER_SCALE, 0.0)
            low = unpack_halves(low_ref[b * rows : (b + 1) * rows, :])
            total += hit * tn_dot(low, features_ref[b * BLOCK : (b + 1) * BLOCK, :])
        ref[0] = total.astype(BF16)


def owner_grads(meta, low, which, features, owned, after=()):
    tokens, width = features.shape
    half_rows, double = low.shape[0] // 2, low.shape[1]
    rank = double // 2
    out = jax.ShapeDtypeStruct((owned, rank, width), BF16)
    return call(
        functools.partial(owner_kernel, tokens // BLOCK),
        meta,
        (low, features),
        (owned,),
        [
            pl.BlockSpec((half_rows, double), lambda i, m: (which, 0)),
            pl.BlockSpec((tokens, width), lambda i, m: (0, 0)),
        ],
        [pl.BlockSpec((1, rank, width), lambda i, m: (i, 0, 0))] * 2,
        [out, out],
        after=after,
    )


def add_kernel(count, m, *refs):
    total = refs[0][...].astype(F32)
    for r in refs[1:count]:
        total += r[...].astype(F32)
    for r in refs[count:]:
        r[...] = total.astype(r.dtype)


def add_after(meta, xs, after, kinds=(BF16,), steps=1):
    rows, width = xs[0].shape
    spec = pl.BlockSpec((rows // steps, width), lambda i, m: (i, 0))
    out = call(
        functools.partial(add_kernel, len(xs)),
        meta,
        xs,
        (steps,),
        [spec] * len(xs),
        [spec] * len(kinds),
        [jax.ShapeDtypeStruct((rows, width), k) for k in kinds],
        vmem=16,
        after=after,
    )
    return out if len(kinds) > 1 else out[0]


def final_kernel(m, *refs):
    total = refs[0][...].astype(F32)
    for r in refs[1:-2]:
        total += r[...].astype(F32)
    rows = refs[-1].shape[0]
    refs[-2][...] = total[:rows].astype(BF16)
    refs[-1][...] = total[rows:].astype(BF16)


def final_sum(meta, xs, after):
    rows, width = xs[0].shape
    return call(
        final_kernel,
        meta,
        xs,
        (1,),
        [pl.BlockSpec((rows, width), lambda i, m: (0, 0))] * len(xs),
        [pl.BlockSpec((rows // 2, width), lambda i, m: (0, 0))] * 2,
        [jax.ShapeDtypeStruct((rows // 2, width), BF16)] * 2,
        vmem=16,
        after=after,
    )


def add(*xs):
    return functools.reduce(jnp.add, [x.astype(F32) for x in xs]).astype(BF16)


def tied(x, *others):
    return lax.optimization_barrier((x, *others))[0]


def grid_body(
    cotangent,
    gate_act,
    up_act,
    gate_matrix,
    up_matrix,
    down_matrix,
    adapter_input_factor,
    adapter_output_factor,
    padded_block_segment,
    segment_adapter_index,
    adapter_grad_slot,
):
    adapters = adapter_input_factor.shape[0]
    blocks = gate_act.shape[0] // BLOCK
    d = lax.axis_index("dp")
    t = lax.axis_index("tensor")
    z, y = t // 2, t % 2
    low_side = z < 2
    slots_z = jnp.stack([z, z ^ 1, jnp.where(low_side, 2, 1), jnp.where(low_side, 3, 0)])
    segments_here = lax.dynamic_slice_in_dim(padded_block_segment, d * blocks, blocks)

    def pick(table, index):
        hit = index[:, None] == jnp.arange(table.shape[0], dtype=jnp.int32)[None, :]
        return jnp.sum(jnp.where(hit, table[None, :], 0), axis=1)

    block_adapter = pick(segment_adapter_index[:, 0], segments_here)
    meta = jnp.concatenate(
        [
            jnp.stack([t, y, d]),
            slots_z,
            pick(block_adapter, slots_z),
            block_adapter,
            pick(adapter_grad_slot, block_adapter),
            pick(block_adapter, jnp.stack([z, z ^ 1, z ^ 2, z ^ 3])),
        ]
    ).astype(jnp.int32)
    a_t = jnp.swapaxes(adapter_input_factor, 1, 2)
    send = functools.partial(lax.ppermute, axis_name="tensor")
    swap_cores = functools.partial(lax.ppermute, axis_name="dp", perm=CORES)
    at_end = (z == 0) | (z == 3)

    down = lax.all_gather(down_matrix, "dp", axis=0, tiled=True)
    pair = send(cotangent, perm=PAIR)
    mid = send(cotangent, perm=MID)
    y0 = send(cotangent, perm=Y_SWAP)
    slab, *others = slabs(meta, adapter_output_factor)
    pieces = [send(s, perm=p) for s, p in zip(others, (PAIR, FAR, ACROSS))]
    hidden, low_in = hidden_and_low_in(meta, gate_act, up_act, a_t, tuple(others))
    y1 = send(tied(pair, y0, low_in, *pieces), perm=Y_SWAP)
    pair_mid = send(tied(pair, low_in), perm=MID)
    mid_out = send(tied(mid, low_in), perm=OUTWARD)
    low_sum, low = low_parts(meta, cotangent, y0, [slab] + pieces, low_in, ())
    low_sum, low = add_after(meta, (low_sum, send(low, perm=Y_SWAP)), (), (F32, BF16))
    slot2 = jnp.where(at_end, mid_out, mid)
    y2 = send(tied(slot2, y1, low), perm=Y_SWAP)
    low = tied(low, y1)
    low_sum, low = add_after(meta, (low_sum, send(low, perm=PAIR)), (), (F32, BF16))
    far_out = send(pair_mid, perm=OUTWARD)
    slot3 = tied(jnp.where(at_end, tied(far_out, low), pair_mid), y2)
    y3 = send(slot3, perm=Y_SWAP)
    low = tied(low, y2)
    low_sum, low = add_after(meta, (low_sum, send(low, perm=FAR)), (), (F32, BF16))
    near, far = (cotangent, y0, pair, y1), (slot2, y2, slot3, y3)
    rest = (gate_act, up_act, low, a_t, down)
    mine0, mine1 = act_grads(meta, (0, 1), near, *rest, (slot3,))
    mine2, mine3 = act_grads(meta, (2, 3), far, *rest, (mine0,))
    other3 = swap_cores(mine3)
    other2 = swap_cores(tied(mine2, other3))
    other1 = swap_cores(tied(mine1, other2))
    other0 = swap_cores(tied(mine0, other1))

    def parts(mine, other, after):
        keep, give = input_grad_parts(meta, mine, other, gate_matrix, up_matrix, after)
        return keep, send(give, perm=Y_SWAP), give

    keep3, got3, give3 = parts(mine3, other3, (mine2,))
    keep2, got2, give2 = parts(mine2, other2, (give3,))
    sum3 = add_after(meta, (keep3, got3), (give2,))
    far_in = send(sum3, perm=INWARD)
    keep1, got1, give1 = parts(mine1, other1, (sum3,))
    sum2 = add_after(meta, (keep2, got2), (give1,))
    mid_in = send(sum2, perm=INWARD)
    sum3 = add_after(meta, (sum3, far_in), (sum2,))
    far_mid = send(sum3, perm=MID)
    keep0, got0, give0 = parts(mine0, other0, (sum3,))
    sum1 = add_after(meta, (keep1, got1, far_mid), (give0,))
    from_pair = send(sum1, perm=PAIR)
    sum2 = add_after(meta, (sum2, mid_in), (sum1,))
    from_mid = send(sum2, perm=MID)
    owned = adapters // 2
    keep_a, give_a = owner_grads(meta, low, 0, hidden, owned, (sum2,))
    columns = own_columns(meta, near + far, adapter_output_factor.shape[2], (keep_a,))
    keep_b, give_b = owner_grads(meta, low, 1, columns, owned)
    own, give = final_sum(meta, (keep0, got0, from_pair, from_mid), (keep_b,))
    grad_b = add(keep_b, swap_cores(give_b))
    shape = keep_a.shape
    flat = (shape[0] * shape[1], shape[2])
    grad_a = add_after(
        meta, (keep_a.reshape(flat), swap_cores(give_a).reshape(flat)), (give,), steps=2
    )
    got = swap_cores(give)
    input_grad = jnp.where(
        d == 0, jnp.concatenate([own, got], axis=1), jnp.concatenate([got, own], axis=1)
    )
    grad_a = jnp.swapaxes(grad_a.reshape(shape), 1, 2)
    return (input_grad, grad_a, grad_b)


def body(
    cotangent,
    gate_activation_stored,
    up_activation_stored,
    gate_matrix,
    up_matrix,
    down_matrix,
    adapter_input_factor,
    adapter_output_factor,
    padded_block_segment,
    segment_adapter_index,
    adapter_grad_slot,
):
    local_token_rows = gate_activation_stored.shape[0]
    local_hidden_units = gate_activation_stored.shape[1]
    adapter_list = adapter_input_factor.shape[0]
    local_columns = adapter_output_factor.shape[2]
    seg_count = segment_adapter_index.shape[0]
    block_count = local_token_rows // BLOCK
    dp_index = lax.axis_index("dp")
    tensor_index = lax.axis_index("tensor")
    grad_all = lax.all_gather(cotangent, "tensor", axis=0, tiled=True)
    segments_here = lax.dynamic_slice_in_dim(
        padded_block_segment, dp_index * block_count, block_count
    )
    seg_onehot = (segments_here[:, None] == jnp.arange(seg_count, dtype=jnp.int32)[None, :]).astype(
        jnp.float32
    )
    adapter_onehot = (
        segment_adapter_index[:, 0][:, None] == jnp.arange(adapter_list, dtype=jnp.int32)[None, :]
    ).astype(jnp.float32)
    block_onehot = jnp.dot(seg_onehot, adapter_onehot)
    block_selector = block_onehot.astype(jnp.bfloat16)
    gate = gate_activation_stored.astype(jnp.float32)
    upper = up_activation_stored.astype(jnp.float32)
    sigmoid_gate = jax.nn.sigmoid(gate)
    silu_gate = gate * sigmoid_gate
    hidden_state = (silu_gate * upper).astype(jnp.bfloat16)
    hidden_blocks = hidden_state.reshape(block_count, BLOCK, local_hidden_units)
    cols_mine = lax.dynamic_slice_in_dim(grad_all, tensor_index * local_columns, local_columns, 1)
    cols_blocks = cols_mine.reshape(block_count, BLOCK, local_columns)
    a_blocks = jnp.einsum(
        "yz,zuo->yuo", block_selector, adapter_input_factor, preferred_element_type=jnp.float32
    ).astype(jnp.bfloat16)
    b_blocks = jnp.einsum(
        "vl,lyt->vyt", block_selector, adapter_output_factor, preferred_element_type=jnp.float32
    ).astype(jnp.bfloat16)
    part_in = jnp.einsum(
        "btf,bfr->btr", hidden_blocks, a_blocks, preferred_element_type=jnp.float32
    )
    part_out = jnp.einsum("btc,brc->btr", cols_blocks, b_blocks, preferred_element_type=jnp.float32)
    lowrank_input, lowrank_output = lax.psum((part_in, part_out), "tensor")
    lowrank_input = lowrank_input.astype(jnp.bfloat16)
    lowrank_output = lowrank_output.astype(jnp.bfloat16)
    gate_full, up_full, down_full = (
        lax.all_gather(gate_matrix, "dp", axis=0, tiled=True),
        lax.all_gather(up_matrix, "dp", axis=0, tiled=True),
        lax.all_gather(down_matrix, "dp", axis=0, tiled=True),
    )
    hidden_gradient = jnp.dot(grad_all, down_full, preferred_element_type=jnp.float32)
    additional_term = jnp.einsum(
        "btr,bfr->btf", lowrank_output, a_blocks, preferred_element_type=jnp.float32
    )
    hidden_gradient = hidden_gradient + ADAPTER_SCALE * additional_term.reshape(
        local_token_rows, local_hidden_units
    )
    gate_grad = (
        hidden_gradient * upper * sigmoid_gate * (1.0 + gate * (1.0 - sigmoid_gate))
    ).astype(jnp.bfloat16)
    up_grad = (hidden_gradient * silu_gate).astype(jnp.bfloat16)
    outer_product_input = jnp.einsum(
        "btf,btr->bfr", hidden_blocks, lowrank_output, preferred_element_type=jnp.float32
    )
    outer_product_output = jnp.einsum(
        "btr,btc->brc", lowrank_input, cols_blocks, preferred_element_type=jnp.float32
    )
    slot_onehot = (
        jnp.arange(adapter_list, dtype=jnp.int32)[:, None] == adapter_grad_slot[None, :]
    ).astype(jnp.float32)
    slot_block_mask = jnp.dot(slot_onehot, block_onehot.T)
    input_factor_terms = ADAPTER_SCALE * jnp.einsum(
        "pc,cdw->pdw", slot_block_mask, outer_product_input
    )
    output_factor_terms = ADAPTER_SCALE * jnp.einsum(
        "fn,nlv->flv", slot_block_mask, outer_product_output
    )
    owned_a, owned_b = (
        lax.psum_scatter(input_factor_terms, "dp", scatter_dimension=0, tiled=True),
        lax.psum_scatter(output_factor_terms, "dp", scatter_dimension=0, tiled=True),
    )
    grad_a = owned_a.astype(jnp.bfloat16)
    grad_b = owned_b.astype(jnp.bfloat16)
    first = lax.dot_general(
        gate_grad, gate_full, (((1,), (1,)), ((), ())), preferred_element_type=jnp.float32
    )
    second = lax.dot_general(
        up_grad, up_full, (((1,), (1,)), ((), ())), preferred_element_type=jnp.float32
    )
    summed = lax.psum_scatter(first + second, "tensor", scatter_dimension=0, tiled=True)
    input_grad = summed.astype(jnp.bfloat16)
    return (input_grad, grad_a, grad_b)


def solution(mesh):
    return jax.shard_map(
        grid_body if mesh.shape["tensor"] == 8 and mesh.shape["dp"] == 2 else body,
        mesh=mesh,
        in_specs=(
            P(("groups", "dp", "tensor"), None),
            P(("groups", "dp"), "tensor"),
            P(("groups", "dp"), "tensor"),
            P("dp", "tensor"),
            P("dp", "tensor"),
            P("dp", "tensor"),
            P(None, "tensor", None),
            P(None, None, "tensor"),
            P("groups"),
            P("groups", None),
            P(),
        ),
        out_specs=(
            P(("groups", "dp", "tensor"), None),
            P(("groups", "dp"), "tensor", None),
            P(("groups", "dp"), None, "tensor"),
        ),
        check_vma=False,
    )
```

```python
import functools

import jax
import jax.numpy as jnp
from jax import lax
from jax.experimental import pallas as pl
from jax.experimental.pallas import tpu as pltpu
from jax.sharding import PartitionSpec as P

BLOCK = 128


ADAPTER_SCALE = 2.0

F32 = jnp.float32
BF16 = jnp.bfloat16
MIB = 1024 * 1024

Y_SWAP = [(t, t ^ 1) for t in range(8)]
PAIR = [(t, t ^ 2) for t in range(8)]
FAR = [(t, t ^ 4) for t in range(8)]
ACROSS = [(t, t ^ 6) for t in range(8)]
MID = [(2, 4), (3, 5), (4, 2), (5, 3)]
OUTWARD = [(2, 0), (3, 1), (4, 6), (5, 7)]
INWARD = [(0, 2), (1, 3), (6, 4), (7, 5)]
CORES = [(0, 1), (1, 0)]

M_T, M_Y, M_D, M_Z, M_SLOT_ADAPTER, M_ADAPTER, M_GRAD_SLOT, M_SLAB = 0, 1, 2, 3, 7, 11, 15, 19


def nt_dot(a, b):
    return lax.dot_general(a, b, (((1,), (1,)), ((), ())), preferred_element_type=F32)


def tn_dot(a, b):
    return lax.dot_general(a, b, (((0,), (0,)), ((), ())), preferred_element_type=F32)


def call(
    kernel, meta, args, grid, in_specs, out_specs, out_shape, scratch=(), vmem=58, after=(), cost=(1000, 1000)
):
    first, extra = len(args), len(after)

    def run(m, *refs):
        kernel(m, *refs[:first], *refs[first + extra :])

    return pl.pallas_call(
        run,
        grid_spec=pltpu.PrefetchScalarGridSpec(
            num_scalar_prefetch=1,
            grid=grid,
            in_specs=list(in_specs) + [pl.BlockSpec(memory_space=pl.ANY)] * extra,
            out_specs=out_specs,
            scratch_shapes=list(scratch),
        ),
        out_shape=out_shape,
        compiler_params=pltpu.CompilerParams(vmem_limit_bytes=vmem * MIB),
        cost_estimate=pl.CostEstimate(flops=cost[0], bytes_accessed=cost[1], transcendentals=0),
    )(meta, *args, *after)


def pack_halves(p):
    h = p.shape[0] // 2
    return jnp.concatenate([p[:h], p[h:]], axis=1)


def unpack_halves(p):
    h = p.shape[1] // 2
    return jnp.concatenate([p[:, :h], p[:, h:]], axis=0)


def hidden_kernel(m, gate_ref, up_ref, a_ref, hidden_ref, low_ref):
    g = gate_ref[...].astype(F32)
    hidden = (g * jax.nn.sigmoid(g) * up_ref[...].astype(F32)).astype(BF16)
    hidden_ref[...] = hidden
    low_ref[...] = pack_halves(nt_dot(hidden, a_ref[0]))


def hidden_and_low_in(meta, gate_act, up_act, a_t, after):
    rows, width = gate_act.shape
    rank = a_t.shape[1]
    blocks = rows // BLOCK
    return call(
        hidden_kernel,
        meta,
        (gate_act, up_act, a_t),
        (blocks,),
        [
            pl.BlockSpec((BLOCK, width), lambda b, m: (b, 0)),
            pl.BlockSpec((BLOCK, width), lambda b, m: (b, 0)),
            pl.BlockSpec((1, rank, width), lambda b, m: (m[M_ADAPTER + b], 0, 0)),
        ],
        [
            pl.BlockSpec((BLOCK, width), lambda b, m: (b, 0)),
            pl.BlockSpec((BLOCK // 2, 2 * rank), lambda b, m: (b, 0)),
        ],
        [
            jax.ShapeDtypeStruct((rows, width), BF16),
            jax.ShapeDtypeStruct((rows // 2, 2 * rank), F32),
        ],
        after=after,
    )


def slabs_kernel(m, *refs):
    for i in range(4):
        refs[4 + i][...] = refs[i][0]


def slabs(meta, b):
    rank, columns = b.shape[1:]

    def spec(k):
        return pl.BlockSpec((1, rank, columns), lambda i, m: (m[M_SLAB + k], 0, 0))

    return call(
        slabs_kernel,
        meta,
        (b,) * 4,
        (1,),
        [spec(k) for k in range(4)],
        [pl.BlockSpec((rank, columns), lambda i, m: (0, 0))] * 4,
        [jax.ShapeDtypeStruct((rank, columns), BF16)] * 4,
    )


def low_out_kernel(m, own_ref, other_ref, s0, s1, s2, s3, out_ref):
    rows = own_ref.shape[0]
    rank, columns = s0.shape
    y, z = m[M_Y], m[M_Z]
    total = jnp.zeros((2 * rows, rank), F32)
    for k, slab in enumerate((s0, s1, s2, s3)):
        at = pl.ds(pl.multiple_of((jnp.bitwise_xor(z, k) * 2 + y) * columns, 128), columns)
        tokens = jnp.concatenate([own_ref[:, at], other_ref[:, at]], axis=0)
        total += nt_dot(tokens, slab[...])
    own, other = total[:rows], total[rows:]
    out_ref[...] = jnp.concatenate(
        [jnp.where(y == 0, own, other), jnp.where(y == 0, other, own)], axis=1
    )


def low_block(meta, own, other, pieces, after):
    rows, full = own.shape
    rank, columns = pieces[0].shape
    return call(
        low_out_kernel,
        meta,
        (own, other, *pieces),
        (1,),
        [pl.BlockSpec((rows, full), lambda i, m: (0, 0))] * 2
        + [pl.BlockSpec((rank, columns), lambda i, m: (0, 0))] * 4,
        pl.BlockSpec((rows, 2 * rank), lambda i, m: (0, 0)),
        jax.ShapeDtypeStruct((rows, 2 * rank), F32),
        after=after,
    )


def place_kernel(m, *refs):
    rows = refs[0].shape[0]
    for k in range(4):
        at = pl.ds(pl.multiple_of(jnp.bitwise_xor(m[M_Z], k) * rows, rows), rows)
        part = refs[k][...]
        refs[4][at, :] = part
        refs[5][at, :] = part.astype(BF16)


def place_blocks(meta, parts):
    rows, width = parts[0].shape
    out = (4 * rows, width)
    return call(
        place_kernel,
        meta,
        parts,
        (1,),
        [pl.BlockSpec((rows, width), lambda i, m: (0, 0))] * 4,
        [pl.BlockSpec(out, lambda i, m: (0, 0))] * 2,
        [jax.ShapeDtypeStruct(out, F32), jax.ShapeDtypeStruct(out, BF16)],
    )


def columns_kernel(m, *refs):
    cols_ref = refs[8]
    rows = refs[0].shape[0]
    y = m[M_Y]
    for s in range(4):
        z = m[M_Z + s]
        own, other = refs[2 * s][...], refs[2 * s + 1][...]
        first = jnp.where(y == 0, own, other)
        second = jnp.where(y == 0, other, own)
        tokens = jnp.concatenate([first, second], axis=0)
        cols_ref[pl.ds(pl.multiple_of(z * 2 * rows, 2 * rows), 2 * rows), :] = tokens


def own_columns(meta, shards, columns, after):
    rows = shards[0].shape[0]
    return call(
        columns_kernel,
        meta,
        shards,
        (1,),
        [pl.BlockSpec((rows, columns), lambda i, m: (0, m[M_T]))] * 8,
        pl.BlockSpec((8 * rows, columns), lambda i, m: (0, 0)),
        jax.ShapeDtypeStruct((8 * rows, columns), BF16),
        after=after,
    )


def act_grad_kernel(joined, m, *refs):
    mine, other = refs[:8], refs[8:16]
    gate_ref, up_ref, low_ref = refs[16:19]
    factors = refs[19:23]
    down_mine, down_other = refs[23:25]
    outs, lhs = refs[25:-1], refs[-1]
    rows = mine[0].shape[0]
    rank = factors[0].shape[1]
    y = m[M_Y]

    @pl.when(pl.program_id(0) == 0)
    def _():
        for s in range(8):
            lhs[0, s * rows : (s + 1) * rows] = mine[s][...]
            lhs[1, s * rows : (s + 1) * rows] = other[s][...]

    total = jnp.dot(lhs[0], down_mine[...], preferred_element_type=F32)
    total += jnp.dot(lhs[1], down_other[...], preferred_element_type=F32)
    for i in range(4):
        z = m[M_Z + i]
        packed = low_ref[pl.ds(pl.multiple_of(z * rows, rows), rows), :]
        first, second = packed[:, :rank], packed[:, rank:]
        low = jnp.concatenate(
            [jnp.where(y == 0, first, second), jnp.where(y == 0, second, first)], axis=0
        )
        term = jnp.dot(low, factors[i][0], preferred_element_type=F32)
        out = outs[0].at[i] if joined else outs[i]
        for j in range(2):
            at = slice(j * rows, (j + 1) * rows)
            hg = total[(2 * i + j) * rows : (2 * i + j + 1) * rows] + ADAPTER_SCALE * term[at]
            source = pl.ds(pl.multiple_of((z * 2 + (1 - y if j else y)) * rows, rows), rows)
            g = gate_ref[source, :].astype(F32)
            u = up_ref[source, :].astype(F32)
            sig = jax.nn.sigmoid(g)
            out[0, at] = (hg * u * sig * (1.0 + g * (1.0 - sig))).astype(BF16)
            out[1, at] = (hg * (g * sig)).astype(BF16)


def act_grads(meta, shards, gate_act, up_act, low, a_t, down_mine, down_other, span, joined, after=()):
    rows = shards[0].shape[0]
    rank = a_t.shape[1]
    half = down_mine.shape[0]
    start, width, step = span
    first = start // step

    def factor_spec(slot):
        return pl.BlockSpec((1, rank, step), lambda n, m: (m[M_SLOT_ADAPTER + slot], 0, n + first))

    if joined:
        out_specs = [pl.BlockSpec((4, 2, 2 * rows, step), lambda n, m: (0, 0, 0, n))]
        out_shape = [jax.ShapeDtypeStruct((4, 2, 2 * rows, width), BF16)]
    else:
        out_specs = [pl.BlockSpec((2, 2 * rows, step), lambda n, m: (0, 0, n))] * 4
        out_shape = [jax.ShapeDtypeStruct((2, 2 * rows, width), BF16)] * 4
    return call(
        functools.partial(act_grad_kernel, joined),
        meta,
        (*shards, *shards, gate_act, up_act, low, *[a_t] * 4, down_mine, down_other),
        (width // step,),
        [pl.BlockSpec((rows, half), lambda n, m: (0, m[M_D]))] * 8
        + [pl.BlockSpec((rows, half), lambda n, m: (0, 1 - m[M_D]))] * 8
        + [pl.BlockSpec((8 * rows, step), lambda n, m: (0, n + first))] * 2
        + [pl.BlockSpec((4 * rows, 2 * rank), lambda n, m: (0, 0))]
        + [factor_spec(slot) for slot in range(4)]
        + [pl.BlockSpec((half, step), lambda n, m: (0, n + first))] * 2,
        out_specs,
        out_shape,
        scratch=[pltpu.VMEM((2, 8 * rows, half), BF16)],
        after=after,
    )


def input_grad_kernel(m, mine_ref, other_ref, tail_ref, other_tail_ref, gate_ref, up_ref, keep_ref, send_ref, lhs):
    rows = mine_ref.shape[1] // 2
    main = mine_ref.shape[2]

    @pl.when(pl.program_id(0) == 0)
    def _():
        for i in range(2):
            for y in range(2):
                at = slice(y * rows, (y + 1) * rows)
                for k, (ref, tail) in enumerate(((mine_ref, tail_ref), (other_ref, other_tail_ref))):
                    to = slice((2 * y + k) * rows, (2 * y + k + 1) * rows)
                    lhs[i, to, :main] = ref[i, at]
                    lhs[i, to, main:] = tail[0, i, at]

    total = nt_dot(lhs[0], gate_ref[...]) + nt_dot(lhs[1], up_ref[...])
    keep_ref[...] = total[: 2 * rows].astype(BF16)
    send_ref[...] = total[2 * rows :].astype(BF16)


def input_grad_parts(meta, slot, mine, other, tail, other_tail, gate, up, after=()):
    rows, main = mine.shape[1:]
    half, width = gate.shape
    step = 512
    out = jax.ShapeDtypeStruct((rows, half), BF16)
    return call(
        input_grad_kernel,
        meta,
        (mine, other, tail, other_tail, gate, up),
        (half // step,),
        [pl.BlockSpec((2, rows, main), lambda n, m: (0, 0, 0))] * 2
        + [pl.BlockSpec((1, 2, rows, width - main), lambda n, m: (slot, 0, 0, 0))] * 2
        + [pl.BlockSpec((step, width), lambda n, m: (n, 0))] * 2,
        [pl.BlockSpec((rows, step), lambda n, m: (0, n))] * 2,
        [out, out],
        scratch=[pltpu.VMEM((2, 2 * rows, width), BF16)],
        after=after,
    )


def owner_kernel(blocks, m, low_ref, features_ref, keep_ref, send_ref):
    i = pl.program_id(0)
    d = m[M_D]
    owned = keep_ref.shape[0] * pl.num_programs(0)
    rows = low_ref.shape[0] // blocks
    for ref, owner in ((keep_ref, d), (send_ref, 1 - d)):
        slot = owner * owned + i
        total = jnp.zeros(ref.shape[1:], F32)
        for b in range(blocks):
            hit = jnp.where(m[M_GRAD_SLOT + b] == slot, ADAPTER_SCALE, 0.0)
            low = unpack_halves(low_ref[b * rows : (b + 1) * rows, :])
            total += hit * tn_dot(low, features_ref[b * BLOCK : (b + 1) * BLOCK, :])
        ref[0] = total.astype(BF16)


def owner_grads(meta, low, features, owned, after=()):
    tokens, width = features.shape
    half_rows, double = low.shape
    rank = double // 2
    out = jax.ShapeDtypeStruct((owned, rank, width), BF16)
    return call(
        functools.partial(owner_kernel, tokens // BLOCK),
        meta,
        (low, features),
        (owned,),
        [
            pl.BlockSpec((half_rows, double), lambda i, m: (0, 0)),
            pl.BlockSpec((tokens, width), lambda i, m: (0, 0)),
        ],
        [pl.BlockSpec((1, rank, width), lambda i, m: (i, 0, 0))] * 2,
        [out, out],
        after=after,
    )


def add_kernel(count, m, *refs):
    total = refs[0][...].astype(F32)
    for r in refs[1:count]:
        total += r[...].astype(F32)
    for r in refs[count:]:
        r[...] = total.astype(r.dtype)


def add_after(meta, xs, after, kinds=(BF16,), steps=1):
    rows, width = xs[0].shape
    spec = pl.BlockSpec((rows // steps, width), lambda i, m: (i, 0))
    out = call(
        functools.partial(add_kernel, len(xs)),
        meta,
        xs,
        (steps,),
        [spec] * len(xs),
        [spec] * len(kinds),
        [jax.ShapeDtypeStruct((rows, width), k) for k in kinds],
        after=after,
    )
    return out if len(kinds) > 1 else out[0]


def final_kernel(m, *refs):
    total = refs[0][...].astype(F32)
    for r in refs[1:-2]:
        total += r[...].astype(F32)
    rows = refs[-1].shape[0]
    refs[-2][...] = total[:rows].astype(BF16)
    refs[-1][...] = total[rows:].astype(BF16)


def final_sum(meta, xs, after):
    rows, width = xs[0].shape
    return call(
        final_kernel,
        meta,
        xs,
        (1,),
        [pl.BlockSpec((rows, width), lambda i, m: (0, 0))] * len(xs),
        [pl.BlockSpec((rows // 2, width), lambda i, m: (0, 0))] * 2,
        [jax.ShapeDtypeStruct((rows // 2, width), BF16)] * 2,
        after=after,
    )


def add(*xs):
    return functools.reduce(jnp.add, [x.astype(F32) for x in xs]).astype(BF16)


def tied(x, *others):
    return lax.optimization_barrier((x, *others))[0]


def grid_body(
    cotangent,
    gate_act,
    up_act,
    gate_matrix,
    up_matrix,
    down_matrix,
    adapter_input_factor,
    adapter_output_factor,
    padded_block_segment,
    segment_adapter_index,
    adapter_grad_slot,
):
    adapters = adapter_input_factor.shape[0]
    blocks = gate_act.shape[0] // BLOCK
    d = lax.axis_index("dp")
    t = lax.axis_index("tensor")
    z, y = t // 2, t % 2
    low_side = z < 2
    slots_z = jnp.stack([z, z ^ 1, jnp.where(low_side, 2, 1), jnp.where(low_side, 3, 0)])
    segments_here = lax.dynamic_slice_in_dim(padded_block_segment, d * blocks, blocks)

    def pick(table, index):
        hit = index[:, None] == jnp.arange(table.shape[0], dtype=jnp.int32)[None, :]
        return jnp.sum(jnp.where(hit, table[None, :], 0), axis=1)

    block_adapter = pick(segment_adapter_index[:, 0], segments_here)
    meta = jnp.concatenate(
        [
            jnp.stack([t, y, d]),
            slots_z,
            pick(block_adapter, slots_z),
            block_adapter,
            pick(adapter_grad_slot, block_adapter),
            pick(block_adapter, jnp.stack([z, z ^ 1, z ^ 2, z ^ 3])),
        ]
    ).astype(jnp.int32)
    a_t = jnp.swapaxes(adapter_input_factor, 1, 2)
    send = functools.partial(lax.ppermute, axis_name="tensor")
    swap_cores = functools.partial(lax.ppermute, axis_name="dp", perm=CORES)
    at_end = (z == 0) | (z == 3)

    down_other = swap_cores(down_matrix)
    pair = send(cotangent, perm=PAIR)
    mid = send(cotangent, perm=MID)
    y0 = send(cotangent, perm=Y_SWAP)
    slab, *others = slabs(meta, adapter_output_factor)
    hidden, low_in = hidden_and_low_in(meta, gate_act, up_act, a_t, tuple(others))
    piece1 = send(others[0], perm=PAIR)
    piece2 = send(tied(others[1], y0, low_in), perm=FAR)
    piece3 = send(tied(others[2], y0, low_in), perm=ACROSS)
    y1 = send(tied(pair, y0, low_in, piece1), perm=Y_SWAP)
    pair_mid = send(tied(pair, y0, low_in), perm=MID)
    mid_out = send(tied(mid, y0, low_in), perm=OUTWARD)
    slot2 = jnp.where(at_end, mid_out, mid)
    y2 = send(tied(slot2, y1, piece2, piece3), perm=Y_SWAP)
    far_out = send(tied(pair_mid, y1), perm=OUTWARD)
    block = low_block(meta, cotangent, y0, (slab, piece1, piece2, piece3), (y1, down_other))
    blocks_z = [block] + [send(block, perm=p) for p in (PAIR, FAR, ACROSS)]
    low_half, low_half_short = place_blocks(meta, blocks_z)
    slot3 = tied(jnp.where(at_end, far_out, pair_mid), y2, low_half)
    y3 = send(slot3, perm=Y_SWAP)
    low = add_after(meta, (low_half, send(tied(low_half_short, y2), perm=Y_SWAP)), ())
    shards = (cotangent, y0, pair, y1, slot2, y2, slot3, y3)
    width = gate_act.shape[1]
    main = width // 256 * 256
    rest = (shards, gate_act, up_act, low, a_t, down_matrix, down_other)
    (tail,) = act_grads(meta, *rest, (main, width - main, width - main), True)
    mine = act_grads(meta, *rest, (0, main, 256), False, (tail,))
    other_tail = swap_cores(tail)
    other3 = swap_cores(mine[3])
    other2 = swap_cores(tied(mine[2], other3))

    def parts(slot, other, after):
        keep, give = input_grad_parts(
            meta, slot, mine[slot], other, tail, other_tail, gate_matrix, up_matrix, after
        )
        return keep, send(give, perm=Y_SWAP), give

    got_in = send(tied(low_in, mine[3]).astype(BF16), perm=Y_SWAP)
    keep3, got3, give3 = parts(3, other3, ())
    low_in, short = add_after(meta, (low_in, got_in), (give3,), (F32, BF16))
    got_in = send(short, perm=PAIR)
    keep2, got2, give2 = parts(2, other2, (short,))
    low_in, short = add_after(meta, (low_in, got_in), (give2,), (F32, BF16))
    got_in = send(short, perm=FAR)
    sum3 = add_after(meta, (keep3, got3), (short,))
    far_in = send(sum3, perm=INWARD)
    other1 = swap_cores(tied(mine[1], give3))
    keep1, got1, give1 = parts(1, other1, (sum3,))
    low_in = add_after(meta, (low_in, got_in), (give1,))
    sum2 = add_after(meta, (keep2, got2), (low_in,))
    mid_in = send(sum2, perm=INWARD)
    sum3 = add_after(meta, (sum3, far_in), (sum2,))
    far_mid = send(sum3, perm=MID)
    other0 = swap_cores(tied(mine[0], give2))
    keep0, got0, give0 = parts(0, other0, (sum3,))
    sum1 = add_after(meta, (keep1, got1, far_mid), (give0,))
    from_pair = send(sum1, perm=PAIR)
    sum2 = add_after(meta, (sum2, mid_in), (sum1,))
    from_mid = send(sum2, perm=MID)
    owned = adapters // 2
    keep_a, give_a = owner_grads(meta, low, hidden, owned, (sum2,))
    columns = own_columns(meta, shards, adapter_output_factor.shape[2], (keep_a,))
    keep_b, give_b = owner_grads(meta, low_in, columns, owned)
    own, give = final_sum(meta, (keep0, got0, from_pair, from_mid), (keep_b,))
    grad_b = add(keep_b, swap_cores(give_b))
    shape = keep_a.shape
    flat = (shape[0] * shape[1], shape[2])
    grad_a = add_after(
        meta, (keep_a.reshape(flat), swap_cores(give_a).reshape(flat)), (give,), steps=2
    )
    got = swap_cores(give)
    input_grad = jnp.where(
        d == 0, jnp.concatenate([own, got], axis=1), jnp.concatenate([got, own], axis=1)
    )
    grad_a = jnp.swapaxes(grad_a.reshape(shape), 1, 2)
    return (input_grad, grad_a, grad_b)


def body(
    cotangent,
    gate_activation_stored,
    up_activation_stored,
    gate_matrix,
    up_matrix,
    down_matrix,
    adapter_input_factor,
    adapter_output_factor,
    padded_block_segment,
    segment_adapter_index,
    adapter_grad_slot,
):
    local_token_rows = gate_activation_stored.shape[0]
    local_hidden_units = gate_activation_stored.shape[1]
    adapter_list = adapter_input_factor.shape[0]
    local_columns = adapter_output_factor.shape[2]
    seg_count = segment_adapter_index.shape[0]
    block_count = local_token_rows // BLOCK
    dp_index = lax.axis_index("dp")
    tensor_index = lax.axis_index("tensor")
    grad_all = lax.all_gather(cotangent, "tensor", axis=0, tiled=True)
    segments_here = lax.dynamic_slice_in_dim(
        padded_block_segment, dp_index * block_count, block_count
    )
    seg_onehot = (segments_here[:, None] == jnp.arange(seg_count, dtype=jnp.int32)[None, :]).astype(
        jnp.float32
    )
    adapter_onehot = (
        segment_adapter_index[:, 0][:, None] == jnp.arange(adapter_list, dtype=jnp.int32)[None, :]
    ).astype(jnp.float32)
    block_onehot = jnp.dot(seg_onehot, adapter_onehot)
    block_selector = block_onehot.astype(jnp.bfloat16)
    gate = gate_activation_stored.astype(jnp.float32)
    upper = up_activation_stored.astype(jnp.float32)
    sigmoid_gate = jax.nn.sigmoid(gate)
    silu_gate = gate * sigmoid_gate
    hidden_state = (silu_gate * upper).astype(jnp.bfloat16)
    hidden_blocks = hidden_state.reshape(block_count, BLOCK, local_hidden_units)
    cols_mine = lax.dynamic_slice_in_dim(grad_all, tensor_index * local_columns, local_columns, 1)
    cols_blocks = cols_mine.reshape(block_count, BLOCK, local_columns)
    a_blocks = jnp.einsum(
        "yz,zuo->yuo", block_selector, adapter_input_factor, preferred_element_type=jnp.float32
    ).astype(jnp.bfloat16)
    b_blocks = jnp.einsum(
        "vl,lyt->vyt", block_selector, adapter_output_factor, preferred_element_type=jnp.float32
    ).astype(jnp.bfloat16)
    part_in = jnp.einsum(
        "btf,bfr->btr", hidden_blocks, a_blocks, preferred_element_type=jnp.float32
    )
    part_out = jnp.einsum("btc,brc->btr", cols_blocks, b_blocks, preferred_element_type=jnp.float32)
    lowrank_input, lowrank_output = lax.psum((part_in, part_out), "tensor")
    lowrank_input = lowrank_input.astype(jnp.bfloat16)
    lowrank_output = lowrank_output.astype(jnp.bfloat16)
    gate_full, up_full, down_full = (
        lax.all_gather(gate_matrix, "dp", axis=0, tiled=True),
        lax.all_gather(up_matrix, "dp", axis=0, tiled=True),
        lax.all_gather(down_matrix, "dp", axis=0, tiled=True),
    )
    hidden_gradient = jnp.dot(grad_all, down_full, preferred_element_type=jnp.float32)
    additional_term = jnp.einsum(
        "btr,bfr->btf", lowrank_output, a_blocks, preferred_element_type=jnp.float32
    )
    hidden_gradient = hidden_gradient + ADAPTER_SCALE * additional_term.reshape(
        local_token_rows, local_hidden_units
    )
    gate_grad = (
        hidden_gradient * upper * sigmoid_gate * (1.0 + gate * (1.0 - sigmoid_gate))
    ).astype(jnp.bfloat16)
    up_grad = (hidden_gradient * silu_gate).astype(jnp.bfloat16)
    outer_product_input = jnp.einsum(
        "btf,btr->bfr", hidden_blocks, lowrank_output, preferred_element_type=jnp.float32
    )
    outer_product_output = jnp.einsum(
        "btr,btc->brc", lowrank_input, cols_blocks, preferred_element_type=jnp.float32
    )
    slot_onehot = (
        jnp.arange(adapter_list, dtype=jnp.int32)[:, None] == adapter_grad_slot[None, :]
    ).astype(jnp.float32)
    slot_block_mask = jnp.dot(slot_onehot, block_onehot.T)
    input_factor_terms = ADAPTER_SCALE * jnp.einsum(
        "pc,cdw->pdw", slot_block_mask, outer_product_input
    )
    output_factor_terms = ADAPTER_SCALE * jnp.einsum(
        "fn,nlv->flv", slot_block_mask, outer_product_output
    )
    owned_a, owned_b = (
        lax.psum_scatter(input_factor_terms, "dp", scatter_dimension=0, tiled=True),
        lax.psum_scatter(output_factor_terms, "dp", scatter_dimension=0, tiled=True),
    )
    grad_a = owned_a.astype(jnp.bfloat16)
    grad_b = owned_b.astype(jnp.bfloat16)
    first = lax.dot_general(
        gate_grad, gate_full, (((1,), (1,)), ((), ())), preferred_element_type=jnp.float32
    )
    second = lax.dot_general(
        up_grad, up_full, (((1,), (1,)), ((), ())), preferred_element_type=jnp.float32
    )
    summed = lax.psum_scatter(first + second, "tensor", scatter_dimension=0, tiled=True)
    input_grad = summed.astype(jnp.bfloat16)
    return (input_grad, grad_a, grad_b)


def solution(mesh):
    return jax.shard_map(
        grid_body if mesh.shape["tensor"] == 8 and mesh.shape["dp"] == 2 else body,
        mesh=mesh,
        in_specs=(
            P(("groups", "dp", "tensor"), None),
            P(("groups", "dp"), "tensor"),
            P(("groups", "dp"), "tensor"),
            P("dp", "tensor"),
            P("dp", "tensor"),
            P("dp", "tensor"),
            P(None, "tensor", None),
            P(None, None, "tensor"),
            P("groups"),
            P("groups", None),
            P(),
        ),
        out_specs=(
            P(("groups", "dp", "tensor"), None),
            P(("groups", "dp"), "tensor", None),
            P(("groups", "dp"), None, "tensor"),
        ),
        check_vma=False,
    )
```

```python
import functools

import jax
import jax.numpy as jnp
from jax import lax
from jax.experimental import pallas as pl
from jax.experimental.pallas import tpu as pltpu
from jax.sharding import PartitionSpec as P

BLOCK = 128


ADAPTER_SCALE = 2.0

F32 = jnp.float32
BF16 = jnp.bfloat16
MIB = 1024 * 1024

Y_SWAP = [(t, t ^ 1) for t in range(8)]
PAIR = [(t, t ^ 2) for t in range(8)]
FAR = [(t, t ^ 4) for t in range(8)]
MID = [(2, 4), (3, 5), (4, 2), (5, 3)]
OUTWARD = [(2, 0), (3, 1), (4, 6), (5, 7)]
INWARD = [(0, 2), (1, 3), (6, 4), (7, 5)]
CORES = [(0, 1), (1, 0)]

M_T, M_Y, M_D, M_Z, M_SLOT_ADAPTER, M_ADAPTER, M_GRAD_SLOT = 0, 1, 2, 3, 7, 11, 15


def nt_dot(a, b):
    return lax.dot_general(a, b, (((1,), (1,)), ((), ())), preferred_element_type=F32)


def tn_dot(a, b):
    return lax.dot_general(a, b, (((0,), (0,)), ((), ())), preferred_element_type=F32)


def call(
    kernel, meta, args, grid, in_specs, out_specs, out_shape, scratch=(), vmem=48, after=(), cost=(1000, 1000)
):
    first, extra = len(args), len(after)

    def run(m, *refs):
        kernel(m, *refs[:first], *refs[first + extra :])

    return pl.pallas_call(
        run,
        grid_spec=pltpu.PrefetchScalarGridSpec(
            num_scalar_prefetch=1,
            grid=grid,
            in_specs=list(in_specs) + [pl.BlockSpec(memory_space=pl.ANY)] * extra,
            out_specs=out_specs,
            scratch_shapes=list(scratch),
        ),
        out_shape=out_shape,
        compiler_params=pltpu.CompilerParams(vmem_limit_bytes=vmem * MIB),
        cost_estimate=pl.CostEstimate(flops=cost[0], bytes_accessed=cost[1], transcendentals=0),
    )(meta, *args, *after)


def pack_halves(p):
    h = p.shape[0] // 2
    return jnp.concatenate([p[:h], p[h:]], axis=1)


def unpack_halves(p):
    h = p.shape[1] // 2
    return jnp.concatenate([p[:, :h], p[:, h:]], axis=0)


def hidden_kernel(m, gate_ref, up_ref, a_ref, hidden_ref, low_ref):
    g = gate_ref[...].astype(F32)
    hidden = (g * jax.nn.sigmoid(g) * up_ref[...].astype(F32)).astype(BF16)
    hidden_ref[...] = hidden
    low_ref[...] = pack_halves(nt_dot(hidden, a_ref[0]))


def hidden_and_low_in(meta, gate_act, up_act, a_t):
    rows, width = gate_act.shape
    rank = a_t.shape[1]
    blocks = rows // BLOCK
    return call(
        hidden_kernel,
        meta,
        (gate_act, up_act, a_t),
        (blocks,),
        [
            pl.BlockSpec((BLOCK, width), lambda b, m: (b, 0)),
            pl.BlockSpec((BLOCK, width), lambda b, m: (b, 0)),
            pl.BlockSpec((1, rank, width), lambda b, m: (m[M_ADAPTER + b], 0, 0)),
        ],
        [
            pl.BlockSpec((BLOCK, width), lambda b, m: (b, 0)),
            pl.BlockSpec((BLOCK // 2, 2 * rank), lambda b, m: (b, 0)),
        ],
        [
            jax.ShapeDtypeStruct((rows, width), BF16),
            jax.ShapeDtypeStruct((rows // 2, 2 * rank), F32),
        ],
    )


def low_out_kernel(m, *refs):
    shards, b_ref, low_in_ref = refs[:8], refs[8], refs[9]
    cols_ref, full_ref, short_ref = refs[10:]
    rows = shards[0].shape[0]
    y = m[M_Y]
    for s in range(4):
        z = m[M_Z + s]
        own, other = shards[2 * s][...], shards[2 * s + 1][...]
        first = jnp.where(y == 0, own, other)
        second = jnp.where(y == 0, other, own)
        tokens = jnp.concatenate([first, second], axis=0)
        cols_ref[pl.ds(pl.multiple_of(z * 2 * rows, 2 * rows), 2 * rows), :] = tokens
        part = pack_halves(nt_dot(tokens, b_ref[m[M_SLOT_ADAPTER + s]]))
        at = pl.ds(pl.multiple_of(z * rows, rows), rows)
        full_ref[at, :] = part
        short_ref[at, :] = part.astype(BF16)
    full_ref[4 * rows :] = low_in_ref[...]
    short_ref[4 * rows :] = low_in_ref[...].astype(BF16)


def low_parts(meta, shards, b, low_in, after):
    rows = shards[0].shape[0]
    adapters, rank, columns = b.shape
    out = (8 * rows, 2 * rank)
    return call(
        low_out_kernel,
        meta,
        (*shards, b, low_in),
        (1,),
        [pl.BlockSpec((rows, columns), lambda i, m: (0, m[M_T]))] * 8
        + [pl.BlockSpec((adapters, rank, columns), lambda i, m: (0, 0, 0))]
        + [pl.BlockSpec((4 * rows, 2 * rank), lambda i, m: (0, 0))],
        [pl.BlockSpec((8 * rows, columns), lambda i, m: (0, 0))]
        + [pl.BlockSpec(out, lambda i, m: (0, 0))] * 2,
        [
            jax.ShapeDtypeStruct((8 * rows, columns), BF16),
            jax.ShapeDtypeStruct(out, F32),
            jax.ShapeDtypeStruct(out, BF16),
        ],
        after=after,
    )


def hidden_grad_kernel(count, m, *refs):
    mine, other = refs[:count], refs[count : 2 * count]
    down_mine, down_other, out_ref, lhs = refs[2 * count :]
    rows = mine[0].shape[0]

    @pl.when(pl.program_id(0) == 0)
    def _():
        for s in range(count):
            lhs[0, s * rows : (s + 1) * rows] = mine[s][...]
            lhs[1, s * rows : (s + 1) * rows] = other[s][...]

    total = jnp.dot(lhs[0], down_mine[...], preferred_element_type=F32)
    out_ref[...] = total + jnp.dot(lhs[1], down_other[...], preferred_element_type=F32)


def hidden_grad(meta, shards, mine, other, span, after=()):
    rows = shards[0].shape[0]
    half = mine.shape[0]
    start, width, step = span
    count = len(shards)
    total = rows * count
    return call(
        functools.partial(hidden_grad_kernel, count),
        meta,
        (*shards, *shards, mine, other),
        (width // step,),
        [pl.BlockSpec((rows, half), lambda n, m: (0, m[M_D]))] * count
        + [pl.BlockSpec((rows, half), lambda n, m: (0, 1 - m[M_D]))] * count
        + [pl.BlockSpec((half, step), lambda n, m: (0, n + start // step))] * 2,
        pl.BlockSpec((total, step), lambda n, m: (0, n)),
        jax.ShapeDtypeStruct((total, width), F32),
        scratch=[pltpu.VMEM((2, total, half), BF16)],
        after=after,
    )


def act_grad_kernel(spans, m, *refs):
    hg_refs, (gate_ref, up_ref, low_ref, a_ref, out_ref) = refs[: len(spans)], refs[len(spans) :]
    j = pl.program_id(0)
    y = m[M_Y]
    rank = low_ref.shape[1] // 2
    second = jnp.where(j == 0, y, 1 - y) == 1
    low = jnp.where(second, low_ref[:, rank:], low_ref[:, :rank])
    for hg_ref, (start, width, _) in zip(hg_refs, spans):
        at = slice(start, start + width)
        hg = hg_ref[...] + ADAPTER_SCALE * jnp.dot(low, a_ref[0, :, at], preferred_element_type=F32)
        g = gate_ref[:, at].astype(F32)
        u = up_ref[:, at].astype(F32)
        sig = jax.nn.sigmoid(g)
        out_ref[0, :, at] = (hg * u * sig * (1.0 + g * (1.0 - sig))).astype(BF16)
        out_ref[1, :, at] = (hg * (g * sig)).astype(BF16)


def act_grad(meta, slot, spans, hgs, gate_act, up_act, low, a_t, after=()):
    rank, width = a_t.shape[1:]
    rows = BLOCK // 2

    def shard_of(j, m):
        y = m[M_Y]
        return (m[M_Z + slot] * 2 + y + j * (1 - 2 * y), 0)

    return call(
        functools.partial(act_grad_kernel, spans),
        meta,
        (*hgs, gate_act, up_act, low, a_t),
        (2,),
        [pl.BlockSpec((rows, w), lambda j, m: ((slot % 2) * 2 + j, 0)) for _, w, _ in spans]
        + [
            pl.BlockSpec((rows, width), shard_of),
            pl.BlockSpec((rows, width), shard_of),
            pl.BlockSpec((rows, 2 * rank), lambda j, m: (m[M_Z + slot], 0)),
            pl.BlockSpec((1, rank, width), lambda j, m: (m[M_SLOT_ADAPTER + slot], 0, 0)),
        ],
        pl.BlockSpec((2, rows, width), lambda j, m: (0, j, 0)),
        jax.ShapeDtypeStruct((2, 2 * rows, width), BF16),
        after=after,
    )


def input_grad_kernel(m, mine_ref, other_ref, gate_ref, up_ref, keep_ref, send_ref, lhs):
    rows = mine_ref.shape[1] // 2

    @pl.when(pl.program_id(0) == 0)
    def _():
        for i in range(2):
            for y in range(2):
                lhs[i, (2 * y) * rows : (2 * y + 1) * rows] = mine_ref[i, y * rows : (y + 1) * rows]
                lhs[i, (2 * y + 1) * rows : (2 * y + 2) * rows] = other_ref[i, y * rows : (y + 1) * rows]

    total = nt_dot(lhs[0], gate_ref[...]) + nt_dot(lhs[1], up_ref[...])
    keep_ref[...] = total[: 2 * rows].astype(BF16)
    send_ref[...] = total[2 * rows :].astype(BF16)


def input_grad_parts(meta, mine, other, gate, up, after=()):
    rows, width = mine.shape[1:]
    half = gate.shape[0]
    step = 512
    out = jax.ShapeDtypeStruct((rows, half), BF16)
    return call(
        input_grad_kernel,
        meta,
        (mine, other, gate, up),
        (half // step,),
        [pl.BlockSpec((2, rows, width), lambda n, m: (0, 0, 0))] * 2
        + [pl.BlockSpec((step, width), lambda n, m: (n, 0))] * 2,
        [pl.BlockSpec((rows, step), lambda n, m: (0, n))] * 2,
        [out, out],
        scratch=[pltpu.VMEM((2, 2 * rows, width), BF16)],
        after=after,
    )


def owner_kernel(m, low_ref, features_ref, keep_ref, send_ref, lhs):
    owned, rank = keep_ref.shape[:2]
    blocks = features_ref.shape[0] // BLOCK
    rows = low_ref.shape[0] // blocks
    d = m[M_D]

    @pl.when(pl.program_id(0) == 0)
    def _():
        for b in range(blocks):
            low = unpack_halves(low_ref[b * rows : (b + 1) * rows, :])
            masked = []
            for owner in (d, 1 - d):
                for i in range(owned):
                    hit = m[M_GRAD_SLOT + b] == owner * owned + i
                    masked.append(jnp.where(hit, low, jnp.zeros_like(low)))
            lhs[b * BLOCK : (b + 1) * BLOCK] = jnp.concatenate(masked, axis=1)

    total = (ADAPTER_SCALE * tn_dot(lhs[...], features_ref[...])).astype(BF16)
    for i in range(owned):
        keep_ref[i] = total[i * rank : (i + 1) * rank]
        send_ref[i] = total[(owned + i) * rank : (owned + i + 1) * rank]


def owner_grads(meta, low, which, features, owned, after=()):
    tokens, width = features.shape
    half_rows, double = low.shape[0] // 2, low.shape[1]
    rank = double // 2
    step = 640
    out = jax.ShapeDtypeStruct((owned, rank, width), BF16)
    return call(
        owner_kernel,
        meta,
        (low, features),
        (width // step,),
        [
            pl.BlockSpec((half_rows, double), lambda n, m: (which, 0)),
            pl.BlockSpec((tokens, step), lambda n, m: (0, n)),
        ],
        [pl.BlockSpec((owned, rank, step), lambda n, m: (0, 0, n))] * 2,
        [out, out],
        scratch=[pltpu.VMEM((tokens, 2 * owned * rank), BF16)],
        after=after,
    )


def add_kernel(count, m, *refs):
    total = refs[0][...].astype(F32)
    for r in refs[1:count]:
        total += r[...].astype(F32)
    for r in refs[count:]:
        r[...] = total.astype(r.dtype)


def add_after(meta, xs, after, kinds=(BF16,), steps=1):
    rows, width = xs[0].shape
    spec = pl.BlockSpec((rows // steps, width), lambda i, m: (i, 0))
    out = call(
        functools.partial(add_kernel, len(xs)),
        meta,
        xs,
        (steps,),
        [spec] * len(xs),
        [spec] * len(kinds),
        [jax.ShapeDtypeStruct((rows, width), k) for k in kinds],
        vmem=16,
        after=after,
    )
    return out if len(kinds) > 1 else out[0]


def final_kernel(m, *refs):
    total = refs[0][...].astype(F32)
    for r in refs[1:-2]:
        total += r[...].astype(F32)
    rows = refs[-1].shape[0]
    refs[-2][...] = total[:rows].astype(BF16)
    refs[-1][...] = total[rows:].astype(BF16)


def final_sum(meta, xs, after):
    rows, width = xs[0].shape
    return call(
        final_kernel,
        meta,
        xs,
        (1,),
        [pl.BlockSpec((rows, width), lambda i, m: (0, 0))] * len(xs),
        [pl.BlockSpec((rows // 2, width), lambda i, m: (0, 0))] * 2,
        [jax.ShapeDtypeStruct((rows // 2, width), BF16)] * 2,
        vmem=16,
        after=after,
    )


def add(*xs):
    return functools.reduce(jnp.add, [x.astype(F32) for x in xs]).astype(BF16)


def tied(x, *others):
    return lax.optimization_barrier((x, *others))[0]


def grid_body(
    cotangent,
    gate_act,
    up_act,
    gate_matrix,
    up_matrix,
    down_matrix,
    adapter_input_factor,
    adapter_output_factor,
    padded_block_segment,
    segment_adapter_index,
    adapter_grad_slot,
):
    adapters = adapter_input_factor.shape[0]
    blocks = gate_act.shape[0] // BLOCK
    d = lax.axis_index("dp")
    t = lax.axis_index("tensor")
    z, y = t // 2, t % 2
    low_side = z < 2
    slots_z = jnp.stack([z, z ^ 1, jnp.where(low_side, 2, 1), jnp.where(low_side, 3, 0)])
    segments_here = lax.dynamic_slice_in_dim(padded_block_segment, d * blocks, blocks)

    def pick(table, index):
        hit = index[:, None] == jnp.arange(table.shape[0], dtype=jnp.int32)[None, :]
        return jnp.sum(jnp.where(hit, table[None, :], 0), axis=1)

    block_adapter = pick(segment_adapter_index[:, 0], segments_here)
    meta = jnp.concatenate(
        [
            jnp.stack([t, y, d]),
            slots_z,
            pick(block_adapter, slots_z),
            block_adapter,
            pick(adapter_grad_slot, block_adapter),
        ]
    ).astype(jnp.int32)
    a_t = jnp.swapaxes(adapter_input_factor, 1, 2)
    send = functools.partial(lax.ppermute, axis_name="tensor")
    swap_cores = functools.partial(lax.ppermute, axis_name="dp", perm=CORES)
    at_end = (z == 0) | (z == 3)

    width = gate_act.shape[1]
    step = width * 2 // 5
    spans = ((0, step, step // 2), (step, step, step // 2), (2 * step, width - 2 * step, width - 2 * step))

    down_other = swap_cores(down_matrix)
    pair = send(cotangent, perm=PAIR)
    mid = send(cotangent, perm=MID)
    y0 = send(cotangent, perm=Y_SWAP)
    hidden, low_in = hidden_and_low_in(meta, gate_act, up_act, a_t)
    y1 = send(tied(pair, y0, low_in), perm=Y_SWAP)
    pair_mid = send(tied(pair, low_in), perm=MID)
    mid_out = send(tied(mid, low_in), perm=OUTWARD)
    slot2 = jnp.where(at_end, mid_out, mid)
    y2 = send(tied(slot2, y1), perm=Y_SWAP)
    far_out = send(pair_mid, perm=OUTWARD)
    hg_near, last = [], (low_in,)
    for span in spans:
        hg_near.append(hidden_grad(meta, (cotangent, y0, pair, y1), down_matrix, down_other, span, last))
        last = (hg_near[-1],)
    slot3 = jnp.where(at_end, tied(far_out, hg_near[0]), pair_mid)
    y3 = send(tied(slot3, y2), perm=Y_SWAP)

    far = (slot2, y2, slot3, y3)
    near = (cotangent, y0, pair, y1)
    columns, low_sum, low = low_parts(meta, near + far, adapter_output_factor, low_in, last)
    hg_far = []
    for perm, span in zip((Y_SWAP, PAIR, FAR), spans):
        got = send(low, perm=perm)
        hg_far.append(hidden_grad(meta, far, down_matrix, down_other, span, (low,)))
        low_sum, low = add_after(meta, (low_sum, got), (hg_far[-1],), (F32, BF16))

    def grads(slot, after):
        hgs = hg_far if slot >= 2 else hg_near
        return act_grad(meta, slot, spans, hgs, gate_act, up_act, low, a_t, after)

    def parts(mine, other, after):
        keep, give = input_grad_parts(meta, mine, other, gate_matrix, up_matrix, after)
        return keep, send(give, perm=Y_SWAP), give

    mine3 = grads(3, ())
    other3 = swap_cores(mine3)
    mine2 = grads(2, (mine3,))
    other2 = swap_cores(tied(mine2, other3))
    keep3, got3, give3 = parts(mine3, other3, (mine2,))
    mine1 = grads(1, (give3,))
    keep2, got2, give2 = parts(mine2, other2, (mine1,))
    other1 = swap_cores(tied(mine1, other2))
    sum3 = add_after(meta, (keep3, got3), (give2,))
    far_in = send(sum3, perm=INWARD)
    mine0 = grads(0, (sum3,))
    keep1, got1, give1 = parts(mine1, other1, (mine0,))
    other0 = swap_cores(tied(mine0, other1))
    sum2 = add_after(meta, (keep2, got2), (give1,))
    mid_in = send(sum2, perm=INWARD)
    sum3 = add_after(meta, (sum3, far_in), (sum2,))
    far_mid = send(sum3, perm=MID)
    keep0, got0, give0 = parts(mine0, other0, (sum3,))
    sum1 = add_after(meta, (keep1, got1, far_mid), (give0,))
    from_pair = send(sum1, perm=PAIR)
    sum2 = add_after(meta, (sum2, mid_in), (sum1,))
    from_mid = send(sum2, perm=MID)
    owned = adapters // 2
    keep_a, give_a = owner_grads(meta, low, 0, hidden, owned, (sum2,))
    keep_b, give_b = owner_grads(meta, low, 1, columns, owned, (keep_a,))
    own, give = final_sum(meta, (keep0, got0, from_pair, from_mid), (keep_b,))
    grad_b = add(keep_b, swap_cores(give_b))
    shape = keep_a.shape
    flat = (shape[0] * shape[1], shape[2])
    grad_a = add_after(
        meta, (keep_a.reshape(flat), swap_cores(give_a).reshape(flat)), (give,), steps=2
    )
    got = swap_cores(give)
    input_grad = jnp.where(
        d == 0, jnp.concatenate([own, got], axis=1), jnp.concatenate([got, own], axis=1)
    )
    grad_a = jnp.swapaxes(grad_a.reshape(shape), 1, 2)
    return (input_grad, grad_a, grad_b)


def body(
    cotangent,
    gate_activation_stored,
    up_activation_stored,
    gate_matrix,
    up_matrix,
    down_matrix,
    adapter_input_factor,
    adapter_output_factor,
    padded_block_segment,
    segment_adapter_index,
    adapter_grad_slot,
):
    local_token_rows = gate_activation_stored.shape[0]
    local_hidden_units = gate_activation_stored.shape[1]
    adapter_list = adapter_input_factor.shape[0]
    local_columns = adapter_output_factor.shape[2]
    seg_count = segment_adapter_index.shape[0]
    block_count = local_token_rows // BLOCK
    dp_index = lax.axis_index("dp")
    tensor_index = lax.axis_index("tensor")
    grad_all = lax.all_gather(cotangent, "tensor", axis=0, tiled=True)
    segments_here = lax.dynamic_slice_in_dim(
        padded_block_segment, dp_index * block_count, block_count
    )
    seg_onehot = (segments_here[:, None] == jnp.arange(seg_count, dtype=jnp.int32)[None, :]).astype(
        jnp.float32
    )
    adapter_onehot = (
        segment_adapter_index[:, 0][:, None] == jnp.arange(adapter_list, dtype=jnp.int32)[None, :]
    ).astype(jnp.float32)
    block_onehot = jnp.dot(seg_onehot, adapter_onehot)
    block_selector = block_onehot.astype(jnp.bfloat16)
    gate = gate_activation_stored.astype(jnp.float32)
    upper = up_activation_stored.astype(jnp.float32)
    sigmoid_gate = jax.nn.sigmoid(gate)
    silu_gate = gate * sigmoid_gate
    hidden_state = (silu_gate * upper).astype(jnp.bfloat16)
    hidden_blocks = hidden_state.reshape(block_count, BLOCK, local_hidden_units)
    cols_mine = lax.dynamic_slice_in_dim(grad_all, tensor_index * local_columns, local_columns, 1)
    cols_blocks = cols_mine.reshape(block_count, BLOCK, local_columns)
    a_blocks = jnp.einsum(
        "yz,zuo->yuo", block_selector, adapter_input_factor, preferred_element_type=jnp.float32
    ).astype(jnp.bfloat16)
    b_blocks = jnp.einsum(
        "vl,lyt->vyt", block_selector, adapter_output_factor, preferred_element_type=jnp.float32
    ).astype(jnp.bfloat16)
    part_in = jnp.einsum(
        "btf,bfr->btr", hidden_blocks, a_blocks, preferred_element_type=jnp.float32
    )
    part_out = jnp.einsum("btc,brc->btr", cols_blocks, b_blocks, preferred_element_type=jnp.float32)
    lowrank_input, lowrank_output = lax.psum((part_in, part_out), "tensor")
    lowrank_input = lowrank_input.astype(jnp.bfloat16)
    lowrank_output = lowrank_output.astype(jnp.bfloat16)
    gate_full, up_full, down_full = (
        lax.all_gather(gate_matrix, "dp", axis=0, tiled=True),
        lax.all_gather(up_matrix, "dp", axis=0, tiled=True),
        lax.all_gather(down_matrix, "dp", axis=0, tiled=True),
    )
    hidden_gradient = jnp.dot(grad_all, down_full, preferred_element_type=jnp.float32)
    additional_term = jnp.einsum(
        "btr,bfr->btf", lowrank_output, a_blocks, preferred_element_type=jnp.float32
    )
    hidden_gradient = hidden_gradient + ADAPTER_SCALE * additional_term.reshape(
        local_token_rows, local_hidden_units
    )
    gate_grad = (
        hidden_gradient * upper * sigmoid_gate * (1.0 + gate * (1.0 - sigmoid_gate))
    ).astype(jnp.bfloat16)
    up_grad = (hidden_gradient * silu_gate).astype(jnp.bfloat16)
    outer_product_input = jnp.einsum(
        "btf,btr->bfr", hidden_blocks, lowrank_output, preferred_element_type=jnp.float32
    )
    outer_product_output = jnp.einsum(
        "btr,btc->brc", lowrank_input, cols_blocks, preferred_element_type=jnp.float32
    )
    slot_onehot = (
        jnp.arange(adapter_list, dtype=jnp.int32)[:, None] == adapter_grad_slot[None, :]
    ).astype(jnp.float32)
    slot_block_mask = jnp.dot(slot_onehot, block_onehot.T)
    input_factor_terms = ADAPTER_SCALE * jnp.einsum(
        "pc,cdw->pdw", slot_block_mask, outer_product_input
    )
    output_factor_terms = ADAPTER_SCALE * jnp.einsum(
        "fn,nlv->flv", slot_block_mask, outer_product_output
    )
    owned_a, owned_b = (
        lax.psum_scatter(input_factor_terms, "dp", scatter_dimension=0, tiled=True),
        lax.psum_scatter(output_factor_terms, "dp", scatter_dimension=0, tiled=True),
    )
    grad_a = owned_a.astype(jnp.bfloat16)
    grad_b = owned_b.astype(jnp.bfloat16)
    first = lax.dot_general(
        gate_grad, gate_full, (((1,), (1,)), ((), ())), preferred_element_type=jnp.float32
    )
    second = lax.dot_general(
        up_grad, up_full, (((1,), (1,)), ((), ())), preferred_element_type=jnp.float32
    )
    summed = lax.psum_scatter(first + second, "tensor", scatter_dimension=0, tiled=True)
    input_grad = summed.astype(jnp.bfloat16)
    return (input_grad, grad_a, grad_b)


def solution(mesh):
    return jax.shard_map(
        grid_body if mesh.shape["tensor"] == 8 and mesh.shape["dp"] == 2 else body,
        mesh=mesh,
        in_specs=(
            P(("groups", "dp", "tensor"), None),
            P(("groups", "dp"), "tensor"),
            P(("groups", "dp"), "tensor"),
            P("dp", "tensor"),
            P("dp", "tensor"),
            P("dp", "tensor"),
            P(None, "tensor", None),
            P(None, None, "tensor"),
            P("groups"),
            P("groups", None),
            P(),
        ),
        out_specs=(
            P(("groups", "dp", "tensor"), None),
            P(("groups", "dp"), "tensor", None),
            P(("groups", "dp"), None, "tensor"),
        ),
        check_vma=False,
    )
```

```python
import functools

import jax
import jax.numpy as jnp
from jax import lax
from jax.experimental import pallas as pl
from jax.experimental.pallas import tpu as pltpu
from jax.sharding import PartitionSpec as P

BLOCK = 128


ADAPTER_SCALE = 2.0

F32 = jnp.float32
BF16 = jnp.bfloat16
MIB = 1024 * 1024

Y_SWAP = [(t, t ^ 1) for t in range(8)]
PAIR = [(t, t ^ 2) for t in range(8)]
FAR = [(t, t ^ 4) for t in range(8)]
MID = [(2, 4), (3, 5), (4, 2), (5, 3)]
OUTWARD = [(2, 0), (3, 1), (4, 6), (5, 7)]
INWARD = [(0, 2), (1, 3), (6, 4), (7, 5)]
CORES = [(0, 1), (1, 0)]

M_T, M_Y, M_D, M_Z, M_SLOT_ADAPTER, M_ADAPTER, M_GRAD_SLOT = 0, 1, 2, 3, 7, 11, 15


def nt_dot(a, b):
    return lax.dot_general(a, b, (((1,), (1,)), ((), ())), preferred_element_type=F32)


def tn_dot(a, b):
    return lax.dot_general(a, b, (((0,), (0,)), ((), ())), preferred_element_type=F32)


def call(
    kernel, meta, args, grid, in_specs, out_specs, out_shape, scratch=(), vmem=26, after=(), cost=(1000, 1000)
):
    first, extra = len(args), len(after)

    def run(m, *refs):
        kernel(m, *refs[:first], *refs[first + extra :])

    return pl.pallas_call(
        run,
        grid_spec=pltpu.PrefetchScalarGridSpec(
            num_scalar_prefetch=1,
            grid=grid,
            in_specs=list(in_specs) + [pl.BlockSpec(memory_space=pl.ANY)] * extra,
            out_specs=out_specs,
            scratch_shapes=list(scratch),
        ),
        out_shape=out_shape,
        compiler_params=pltpu.CompilerParams(vmem_limit_bytes=vmem * MIB),
        cost_estimate=pl.CostEstimate(flops=cost[0], bytes_accessed=cost[1], transcendentals=0),
    )(meta, *args, *after)


def pack_halves(p):
    h = p.shape[0] // 2
    return jnp.concatenate([p[:h], p[h:]], axis=1)


def unpack_halves(p):
    h = p.shape[1] // 2
    return jnp.concatenate([p[:, :h], p[:, h:]], axis=0)


def hidden_kernel(m, gate_ref, up_ref, a_ref, hidden_ref, low_ref):
    g = gate_ref[...].astype(F32)
    hidden = (g * jax.nn.sigmoid(g) * up_ref[...].astype(F32)).astype(BF16)
    hidden_ref[...] = hidden
    low_ref[...] = pack_halves(nt_dot(hidden, a_ref[0]))


def hidden_and_low_in(meta, gate_act, up_act, a_t):
    rows, width = gate_act.shape
    rank = a_t.shape[1]
    blocks = rows // BLOCK
    return call(
        hidden_kernel,
        meta,
        (gate_act, up_act, a_t),
        (blocks,),
        [
            pl.BlockSpec((BLOCK, width), lambda b, m: (b, 0)),
            pl.BlockSpec((BLOCK, width), lambda b, m: (b, 0)),
            pl.BlockSpec((1, rank, width), lambda b, m: (m[M_ADAPTER + b], 0, 0)),
        ],
        [
            pl.BlockSpec((BLOCK, width), lambda b, m: (b, 0)),
            pl.BlockSpec((BLOCK // 2, 2 * rank), lambda b, m: (b, 0)),
        ],
        [
            jax.ShapeDtypeStruct((rows, width), BF16),
            jax.ShapeDtypeStruct((rows // 2, 2 * rank), F32),
        ],
    )


def low_out_kernel(m, *refs):
    shards, b_ref, low_in_ref = refs[:8], refs[8], refs[9]
    cols_ref, full_ref, short_ref = refs[10:]
    rows = shards[0].shape[0]
    y = m[M_Y]
    for s in range(4):
        z = m[M_Z + s]
        own, other = shards[2 * s][...], shards[2 * s + 1][...]
        first = jnp.where(y == 0, own, other)
        second = jnp.where(y == 0, other, own)
        tokens = jnp.concatenate([first, second], axis=0)
        cols_ref[pl.ds(pl.multiple_of(z * 2 * rows, 2 * rows), 2 * rows), :] = tokens
        part = pack_halves(nt_dot(tokens, b_ref[m[M_SLOT_ADAPTER + s]]))
        at = pl.ds(pl.multiple_of(z * rows, rows), rows)
        full_ref[at, :] = part
        short_ref[at, :] = part.astype(BF16)
    full_ref[4 * rows :] = low_in_ref[...]
    short_ref[4 * rows :] = low_in_ref[...].astype(BF16)


def low_parts(meta, shards, b, low_in, after):
    rows = shards[0].shape[0]
    adapters, rank, columns = b.shape
    out = (8 * rows, 2 * rank)
    return call(
        low_out_kernel,
        meta,
        (*shards, b, low_in),
        (1,),
        [pl.BlockSpec((rows, columns), lambda i, m: (0, m[M_T]))] * 8
        + [pl.BlockSpec((adapters, rank, columns), lambda i, m: (0, 0, 0))]
        + [pl.BlockSpec((4 * rows, 2 * rank), lambda i, m: (0, 0))],
        [pl.BlockSpec((8 * rows, columns), lambda i, m: (0, 0))]
        + [pl.BlockSpec(out, lambda i, m: (0, 0))] * 2,
        [
            jax.ShapeDtypeStruct((8 * rows, columns), BF16),
            jax.ShapeDtypeStruct(out, F32),
            jax.ShapeDtypeStruct(out, BF16),
        ],
        after=after,
    )


def hidden_grad_kernel(count, m, *refs):
    mine, other = refs[:count], refs[count : 2 * count]
    down_mine, down_other, out_ref, lhs = refs[2 * count :]
    rows = mine[0].shape[0]

    @pl.when(pl.program_id(0) == 0)
    def _():
        for s in range(count):
            lhs[0, s * rows : (s + 1) * rows] = mine[s][...]
            lhs[1, s * rows : (s + 1) * rows] = other[s][...]

    total = jnp.dot(lhs[0], down_mine[...], preferred_element_type=F32)
    out_ref[...] = total + jnp.dot(lhs[1], down_other[...], preferred_element_type=F32)


def hidden_grad(meta, shards, mine, other, span, after=()):
    rows = shards[0].shape[0]
    half = mine.shape[0]
    start, width, step = span
    count = len(shards)
    total = rows * count
    return call(
        functools.partial(hidden_grad_kernel, count),
        meta,
        (*shards, *shards, mine, other),
        (width // step,),
        [pl.BlockSpec((rows, half), lambda n, m: (0, m[M_D]))] * count
        + [pl.BlockSpec((rows, half), lambda n, m: (0, 1 - m[M_D]))] * count
        + [pl.BlockSpec((half, step), lambda n, m: (0, n + start // step))] * 2,
        pl.BlockSpec((total, step), lambda n, m: (0, n)),
        jax.ShapeDtypeStruct((total, width), F32),
        scratch=[pltpu.VMEM((2, total, half), BF16)],
        after=after,
    )


def act_grad_kernel(spans, m, *refs):
    hg_refs, (gate_ref, up_ref, low_ref, a_ref, out_ref) = refs[: len(spans)], refs[len(spans) :]
    j = pl.program_id(0)
    y = m[M_Y]
    rank = low_ref.shape[1] // 2
    second = jnp.where(j == 0, y, 1 - y) == 1
    low = jnp.where(second, low_ref[:, rank:], low_ref[:, :rank])
    for hg_ref, (start, width, _) in zip(hg_refs, spans):
        at = slice(start, start + width)
        hg = hg_ref[...] + ADAPTER_SCALE * jnp.dot(low, a_ref[0, :, at], preferred_element_type=F32)
        g = gate_ref[:, at].astype(F32)
        u = up_ref[:, at].astype(F32)
        sig = jax.nn.sigmoid(g)
        out_ref[0, :, at] = (hg * u * sig * (1.0 + g * (1.0 - sig))).astype(BF16)
        out_ref[1, :, at] = (hg * (g * sig)).astype(BF16)


def act_grad(meta, slot, spans, hgs, gate_act, up_act, low, a_t, after=()):
    rank, width = a_t.shape[1:]
    rows = BLOCK // 2

    def shard_of(j, m):
        y = m[M_Y]
        return (m[M_Z + slot] * 2 + y + j * (1 - 2 * y), 0)

    return call(
        functools.partial(act_grad_kernel, spans),
        meta,
        (*hgs, gate_act, up_act, low, a_t),
        (2,),
        [pl.BlockSpec((rows, w), lambda j, m: ((slot % 2) * 2 + j, 0)) for _, w, _ in spans]
        + [
            pl.BlockSpec((rows, width), shard_of),
            pl.BlockSpec((rows, width), shard_of),
            pl.BlockSpec((rows, 2 * rank), lambda j, m: (m[M_Z + slot], 0)),
            pl.BlockSpec((1, rank, width), lambda j, m: (m[M_SLOT_ADAPTER + slot], 0, 0)),
        ],
        pl.BlockSpec((2, rows, width), lambda j, m: (0, j, 0)),
        jax.ShapeDtypeStruct((2, 2 * rows, width), BF16),
        after=after,
    )


def input_grad_kernel(m, mine_ref, other_ref, gate_ref, up_ref, keep_ref, send_ref, lhs):
    rows = mine_ref.shape[1] // 2

    @pl.when(pl.program_id(0) == 0)
    def _():
        for i in range(2):
            for y in range(2):
                lhs[i, (2 * y) * rows : (2 * y + 1) * rows] = mine_ref[i, y * rows : (y + 1) * rows]
                lhs[i, (2 * y + 1) * rows : (2 * y + 2) * rows] = other_ref[i, y * rows : (y + 1) * rows]

    total = nt_dot(lhs[0], gate_ref[...]) + nt_dot(lhs[1], up_ref[...])
    keep_ref[...] = total[: 2 * rows].astype(BF16)
    send_ref[...] = total[2 * rows :].astype(BF16)


def input_grad_parts(meta, mine, other, gate, up, after=()):
    rows, width = mine.shape[1:]
    half = gate.shape[0]
    step = 512
    out = jax.ShapeDtypeStruct((rows, half), BF16)
    return call(
        input_grad_kernel,
        meta,
        (mine, other, gate, up),
        (half // step,),
        [pl.BlockSpec((2, rows, width), lambda n, m: (0, 0, 0))] * 2
        + [pl.BlockSpec((step, width), lambda n, m: (n, 0))] * 2,
        [pl.BlockSpec((rows, step), lambda n, m: (0, n))] * 2,
        [out, out],
        scratch=[pltpu.VMEM((2, 2 * rows, width), BF16)],
        after=after,
    )


def owner_kernel(m, low_ref, features_ref, keep_ref, send_ref, lhs):
    owned, rank = keep_ref.shape[:2]
    blocks = features_ref.shape[0] // BLOCK
    rows = low_ref.shape[0] // blocks
    d = m[M_D]

    @pl.when(pl.program_id(0) == 0)
    def _():
        for b in range(blocks):
            low = unpack_halves(low_ref[b * rows : (b + 1) * rows, :])
            masked = []
            for owner in (d, 1 - d):
                for i in range(owned):
                    hit = m[M_GRAD_SLOT + b] == owner * owned + i
                    masked.append(jnp.where(hit, low, jnp.zeros_like(low)))
            lhs[b * BLOCK : (b + 1) * BLOCK] = jnp.concatenate(masked, axis=1)

    total = (ADAPTER_SCALE * tn_dot(lhs[...], features_ref[...])).astype(BF16)
    for i in range(owned):
        keep_ref[i] = total[i * rank : (i + 1) * rank]
        send_ref[i] = total[(owned + i) * rank : (owned + i + 1) * rank]


def owner_grads(meta, low, which, features, owned, after=()):
    tokens, width = features.shape
    half_rows, double = low.shape[0] // 2, low.shape[1]
    rank = double // 2
    step = 640
    out = jax.ShapeDtypeStruct((owned, rank, width), BF16)
    return call(
        owner_kernel,
        meta,
        (low, features),
        (width // step,),
        [
            pl.BlockSpec((half_rows, double), lambda n, m: (which, 0)),
            pl.BlockSpec((tokens, step), lambda n, m: (0, n)),
        ],
        [pl.BlockSpec((owned, rank, step), lambda n, m: (0, 0, n))] * 2,
        [out, out],
        scratch=[pltpu.VMEM((tokens, 2 * owned * rank), BF16)],
        after=after,
    )


def add_kernel(count, m, *refs):
    total = refs[0][...].astype(F32)
    for r in refs[1:count]:
        total += r[...].astype(F32)
    for r in refs[count:]:
        r[...] = total.astype(r.dtype)


def add_after(meta, xs, after, kinds=(BF16,), steps=1):
    rows, width = xs[0].shape
    spec = pl.BlockSpec((rows // steps, width), lambda i, m: (i, 0))
    out = call(
        functools.partial(add_kernel, len(xs)),
        meta,
        xs,
        (steps,),
        [spec] * len(xs),
        [spec] * len(kinds),
        [jax.ShapeDtypeStruct((rows, width), k) for k in kinds],
        vmem=16,
        after=after,
    )
    return out if len(kinds) > 1 else out[0]


def final_kernel(m, *refs):
    total = refs[0][...].astype(F32)
    for r in refs[1:-2]:
        total += r[...].astype(F32)
    rows = refs[-1].shape[0]
    refs[-2][...] = total[:rows].astype(BF16)
    refs[-1][...] = total[rows:].astype(BF16)


def final_sum(meta, xs, after):
    rows, width = xs[0].shape
    return call(
        final_kernel,
        meta,
        xs,
        (1,),
        [pl.BlockSpec((rows, width), lambda i, m: (0, 0))] * len(xs),
        [pl.BlockSpec((rows // 2, width), lambda i, m: (0, 0))] * 2,
        [jax.ShapeDtypeStruct((rows // 2, width), BF16)] * 2,
        vmem=16,
        after=after,
    )


def add(*xs):
    return functools.reduce(jnp.add, [x.astype(F32) for x in xs]).astype(BF16)


def tied(x, *others):
    return lax.optimization_barrier((x, *others))[0]


def grid_body(
    cotangent,
    gate_act,
    up_act,
    gate_matrix,
    up_matrix,
    down_matrix,
    adapter_input_factor,
    adapter_output_factor,
    padded_block_segment,
    segment_adapter_index,
    adapter_grad_slot,
):
    adapters = adapter_input_factor.shape[0]
    blocks = gate_act.shape[0] // BLOCK
    d = lax.axis_index("dp")
    t = lax.axis_index("tensor")
    z, y = t // 2, t % 2
    low_side = z < 2
    slots_z = jnp.stack([z, z ^ 1, jnp.where(low_side, 2, 1), jnp.where(low_side, 3, 0)])
    segments_here = lax.dynamic_slice_in_dim(padded_block_segment, d * blocks, blocks)

    def pick(table, index):
        hit = index[:, None] == jnp.arange(table.shape[0], dtype=jnp.int32)[None, :]
        return jnp.sum(jnp.where(hit, table[None, :], 0), axis=1)

    block_adapter = pick(segment_adapter_index[:, 0], segments_here)
    meta = jnp.concatenate(
        [
            jnp.stack([t, y, d]),
            slots_z,
            pick(block_adapter, slots_z),
            block_adapter,
            pick(adapter_grad_slot, block_adapter),
        ]
    ).astype(jnp.int32)
    a_t = jnp.swapaxes(adapter_input_factor, 1, 2)
    send = functools.partial(lax.ppermute, axis_name="tensor")
    swap_cores = functools.partial(lax.ppermute, axis_name="dp", perm=CORES)
    at_end = (z == 0) | (z == 3)

    width = gate_act.shape[1]
    step = width * 2 // 5
    spans = ((0, step, step // 2), (step, step, step // 2), (2 * step, width - 2 * step, width - 2 * step))

    down_other = swap_cores(down_matrix)
    pair = send(cotangent, perm=PAIR)
    mid = send(cotangent, perm=MID)
    y0 = send(cotangent, perm=Y_SWAP)
    hidden, low_in = hidden_and_low_in(meta, gate_act, up_act, a_t)
    y1 = send(tied(pair, y0, low_in), perm=Y_SWAP)
    pair_mid = send(tied(pair, low_in), perm=MID)
    mid_out = send(tied(mid, low_in), perm=OUTWARD)
    slot2 = jnp.where(at_end, mid_out, mid)
    y2 = send(tied(slot2, y1), perm=Y_SWAP)
    far_out = send(pair_mid, perm=OUTWARD)
    hg_near, last = [], (low_in,)
    for span in spans:
        hg_near.append(hidden_grad(meta, (cotangent, y0, pair, y1), down_matrix, down_other, span, last))
        last = (hg_near[-1],)
    slot3 = jnp.where(at_end, tied(far_out, hg_near[0]), pair_mid)
    y3 = send(tied(slot3, y2), perm=Y_SWAP)

    far = (slot2, y2, slot3, y3)
    near = (cotangent, y0, pair, y1)
    columns, low_sum, low = low_parts(meta, near + far, adapter_output_factor, low_in, last)
    hg_far = []
    for perm, span in zip((Y_SWAP, PAIR, FAR), spans):
        got = send(low, perm=perm)
        hg_far.append(hidden_grad(meta, far, down_matrix, down_other, span, (low,)))
        low_sum, low = add_after(meta, (low_sum, got), (hg_far[-1],), (F32, BF16))

    def grads(slot, after):
        hgs = hg_far if slot >= 2 else hg_near
        return act_grad(meta, slot, spans, hgs, gate_act, up_act, low, a_t, after)

    def parts(mine, other, after):
        keep, give = input_grad_parts(meta, mine, other, gate_matrix, up_matrix, after)
        return keep, send(give, perm=Y_SWAP), give

    mine3 = grads(3, ())
    other3 = swap_cores(mine3)
    mine2 = grads(2, (mine3,))
    other2 = swap_cores(tied(mine2, other3))
    keep3, got3, give3 = parts(mine3, other3, (mine2,))
    mine1 = grads(1, (give3,))
    keep2, got2, give2 = parts(mine2, other2, (mine1,))
    other1 = swap_cores(tied(mine1, other2))
    sum3 = add_after(meta, (keep3, got3), (give2,))
    far_in = send(sum3, perm=INWARD)
    mine0 = grads(0, (sum3,))
    keep1, got1, give1 = parts(mine1, other1, (mine0,))
    other0 = swap_cores(tied(mine0, other1))
    sum2 = add_after(meta, (keep2, got2), (give1,))
    mid_in = send(sum2, perm=INWARD)
    sum3 = add_after(meta, (sum3, far_in), (sum2,))
    far_mid = send(sum3, perm=MID)
    keep0, got0, give0 = parts(mine0, other0, (sum3,))
    sum1 = add_after(meta, (keep1, got1, far_mid), (give0,))
    from_pair = send(sum1, perm=PAIR)
    sum2 = add_after(meta, (sum2, mid_in), (sum1,))
    from_mid = send(sum2, perm=MID)
    owned = adapters // 2
    keep_a, give_a = owner_grads(meta, low, 0, hidden, owned, (sum2,))
    keep_b, give_b = owner_grads(meta, low, 1, columns, owned, (keep_a,))
    own, give = final_sum(meta, (keep0, got0, from_pair, from_mid), (keep_b,))
    grad_b = add(keep_b, swap_cores(give_b))
    shape = keep_a.shape
    flat = (shape[0] * shape[1], shape[2])
    grad_a = add_after(
        meta, (keep_a.reshape(flat), swap_cores(give_a).reshape(flat)), (give,), steps=2
    )
    got = swap_cores(give)
    input_grad = jnp.where(
        d == 0, jnp.concatenate([own, got], axis=1), jnp.concatenate([got, own], axis=1)
    )
    grad_a = jnp.swapaxes(grad_a.reshape(shape), 1, 2)
    return (input_grad, grad_a, grad_b)


def body(
    cotangent,
    gate_activation_stored,
    up_activation_stored,
    gate_matrix,
    up_matrix,
    down_matrix,
    adapter_input_factor,
    adapter_output_factor,
    padded_block_segment,
    segment_adapter_index,
    adapter_grad_slot,
):
    local_token_rows = gate_activation_stored.shape[0]
    local_hidden_units = gate_activation_stored.shape[1]
    adapter_list = adapter_input_factor.shape[0]
    local_columns = adapter_output_factor.shape[2]
    seg_count = segment_adapter_index.shape[0]
    block_count = local_token_rows // BLOCK
    dp_index = lax.axis_index("dp")
    tensor_index = lax.axis_index("tensor")
    grad_all = lax.all_gather(cotangent, "tensor", axis=0, tiled=True)
    segments_here = lax.dynamic_slice_in_dim(
        padded_block_segment, dp_index * block_count, block_count
    )
    seg_onehot = (segments_here[:, None] == jnp.arange(seg_count, dtype=jnp.int32)[None, :]).astype(
        jnp.float32
    )
    adapter_onehot = (
        segment_adapter_index[:, 0][:, None] == jnp.arange(adapter_list, dtype=jnp.int32)[None, :]
    ).astype(jnp.float32)
    block_onehot = jnp.dot(seg_onehot, adapter_onehot)
    block_selector = block_onehot.astype(jnp.bfloat16)
    gate = gate_activation_stored.astype(jnp.float32)
    upper = up_activation_stored.astype(jnp.float32)
    sigmoid_gate = jax.nn.sigmoid(gate)
    silu_gate = gate * sigmoid_gate
    hidden_state = (silu_gate * upper).astype(jnp.bfloat16)
    hidden_blocks = hidden_state.reshape(block_count, BLOCK, local_hidden_units)
    cols_mine = lax.dynamic_slice_in_dim(grad_all, tensor_index * local_columns, local_columns, 1)
    cols_blocks = cols_mine.reshape(block_count, BLOCK, local_columns)
    a_blocks = jnp.einsum(
        "yz,zuo->yuo", block_selector, adapter_input_factor, preferred_element_type=jnp.float32
    ).astype(jnp.bfloat16)
    b_blocks = jnp.einsum(
        "vl,lyt->vyt", block_selector, adapter_output_factor, preferred_element_type=jnp.float32
    ).astype(jnp.bfloat16)
    part_in = jnp.einsum(
        "btf,bfr->btr", hidden_blocks, a_blocks, preferred_element_type=jnp.float32
    )
    part_out = jnp.einsum("btc,brc->btr", cols_blocks, b_blocks, preferred_element_type=jnp.float32)
    lowrank_input, lowrank_output = lax.psum((part_in, part_out), "tensor")
    lowrank_input = lowrank_input.astype(jnp.bfloat16)
    lowrank_output = lowrank_output.astype(jnp.bfloat16)
    gate_full, up_full, down_full = (
        lax.all_gather(gate_matrix, "dp", axis=0, tiled=True),
        lax.all_gather(up_matrix, "dp", axis=0, tiled=True),
        lax.all_gather(down_matrix, "dp", axis=0, tiled=True),
    )
    hidden_gradient = jnp.dot(grad_all, down_full, preferred_element_type=jnp.float32)
    additional_term = jnp.einsum(
        "btr,bfr->btf", lowrank_output, a_blocks, preferred_element_type=jnp.float32
    )
    hidden_gradient = hidden_gradient + ADAPTER_SCALE * additional_term.reshape(
        local_token_rows, local_hidden_units
    )
    gate_grad = (
        hidden_gradient * upper * sigmoid_gate * (1.0 + gate * (1.0 - sigmoid_gate))
    ).astype(jnp.bfloat16)
    up_grad = (hidden_gradient * silu_gate).astype(jnp.bfloat16)
    outer_product_input = jnp.einsum(
        "btf,btr->bfr", hidden_blocks, lowrank_output, preferred_element_type=jnp.float32
    )
    outer_product_output = jnp.einsum(
        "btr,btc->brc", lowrank_input, cols_blocks, preferred_element_type=jnp.float32
    )
    slot_onehot = (
        jnp.arange(adapter_list, dtype=jnp.int32)[:, None] == adapter_grad_slot[None, :]
    ).astype(jnp.float32)
    slot_block_mask = jnp.dot(slot_onehot, block_onehot.T)
    input_factor_terms = ADAPTER_SCALE * jnp.einsum(
        "pc,cdw->pdw", slot_block_mask, outer_product_input
    )
    output_factor_terms = ADAPTER_SCALE * jnp.einsum(
        "fn,nlv->flv", slot_block_mask, outer_product_output
    )
    owned_a, owned_b = (
        lax.psum_scatter(input_factor_terms, "dp", scatter_dimension=0, tiled=True),
        lax.psum_scatter(output_factor_terms, "dp", scatter_dimension=0, tiled=True),
    )
    grad_a = owned_a.astype(jnp.bfloat16)
    grad_b = owned_b.astype(jnp.bfloat16)
    first = lax.dot_general(
        gate_grad, gate_full, (((1,), (1,)), ((), ())), preferred_element_type=jnp.float32
    )
    second = lax.dot_general(
        up_grad, up_full, (((1,), (1,)), ((), ())), preferred_element_type=jnp.float32
    )
    summed = lax.psum_scatter(first + second, "tensor", scatter_dimension=0, tiled=True)
    input_grad = summed.astype(jnp.bfloat16)
    return (input_grad, grad_a, grad_b)


def solution(mesh):
    return jax.shard_map(
        grid_body if mesh.shape["tensor"] == 8 and mesh.shape["dp"] == 2 else body,
        mesh=mesh,
        in_specs=(
            P(("groups", "dp", "tensor"), None),
            P(("groups", "dp"), "tensor"),
            P(("groups", "dp"), "tensor"),
            P("dp", "tensor"),
            P("dp", "tensor"),
            P("dp", "tensor"),
            P(None, "tensor", None),
            P(None, None, "tensor"),
            P("groups"),
            P("groups", None),
            P(),
        ),
        out_specs=(
            P(("groups", "dp", "tensor"), None),
            P(("groups", "dp"), "tensor", None),
            P(("groups", "dp"), None, "tensor"),
        ),
        check_vma=False,
    )
```

```python
import functools

import jax
import jax.numpy as jnp
from jax import lax
from jax.experimental import pallas as pl
from jax.experimental.pallas import tpu as pltpu
from jax.sharding import PartitionSpec as P

BLOCK = 128


ADAPTER_SCALE = 2.0

F32 = jnp.float32
BF16 = jnp.bfloat16
MIB = 1024 * 1024

Y_SWAP = [(t, t ^ 1) for t in range(8)]
PAIR = [(t, t ^ 2) for t in range(8)]
FAR = [(t, t ^ 4) for t in range(8)]
MID = [(2, 4), (3, 5), (4, 2), (5, 3)]
OUTWARD = [(2, 0), (3, 1), (4, 6), (5, 7)]
INWARD = [(0, 2), (1, 3), (6, 4), (7, 5)]
CORES = [(0, 1), (1, 0)]

M_T, M_Y, M_D, M_Z, M_SLOT_ADAPTER, M_ADAPTER, M_GRAD_SLOT = 0, 1, 2, 3, 7, 11, 15


def nt_dot(a, b):
    return lax.dot_general(a, b, (((1,), (1,)), ((), ())), preferred_element_type=F32)


def tn_dot(a, b):
    return lax.dot_general(a, b, (((0,), (0,)), ((), ())), preferred_element_type=F32)


def call(
    kernel, meta, args, grid, in_specs, out_specs, out_shape, scratch=(), vmem=26, after=(), cost=(1000, 1000)
):
    first, extra = len(args), len(after)

    def run(m, *refs):
        kernel(m, *refs[:first], *refs[first + extra :])

    return pl.pallas_call(
        run,
        grid_spec=pltpu.PrefetchScalarGridSpec(
            num_scalar_prefetch=1,
            grid=grid,
            in_specs=list(in_specs) + [pl.BlockSpec(memory_space=pl.ANY)] * extra,
            out_specs=out_specs,
            scratch_shapes=list(scratch),
        ),
        out_shape=out_shape,
        compiler_params=pltpu.CompilerParams(vmem_limit_bytes=vmem * MIB),
        cost_estimate=pl.CostEstimate(flops=cost[0], bytes_accessed=cost[1], transcendentals=0),
    )(meta, *args, *after)


def pack_halves(p):
    h = p.shape[0] // 2
    return jnp.concatenate([p[:h], p[h:]], axis=1)


def unpack_halves(p):
    h = p.shape[1] // 2
    return jnp.concatenate([p[:, :h], p[:, h:]], axis=0)


def hidden_kernel(m, gate_ref, up_ref, a_ref, hidden_ref, low_ref):
    g = gate_ref[...].astype(F32)
    hidden = (g * jax.nn.sigmoid(g) * up_ref[...].astype(F32)).astype(BF16)
    hidden_ref[...] = hidden
    low_ref[...] = pack_halves(nt_dot(hidden, a_ref[0]))


def hidden_and_low_in(meta, gate_act, up_act, a_t):
    rows, width = gate_act.shape
    rank = a_t.shape[1]
    blocks = rows // BLOCK
    return call(
        hidden_kernel,
        meta,
        (gate_act, up_act, a_t),
        (blocks,),
        [
            pl.BlockSpec((BLOCK, width), lambda b, m: (b, 0)),
            pl.BlockSpec((BLOCK, width), lambda b, m: (b, 0)),
            pl.BlockSpec((1, rank, width), lambda b, m: (m[M_ADAPTER + b], 0, 0)),
        ],
        [
            pl.BlockSpec((BLOCK, width), lambda b, m: (b, 0)),
            pl.BlockSpec((BLOCK // 2, 2 * rank), lambda b, m: (b, 0)),
        ],
        [
            jax.ShapeDtypeStruct((rows, width), BF16),
            jax.ShapeDtypeStruct((rows // 2, 2 * rank), F32),
        ],
    )


def low_out_kernel(m, *refs):
    shards, b_ref, low_in_ref = refs[:8], refs[8], refs[9]
    cols_ref, full_ref, short_ref = refs[10:]
    rows = shards[0].shape[0]
    y = m[M_Y]
    for s in range(4):
        z = m[M_Z + s]
        own, other = shards[2 * s][...], shards[2 * s + 1][...]
        first = jnp.where(y == 0, own, other)
        second = jnp.where(y == 0, other, own)
        tokens = jnp.concatenate([first, second], axis=0)
        cols_ref[pl.ds(pl.multiple_of(z * 2 * rows, 2 * rows), 2 * rows), :] = tokens
        part = pack_halves(nt_dot(tokens, b_ref[m[M_SLOT_ADAPTER + s]]))
        at = pl.ds(pl.multiple_of(z * rows, rows), rows)
        full_ref[at, :] = part
        short_ref[at, :] = part.astype(BF16)
    full_ref[4 * rows :] = low_in_ref[...]
    short_ref[4 * rows :] = low_in_ref[...].astype(BF16)


def low_parts(meta, shards, b, low_in, after):
    rows = shards[0].shape[0]
    adapters, rank, columns = b.shape
    out = (8 * rows, 2 * rank)
    return call(
        low_out_kernel,
        meta,
        (*shards, b, low_in),
        (1,),
        [pl.BlockSpec((rows, columns), lambda i, m: (0, m[M_T]))] * 8
        + [pl.BlockSpec((adapters, rank, columns), lambda i, m: (0, 0, 0))]
        + [pl.BlockSpec((4 * rows, 2 * rank), lambda i, m: (0, 0))],
        [pl.BlockSpec((8 * rows, columns), lambda i, m: (0, 0))]
        + [pl.BlockSpec(out, lambda i, m: (0, 0))] * 2,
        [
            jax.ShapeDtypeStruct((8 * rows, columns), BF16),
            jax.ShapeDtypeStruct(out, F32),
            jax.ShapeDtypeStruct(out, BF16),
        ],
        after=after,
    )


def hidden_grad_kernel(count, m, *refs):
    mine, other = refs[:count], refs[count : 2 * count]
    down_mine, down_other, out_ref, lhs = refs[2 * count :]
    rows = mine[0].shape[0]

    @pl.when(pl.program_id(0) == 0)
    def _():
        for s in range(count):
            lhs[0, s * rows : (s + 1) * rows] = mine[s][...]
            lhs[1, s * rows : (s + 1) * rows] = other[s][...]

    total = jnp.dot(lhs[0], down_mine[...], preferred_element_type=F32)
    out_ref[...] = total + jnp.dot(lhs[1], down_other[...], preferred_element_type=F32)


def hidden_grad(meta, shards, mine, other, span, after=()):
    rows = shards[0].shape[0]
    half = mine.shape[0]
    start, width, step = span
    count = len(shards)
    total = rows * count
    return call(
        functools.partial(hidden_grad_kernel, count),
        meta,
        (*shards, *shards, mine, other),
        (width // step,),
        [pl.BlockSpec((rows, half), lambda n, m: (0, m[M_D]))] * count
        + [pl.BlockSpec((rows, half), lambda n, m: (0, 1 - m[M_D]))] * count
        + [pl.BlockSpec((half, step), lambda n, m: (0, n + start // step))] * 2,
        pl.BlockSpec((total, step), lambda n, m: (0, n)),
        jax.ShapeDtypeStruct((total, width), F32),
        scratch=[pltpu.VMEM((2, total, half), BF16)],
        after=after,
    )


def act_grad_kernel(spans, m, *refs):
    hg_refs, (gate_ref, up_ref, low_ref, a_ref, out_ref) = refs[: len(spans)], refs[len(spans) :]
    j = pl.program_id(0)
    y = m[M_Y]
    rank = low_ref.shape[1] // 2
    second = jnp.where(j == 0, y, 1 - y) == 1
    low = jnp.where(second, low_ref[:, rank:], low_ref[:, :rank])
    for hg_ref, (start, width, _) in zip(hg_refs, spans):
        at = slice(start, start + width)
        hg = hg_ref[...] + ADAPTER_SCALE * jnp.dot(low, a_ref[0, :, at], preferred_element_type=F32)
        g = gate_ref[:, at].astype(F32)
        u = up_ref[:, at].astype(F32)
        sig = jax.nn.sigmoid(g)
        out_ref[0, :, at] = (hg * u * sig * (1.0 + g * (1.0 - sig))).astype(BF16)
        out_ref[1, :, at] = (hg * (g * sig)).astype(BF16)


def act_grad(meta, slot, spans, hgs, gate_act, up_act, low, a_t, after=()):
    rank, width = a_t.shape[1:]
    rows = BLOCK // 2

    def shard_of(j, m):
        y = m[M_Y]
        return (m[M_Z + slot] * 2 + y + j * (1 - 2 * y), 0)

    return call(
        functools.partial(act_grad_kernel, spans),
        meta,
        (*hgs, gate_act, up_act, low, a_t),
        (2,),
        [pl.BlockSpec((rows, w), lambda j, m: ((slot % 2) * 2 + j, 0)) for _, w, _ in spans]
        + [
            pl.BlockSpec((rows, width), shard_of),
            pl.BlockSpec((rows, width), shard_of),
            pl.BlockSpec((rows, 2 * rank), lambda j, m: (m[M_Z + slot], 0)),
            pl.BlockSpec((1, rank, width), lambda j, m: (m[M_SLOT_ADAPTER + slot], 0, 0)),
        ],
        pl.BlockSpec((2, rows, width), lambda j, m: (0, j, 0)),
        jax.ShapeDtypeStruct((2, 2 * rows, width), BF16),
        after=after,
    )


def input_grad_kernel(count, m, *refs):
    mine, other = refs[:count], refs[count : 2 * count]
    gate_ref, up_ref = refs[2 * count : 2 * count + 2]
    outs, lhs = refs[2 * count + 2 : -1], refs[-1]
    rows = mine[0].shape[1] // 2

    @pl.when(pl.program_id(0) == 0)
    def _():
        for s in range(count):
            for i in range(2):
                for y in range(2):
                    for k, ref in enumerate((mine[s], other[s])):
                        to = (4 * s + 2 * y + k) * rows
                        lhs[i, to : to + rows] = ref[i, y * rows : (y + 1) * rows]

    total = nt_dot(lhs[0], gate_ref[...]) + nt_dot(lhs[1], up_ref[...])
    for k, ref in enumerate(outs):
        ref[...] = total[2 * k * rows : 2 * (k + 1) * rows].astype(BF16)


def input_grad_parts(meta, mine, other, gate, up, after=()):
    count = len(mine)
    rows, width = mine[0].shape[1:]
    half = gate.shape[0]
    step = 512 // count
    one = pl.Buffered(1) if count > 1 else None
    out = jax.ShapeDtypeStruct((rows, half), BF16)
    return call(
        functools.partial(input_grad_kernel, count),
        meta,
        (*mine, *other, gate, up),
        (half // step,),
        [pl.BlockSpec((2, rows, width), lambda n, m: (0, 0, 0), pipeline_mode=one)] * (2 * count)
        + [pl.BlockSpec((step, width), lambda n, m: (n, 0))] * 2,
        [pl.BlockSpec((rows, step), lambda n, m: (0, n))] * (2 * count),
        [out] * (2 * count),
        scratch=[pltpu.VMEM((2, 2 * count * rows, width), BF16)],
        after=after,
    )


def owner_kernel(m, low_ref, features_ref, keep_ref, send_ref, lhs):
    owned, rank = keep_ref.shape[:2]
    blocks = features_ref.shape[0] // BLOCK
    rows = low_ref.shape[0] // blocks
    d = m[M_D]

    @pl.when(pl.program_id(0) == 0)
    def _():
        for b in range(blocks):
            low = unpack_halves(low_ref[b * rows : (b + 1) * rows, :])
            masked = []
            for owner in (d, 1 - d):
                for i in range(owned):
                    hit = m[M_GRAD_SLOT + b] == owner * owned + i
                    masked.append(jnp.where(hit, low, jnp.zeros_like(low)))
            lhs[b * BLOCK : (b + 1) * BLOCK] = jnp.concatenate(masked, axis=1)

    total = (ADAPTER_SCALE * tn_dot(lhs[...], features_ref[...])).astype(BF16)
    for i in range(owned):
        keep_ref[i] = total[i * rank : (i + 1) * rank]
        send_ref[i] = total[(owned + i) * rank : (owned + i + 1) * rank]


def owner_grads(meta, low, which, features, owned, after=()):
    tokens, width = features.shape
    half_rows, double = low.shape[0] // 2, low.shape[1]
    rank = double // 2
    step = 640
    out = jax.ShapeDtypeStruct((owned, rank, width), BF16)
    return call(
        owner_kernel,
        meta,
        (low, features),
        (width // step,),
        [
            pl.BlockSpec((half_rows, double), lambda n, m: (which, 0)),
            pl.BlockSpec((tokens, step), lambda n, m: (0, n)),
        ],
        [pl.BlockSpec((owned, rank, step), lambda n, m: (0, 0, n))] * 2,
        [out, out],
        scratch=[pltpu.VMEM((tokens, 2 * owned * rank), BF16)],
        after=after,
    )


def add_kernel(count, m, *refs):
    total = refs[0][...].astype(F32)
    for r in refs[1:count]:
        total += r[...].astype(F32)
    for r in refs[count:]:
        r[...] = total.astype(r.dtype)


def add_after(meta, xs, after, kinds=(BF16,), steps=1):
    rows, width = xs[0].shape
    spec = pl.BlockSpec((rows // steps, width), lambda i, m: (i, 0))
    out = call(
        functools.partial(add_kernel, len(xs)),
        meta,
        xs,
        (steps,),
        [spec] * len(xs),
        [spec] * len(kinds),
        [jax.ShapeDtypeStruct((rows, width), k) for k in kinds],
        vmem=16,
        after=after,
    )
    return out if len(kinds) > 1 else out[0]


def final_kernel(m, *refs):
    total = refs[0][...].astype(F32)
    for r in refs[1:-2]:
        total += r[...].astype(F32)
    rows = refs[-1].shape[0]
    refs[-2][...] = total[:rows].astype(BF16)
    refs[-1][...] = total[rows:].astype(BF16)


def final_sum(meta, xs, after):
    rows, width = xs[0].shape
    return call(
        final_kernel,
        meta,
        xs,
        (1,),
        [pl.BlockSpec((rows, width), lambda i, m: (0, 0))] * len(xs),
        [pl.BlockSpec((rows // 2, width), lambda i, m: (0, 0))] * 2,
        [jax.ShapeDtypeStruct((rows // 2, width), BF16)] * 2,
        vmem=16,
        after=after,
    )


def add(*xs):
    return functools.reduce(jnp.add, [x.astype(F32) for x in xs]).astype(BF16)


def tied(x, *others):
    return lax.optimization_barrier((x, *others))[0]


def grid_body(
    cotangent,
    gate_act,
    up_act,
    gate_matrix,
    up_matrix,
    down_matrix,
    adapter_input_factor,
    adapter_output_factor,
    padded_block_segment,
    segment_adapter_index,
    adapter_grad_slot,
):
    adapters = adapter_input_factor.shape[0]
    blocks = gate_act.shape[0] // BLOCK
    d = lax.axis_index("dp")
    t = lax.axis_index("tensor")
    z, y = t // 2, t % 2
    low_side = z < 2
    slots_z = jnp.stack([z, z ^ 1, jnp.where(low_side, 2, 1), jnp.where(low_side, 3, 0)])
    segments_here = lax.dynamic_slice_in_dim(padded_block_segment, d * blocks, blocks)

    def pick(table, index):
        hit = index[:, None] == jnp.arange(table.shape[0], dtype=jnp.int32)[None, :]
        return jnp.sum(jnp.where(hit, table[None, :], 0), axis=1)

    block_adapter = pick(segment_adapter_index[:, 0], segments_here)
    meta = jnp.concatenate(
        [
            jnp.stack([t, y, d]),
            slots_z,
            pick(block_adapter, slots_z),
            block_adapter,
            pick(adapter_grad_slot, block_adapter),
        ]
    ).astype(jnp.int32)
    a_t = jnp.swapaxes(adapter_input_factor, 1, 2)
    send = functools.partial(lax.ppermute, axis_name="tensor")
    swap_cores = functools.partial(lax.ppermute, axis_name="dp", perm=CORES)
    at_end = (z == 0) | (z == 3)

    width = gate_act.shape[1]
    step = width * 2 // 5
    spans = ((0, step, step // 2), (step, step, step // 2), (2 * step, width - 2 * step, width - 2 * step))

    down_other = swap_cores(down_matrix)
    pair = send(cotangent, perm=PAIR)
    mid = send(cotangent, perm=MID)
    y0 = send(cotangent, perm=Y_SWAP)
    hidden, low_in = hidden_and_low_in(meta, gate_act, up_act, a_t)
    y1 = send(tied(pair, y0, low_in), perm=Y_SWAP)
    pair_mid = send(tied(pair, low_in), perm=MID)
    mid_out = send(tied(mid, low_in), perm=OUTWARD)
    slot2 = jnp.where(at_end, mid_out, mid)
    y2 = send(tied(slot2, y1), perm=Y_SWAP)
    far_out = send(pair_mid, perm=OUTWARD)
    hg_near, last = [], (low_in,)
    for span in spans:
        hg_near.append(hidden_grad(meta, (cotangent, y0, pair, y1), down_matrix, down_other, span, last))
        last = (hg_near[-1],)
    slot3 = jnp.where(at_end, tied(far_out, hg_near[0]), pair_mid)
    y3 = send(tied(slot3, y2), perm=Y_SWAP)

    far = (slot2, y2, slot3, y3)
    near = (cotangent, y0, pair, y1)
    columns, low_sum, low = low_parts(meta, near + far, adapter_output_factor, low_in, last)
    hg_far = []
    for perm, span in zip((Y_SWAP, PAIR, FAR), spans):
        got = send(low, perm=perm)
        hg_far.append(hidden_grad(meta, far, down_matrix, down_other, span, (low,)))
        low_sum, low = add_after(meta, (low_sum, got), (hg_far[-1],), (F32, BF16))

    def grads(slot, after):
        hgs = hg_far if slot >= 2 else hg_near
        return act_grad(meta, slot, spans, hgs, gate_act, up_act, low, a_t, after)

    def parts(mine, other, after):
        return input_grad_parts(meta, mine, other, gate_matrix, up_matrix, after)

    mine3 = grads(3, ())
    other3 = swap_cores(mine3)
    mine2 = grads(2, (mine3,))
    other2 = swap_cores(tied(mine2, other3))
    mine1 = grads(1, (mine2,))
    other1 = swap_cores(tied(mine1, other2))
    keep3, give3 = parts((mine3,), (other3,), (mine1,))
    got3 = send(give3, perm=Y_SWAP)
    keep2, give2, keep1, give1 = parts((mine2, mine1), (other2, other1), (give3,))
    got2 = send(give2, perm=Y_SWAP)
    sum3 = add_after(meta, (keep3, got3), (give2,))
    far_in = send(sum3, perm=INWARD)
    mine0 = grads(0, (sum3,))
    other0 = swap_cores(mine0)
    owned = adapters // 2
    keep_a, give_a = owner_grads(meta, low, 0, hidden, owned, (mine0,))
    keep_b, give_b = owner_grads(meta, low, 1, columns, owned, (keep_a,))
    got_a, got_b = swap_cores(give_a), swap_cores(give_b)
    sum2 = add_after(meta, (keep2, got2), (keep_b,))
    mid_in = send(sum2, perm=INWARD)
    sum3 = add_after(meta, (sum3, far_in), (sum2,))
    far_mid = send(sum3, perm=MID)
    got1 = send(give1, perm=Y_SWAP)
    keep0, give0 = parts((mine0,), (other0,), (sum3, got_a, got_b))
    got0 = send(give0, perm=Y_SWAP)
    sum1 = add_after(meta, (keep1, got1, far_mid), (give0,))
    from_pair = send(sum1, perm=PAIR)
    sum2 = add_after(meta, (sum2, mid_in), (sum1,))
    from_mid = send(sum2, perm=MID)

    def owner_sum(keep, got):
        flat = (keep.shape[0] * keep.shape[1], keep.shape[2])
        out = add_after(meta, (keep.reshape(flat), got.reshape(flat)), (sum2,), steps=2)
        return out.reshape(keep.shape)

    grad_a, grad_b = owner_sum(keep_a, got_a), owner_sum(keep_b, got_b)
    own, give = final_sum(meta, (keep0, got0, from_pair, from_mid), (grad_a, grad_b))
    got = swap_cores(give)
    input_grad = jnp.where(
        d == 0, jnp.concatenate([own, got], axis=1), jnp.concatenate([got, own], axis=1)
    )
    grad_a = jnp.swapaxes(grad_a, 1, 2)
    return (input_grad, grad_a, grad_b)


def body(
    cotangent,
    gate_activation_stored,
    up_activation_stored,
    gate_matrix,
    up_matrix,
    down_matrix,
    adapter_input_factor,
    adapter_output_factor,
    padded_block_segment,
    segment_adapter_index,
    adapter_grad_slot,
):
    local_token_rows = gate_activation_stored.shape[0]
    local_hidden_units = gate_activation_stored.shape[1]
    adapter_list = adapter_input_factor.shape[0]
    local_columns = adapter_output_factor.shape[2]
    seg_count = segment_adapter_index.shape[0]
    block_count = local_token_rows // BLOCK
    dp_index = lax.axis_index("dp")
    tensor_index = lax.axis_index("tensor")
    grad_all = lax.all_gather(cotangent, "tensor", axis=0, tiled=True)
    segments_here = lax.dynamic_slice_in_dim(
        padded_block_segment, dp_index * block_count, block_count
    )
    seg_onehot = (segments_here[:, None] == jnp.arange(seg_count, dtype=jnp.int32)[None, :]).astype(
        jnp.float32
    )
    adapter_onehot = (
        segment_adapter_index[:, 0][:, None] == jnp.arange(adapter_list, dtype=jnp.int32)[None, :]
    ).astype(jnp.float32)
    block_onehot = jnp.dot(seg_onehot, adapter_onehot)
    block_selector = block_onehot.astype(jnp.bfloat16)
    gate = gate_activation_stored.astype(jnp.float32)
    upper = up_activation_stored.astype(jnp.float32)
    sigmoid_gate = jax.nn.sigmoid(gate)
    silu_gate = gate * sigmoid_gate
    hidden_state = (silu_gate * upper).astype(jnp.bfloat16)
    hidden_blocks = hidden_state.reshape(block_count, BLOCK, local_hidden_units)
    cols_mine = lax.dynamic_slice_in_dim(grad_all, tensor_index * local_columns, local_columns, 1)
    cols_blocks = cols_mine.reshape(block_count, BLOCK, local_columns)
    a_blocks = jnp.einsum(
        "yz,zuo->yuo", block_selector, adapter_input_factor, preferred_element_type=jnp.float32
    ).astype(jnp.bfloat16)
    b_blocks = jnp.einsum(
        "vl,lyt->vyt", block_selector, adapter_output_factor, preferred_element_type=jnp.float32
    ).astype(jnp.bfloat16)
    part_in = jnp.einsum(
        "btf,bfr->btr", hidden_blocks, a_blocks, preferred_element_type=jnp.float32
    )
    part_out = jnp.einsum("btc,brc->btr", cols_blocks, b_blocks, preferred_element_type=jnp.float32)
    lowrank_input, lowrank_output = lax.psum((part_in, part_out), "tensor")
    lowrank_input = lowrank_input.astype(jnp.bfloat16)
    lowrank_output = lowrank_output.astype(jnp.bfloat16)
    gate_full, up_full, down_full = (
        lax.all_gather(gate_matrix, "dp", axis=0, tiled=True),
        lax.all_gather(up_matrix, "dp", axis=0, tiled=True),
        lax.all_gather(down_matrix, "dp", axis=0, tiled=True),
    )
    hidden_gradient = jnp.dot(grad_all, down_full, preferred_element_type=jnp.float32)
    additional_term = jnp.einsum(
        "btr,bfr->btf", lowrank_output, a_blocks, preferred_element_type=jnp.float32
    )
    hidden_gradient = hidden_gradient + ADAPTER_SCALE * additional_term.reshape(
        local_token_rows, local_hidden_units
    )
    gate_grad = (
        hidden_gradient * upper * sigmoid_gate * (1.0 + gate * (1.0 - sigmoid_gate))
    ).astype(jnp.bfloat16)
    up_grad = (hidden_gradient * silu_gate).astype(jnp.bfloat16)
    outer_product_input = jnp.einsum(
        "btf,btr->bfr", hidden_blocks, lowrank_output, preferred_element_type=jnp.float32
    )
    outer_product_output = jnp.einsum(
        "btr,btc->brc", lowrank_input, cols_blocks, preferred_element_type=jnp.float32
    )
    slot_onehot = (
        jnp.arange(adapter_list, dtype=jnp.int32)[:, None] == adapter_grad_slot[None, :]
    ).astype(jnp.float32)
    slot_block_mask = jnp.dot(slot_onehot, block_onehot.T)
    input_factor_terms = ADAPTER_SCALE * jnp.einsum(
        "pc,cdw->pdw", slot_block_mask, outer_product_input
    )
    output_factor_terms = ADAPTER_SCALE * jnp.einsum(
        "fn,nlv->flv", slot_block_mask, outer_product_output
    )
    owned_a, owned_b = (
        lax.psum_scatter(input_factor_terms, "dp", scatter_dimension=0, tiled=True),
        lax.psum_scatter(output_factor_terms, "dp", scatter_dimension=0, tiled=True),
    )
    grad_a = owned_a.astype(jnp.bfloat16)
    grad_b = owned_b.astype(jnp.bfloat16)
    first = lax.dot_general(
        gate_grad, gate_full, (((1,), (1,)), ((), ())), preferred_element_type=jnp.float32
    )
    second = lax.dot_general(
        up_grad, up_full, (((1,), (1,)), ((), ())), preferred_element_type=jnp.float32
    )
    summed = lax.psum_scatter(first + second, "tensor", scatter_dimension=0, tiled=True)
    input_grad = summed.astype(jnp.bfloat16)
    return (input_grad, grad_a, grad_b)


def solution(mesh):
    return jax.shard_map(
        grid_body if mesh.shape["tensor"] == 8 and mesh.shape["dp"] == 2 else body,
        mesh=mesh,
        in_specs=(
            P(("groups", "dp", "tensor"), None),
            P(("groups", "dp"), "tensor"),
            P(("groups", "dp"), "tensor"),
            P("dp", "tensor"),
            P("dp", "tensor"),
            P("dp", "tensor"),
            P(None, "tensor", None),
            P(None, None, "tensor"),
            P("groups"),
            P("groups", None),
            P(),
        ),
        out_specs=(
            P(("groups", "dp", "tensor"), None),
            P(("groups", "dp"), "tensor", None),
            P(("groups", "dp"), None, "tensor"),
        ),
        check_vma=False,
    )
```

```python
import functools

import jax
import jax.numpy as jnp
from jax import lax
from jax.experimental import pallas as pl
from jax.experimental.pallas import tpu as pltpu
from jax.sharding import PartitionSpec as P

BLOCK = 128


ADAPTER_SCALE = 2.0

F32 = jnp.float32
BF16 = jnp.bfloat16
MIB = 1024 * 1024

Y_SWAP = [(t, t ^ 1) for t in range(8)]
PAIR = [(t, t ^ 2) for t in range(8)]
FAR = [(t, t ^ 4) for t in range(8)]
MID = [(2, 4), (3, 5), (4, 2), (5, 3)]
OUTWARD = [(2, 0), (3, 1), (4, 6), (5, 7)]
INWARD = [(0, 2), (1, 3), (6, 4), (7, 5)]
CORES = [(0, 1), (1, 0)]

M_T, M_Y, M_D, M_Z, M_SLOT_ADAPTER, M_ADAPTER, M_GRAD_SLOT = 0, 1, 2, 3, 7, 11, 15


def nt_dot(a, b):
    return lax.dot_general(a, b, (((1,), (1,)), ((), ())), preferred_element_type=F32)


def tn_dot(a, b):
    return lax.dot_general(a, b, (((0,), (0,)), ((), ())), preferred_element_type=F32)


def call(
    kernel, meta, args, grid, in_specs, out_specs, out_shape, scratch=(), vmem=24, after=(), cost=(1000, 1000)
):
    first, extra = len(args), len(after)

    def run(m, *refs):
        kernel(m, *refs[:first], *refs[first + extra :])

    return pl.pallas_call(
        run,
        grid_spec=pltpu.PrefetchScalarGridSpec(
            num_scalar_prefetch=1,
            grid=grid,
            in_specs=list(in_specs) + [pl.BlockSpec(memory_space=pl.ANY)] * extra,
            out_specs=out_specs,
            scratch_shapes=list(scratch),
        ),
        out_shape=out_shape,
        compiler_params=pltpu.CompilerParams(vmem_limit_bytes=vmem * MIB),
        cost_estimate=pl.CostEstimate(flops=cost[0], bytes_accessed=cost[1], transcendentals=0),
    )(meta, *args, *after)


def pack_halves(p):
    h = p.shape[0] // 2
    return jnp.concatenate([p[:h], p[h:]], axis=1)


def unpack_halves(p):
    h = p.shape[1] // 2
    return jnp.concatenate([p[:, :h], p[:, h:]], axis=0)


def hidden_kernel(m, gate_ref, up_ref, a_ref, hidden_ref, low_ref):
    g = gate_ref[...].astype(F32)
    hidden = (g * jax.nn.sigmoid(g) * up_ref[...].astype(F32)).astype(BF16)
    hidden_ref[...] = hidden
    low_ref[...] = pack_halves(nt_dot(hidden, a_ref[0]))


def hidden_and_low_in(meta, gate_act, up_act, a_t):
    rows, width = gate_act.shape
    rank = a_t.shape[1]
    blocks = rows // BLOCK
    return call(
        hidden_kernel,
        meta,
        (gate_act, up_act, a_t),
        (blocks,),
        [
            pl.BlockSpec((BLOCK, width), lambda b, m: (b, 0)),
            pl.BlockSpec((BLOCK, width), lambda b, m: (b, 0)),
            pl.BlockSpec((1, rank, width), lambda b, m: (m[M_ADAPTER + b], 0, 0)),
        ],
        [
            pl.BlockSpec((BLOCK, width), lambda b, m: (b, 0)),
            pl.BlockSpec((BLOCK // 2, 2 * rank), lambda b, m: (b, 0)),
        ],
        [
            jax.ShapeDtypeStruct((rows, width), BF16),
            jax.ShapeDtypeStruct((rows // 2, 2 * rank), F32),
        ],
    )


def low_out_kernel(m, *refs):
    shards, b_ref, low_in_ref = refs[:8], refs[8], refs[9]
    cols_ref, full_ref, short_ref = refs[10:]
    rows = shards[0].shape[0]
    y = m[M_Y]
    for s in range(4):
        z = m[M_Z + s]
        own, other = shards[2 * s][...], shards[2 * s + 1][...]
        first = jnp.where(y == 0, own, other)
        second = jnp.where(y == 0, other, own)
        tokens = jnp.concatenate([first, second], axis=0)
        cols_ref[pl.ds(pl.multiple_of(z * 2 * rows, 2 * rows), 2 * rows), :] = tokens
        part = pack_halves(nt_dot(tokens, b_ref[m[M_SLOT_ADAPTER + s]]))
        at = pl.ds(pl.multiple_of(z * rows, rows), rows)
        full_ref[at, :] = part
        short_ref[at, :] = part.astype(BF16)
    full_ref[4 * rows :] = low_in_ref[...]
    short_ref[4 * rows :] = low_in_ref[...].astype(BF16)


def low_parts(meta, shards, b, low_in, after):
    rows = shards[0].shape[0]
    adapters, rank, columns = b.shape
    out = (8 * rows, 2 * rank)
    return call(
        low_out_kernel,
        meta,
        (*shards, b, low_in),
        (1,),
        [pl.BlockSpec((rows, columns), lambda i, m: (0, m[M_T]))] * 8
        + [pl.BlockSpec((adapters, rank, columns), lambda i, m: (0, 0, 0))]
        + [pl.BlockSpec((4 * rows, 2 * rank), lambda i, m: (0, 0))],
        [pl.BlockSpec((8 * rows, columns), lambda i, m: (0, 0))]
        + [pl.BlockSpec(out, lambda i, m: (0, 0))] * 2,
        [
            jax.ShapeDtypeStruct((8 * rows, columns), BF16),
            jax.ShapeDtypeStruct(out, F32),
            jax.ShapeDtypeStruct(out, BF16),
        ],
        after=after,
    )


def hidden_grad_kernel(count, m, *refs):
    mine, other = refs[:count], refs[count : 2 * count]
    down_mine, down_other, out_ref, lhs = refs[2 * count :]
    rows = mine[0].shape[0]

    @pl.when(pl.program_id(0) == 0)
    def _():
        for s in range(count):
            lhs[0, s * rows : (s + 1) * rows] = mine[s][...]
            lhs[1, s * rows : (s + 1) * rows] = other[s][...]

    total = jnp.dot(lhs[0], down_mine[...], preferred_element_type=F32)
    out_ref[...] = total + jnp.dot(lhs[1], down_other[...], preferred_element_type=F32)


def hidden_grad(meta, shards, mine, other, span, after=()):
    rows = shards[0].shape[0]
    half = mine.shape[0]
    start, width, step = span
    count = len(shards)
    total = rows * count
    return call(
        functools.partial(hidden_grad_kernel, count),
        meta,
        (*shards, *shards, mine, other),
        (width // step,),
        [pl.BlockSpec((rows, half), lambda n, m: (0, m[M_D]))] * count
        + [pl.BlockSpec((rows, half), lambda n, m: (0, 1 - m[M_D]))] * count
        + [pl.BlockSpec((half, step), lambda n, m: (0, n + start // step))] * 2,
        pl.BlockSpec((total, step), lambda n, m: (0, n)),
        jax.ShapeDtypeStruct((total, width), F32),
        scratch=[pltpu.VMEM((2, total, half), BF16)],
        after=after,
    )


def act_grad_kernel(spans, m, *refs):
    hg_refs, (gate_ref, up_ref, low_ref, a_ref, out_ref) = refs[: len(spans)], refs[len(spans) :]
    j = pl.program_id(0)
    y = m[M_Y]
    rank = low_ref.shape[1] // 2
    second = jnp.where(j == 0, y, 1 - y) == 1
    low = jnp.where(second, low_ref[:, rank:], low_ref[:, :rank])
    for hg_ref, (start, width, _) in zip(hg_refs, spans):
        at = slice(start, start + width)
        hg = hg_ref[...] + ADAPTER_SCALE * jnp.dot(low, a_ref[0, :, at], preferred_element_type=F32)
        g = gate_ref[:, at].astype(F32)
        u = up_ref[:, at].astype(F32)
        sig = jax.nn.sigmoid(g)
        out_ref[0, :, at] = (hg * u * sig * (1.0 + g * (1.0 - sig))).astype(BF16)
        out_ref[1, :, at] = (hg * (g * sig)).astype(BF16)


def act_grad(meta, slot, spans, hgs, gate_act, up_act, low, a_t, after=()):
    rank, width = a_t.shape[1:]
    rows = BLOCK // 2

    def shard_of(j, m):
        y = m[M_Y]
        return (m[M_Z + slot] * 2 + y + j * (1 - 2 * y), 0)

    return call(
        functools.partial(act_grad_kernel, spans),
        meta,
        (*hgs, gate_act, up_act, low, a_t),
        (2,),
        [pl.BlockSpec((rows, w), lambda j, m: ((slot % 2) * 2 + j, 0)) for _, w, _ in spans]
        + [
            pl.BlockSpec((rows, width), shard_of),
            pl.BlockSpec((rows, width), shard_of),
            pl.BlockSpec((rows, 2 * rank), lambda j, m: (m[M_Z + slot], 0)),
            pl.BlockSpec((1, rank, width), lambda j, m: (m[M_SLOT_ADAPTER + slot], 0, 0)),
        ],
        pl.BlockSpec((2, rows, width), lambda j, m: (0, j, 0)),
        jax.ShapeDtypeStruct((2, 2 * rows, width), BF16),
        after=after,
    )


def input_grad_kernel(m, mine_ref, other_ref, gate_ref, up_ref, keep_ref, send_ref, lhs):
    rows = mine_ref.shape[1] // 2

    @pl.when(pl.program_id(0) == 0)
    def _():
        for i in range(2):
            for y in range(2):
                lhs[i, (2 * y) * rows : (2 * y + 1) * rows] = mine_ref[i, y * rows : (y + 1) * rows]
                lhs[i, (2 * y + 1) * rows : (2 * y + 2) * rows] = other_ref[i, y * rows : (y + 1) * rows]

    total = nt_dot(lhs[0], gate_ref[...]) + nt_dot(lhs[1], up_ref[...])
    keep_ref[...] = total[: 2 * rows].astype(BF16)
    send_ref[...] = total[2 * rows :].astype(BF16)


def input_grad_parts(meta, mine, other, gate, up, after=()):
    rows, width = mine.shape[1:]
    half = gate.shape[0]
    step = 512
    out = jax.ShapeDtypeStruct((rows, half), BF16)
    return call(
        input_grad_kernel,
        meta,
        (mine, other, gate, up),
        (half // step,),
        [pl.BlockSpec((2, rows, width), lambda n, m: (0, 0, 0))] * 2
        + [pl.BlockSpec((step, width), lambda n, m: (n, 0))] * 2,
        [pl.BlockSpec((rows, step), lambda n, m: (0, n))] * 2,
        [out, out],
        scratch=[pltpu.VMEM((2, 2 * rows, width), BF16)],
        after=after,
    )


def owner_kernel(m, low_ref, features_ref, keep_ref, send_ref, lhs):
    owned, rank = keep_ref.shape[:2]
    blocks = features_ref.shape[0] // BLOCK
    rows = low_ref.shape[0] // blocks
    d = m[M_D]

    @pl.when(pl.program_id(0) == 0)
    def _():
        for b in range(blocks):
            low = unpack_halves(low_ref[b * rows : (b + 1) * rows, :])
            masked = []
            for owner in (d, 1 - d):
                for i in range(owned):
                    hit = m[M_GRAD_SLOT + b] == owner * owned + i
                    masked.append(jnp.where(hit, low, jnp.zeros_like(low)))
            lhs[b * BLOCK : (b + 1) * BLOCK] = jnp.concatenate(masked, axis=1)

    total = (ADAPTER_SCALE * tn_dot(lhs[...], features_ref[...])).astype(BF16)
    for i in range(owned):
        keep_ref[i] = total[i * rank : (i + 1) * rank]
        send_ref[i] = total[(owned + i) * rank : (owned + i + 1) * rank]


def owner_grads(meta, low, which, features, owned, after=()):
    tokens, width = features.shape
    half_rows, double = low.shape[0] // 2, low.shape[1]
    rank = double // 2
    step = 640
    out = jax.ShapeDtypeStruct((owned, rank, width), BF16)
    return call(
        owner_kernel,
        meta,
        (low, features),
        (width // step,),
        [
            pl.BlockSpec((half_rows, double), lambda n, m: (which, 0)),
            pl.BlockSpec((tokens, step), lambda n, m: (0, n)),
        ],
        [pl.BlockSpec((owned, rank, step), lambda n, m: (0, 0, n))] * 2,
        [out, out],
        scratch=[pltpu.VMEM((tokens, 2 * owned * rank), BF16)],
        after=after,
    )


def add_kernel(count, m, *refs):
    total = refs[0][...].astype(F32)
    for r in refs[1:count]:
        total += r[...].astype(F32)
    for r in refs[count:]:
        r[...] = total.astype(r.dtype)


def add_after(meta, xs, after, kinds=(BF16,), steps=1):
    rows, width = xs[0].shape
    spec = pl.BlockSpec((rows // steps, width), lambda i, m: (i, 0))
    out = call(
        functools.partial(add_kernel, len(xs)),
        meta,
        xs,
        (steps,),
        [spec] * len(xs),
        [spec] * len(kinds),
        [jax.ShapeDtypeStruct((rows, width), k) for k in kinds],
        vmem=16,
        after=after,
    )
    return out if len(kinds) > 1 else out[0]


def final_kernel(m, *refs):
    total = refs[0][...].astype(F32)
    for r in refs[1:-2]:
        total += r[...].astype(F32)
    rows = refs[-1].shape[0]
    refs[-2][...] = total[:rows].astype(BF16)
    refs[-1][...] = total[rows:].astype(BF16)


def final_sum(meta, xs, after):
    rows, width = xs[0].shape
    return call(
        final_kernel,
        meta,
        xs,
        (1,),
        [pl.BlockSpec((rows, width), lambda i, m: (0, 0))] * len(xs),
        [pl.BlockSpec((rows // 2, width), lambda i, m: (0, 0))] * 2,
        [jax.ShapeDtypeStruct((rows // 2, width), BF16)] * 2,
        vmem=16,
        after=after,
    )


def add(*xs):
    return functools.reduce(jnp.add, [x.astype(F32) for x in xs]).astype(BF16)


def tied(x, *others):
    return lax.optimization_barrier((x, *others))[0]


def grid_body(
    cotangent,
    gate_act,
    up_act,
    gate_matrix,
    up_matrix,
    down_matrix,
    adapter_input_factor,
    adapter_output_factor,
    padded_block_segment,
    segment_adapter_index,
    adapter_grad_slot,
):
    adapters = adapter_input_factor.shape[0]
    blocks = gate_act.shape[0] // BLOCK
    d = lax.axis_index("dp")
    t = lax.axis_index("tensor")
    z, y = t // 2, t % 2
    low_side = z < 2
    slots_z = jnp.stack([z, z ^ 1, jnp.where(low_side, 2, 1), jnp.where(low_side, 3, 0)])
    segments_here = lax.dynamic_slice_in_dim(padded_block_segment, d * blocks, blocks)

    def pick(table, index):
        hit = index[:, None] == jnp.arange(table.shape[0], dtype=jnp.int32)[None, :]
        return jnp.sum(jnp.where(hit, table[None, :], 0), axis=1)

    block_adapter = pick(segment_adapter_index[:, 0], segments_here)
    meta = jnp.concatenate(
        [
            jnp.stack([t, y, d]),
            slots_z,
            pick(block_adapter, slots_z),
            block_adapter,
            pick(adapter_grad_slot, block_adapter),
        ]
    ).astype(jnp.int32)
    a_t = jnp.swapaxes(adapter_input_factor, 1, 2)
    send = functools.partial(lax.ppermute, axis_name="tensor")
    swap_cores = functools.partial(lax.ppermute, axis_name="dp", perm=CORES)
    at_end = (z == 0) | (z == 3)

    width = gate_act.shape[1]
    step = width * 2 // 5
    spans = ((0, step, step // 2), (step, step, step // 2), (2 * step, width - 2 * step, width - 2 * step))

    down_other = swap_cores(down_matrix)
    pair = send(cotangent, perm=PAIR)
    mid = send(cotangent, perm=MID)
    y0 = send(cotangent, perm=Y_SWAP)
    hidden, low_in = hidden_and_low_in(meta, gate_act, up_act, a_t)
    y1 = send(tied(pair, y0, low_in), perm=Y_SWAP)
    pair_mid = send(tied(pair, low_in), perm=MID)
    mid_out = send(tied(mid, low_in), perm=OUTWARD)
    slot2 = jnp.where(at_end, mid_out, mid)
    y2 = send(tied(slot2, y1), perm=Y_SWAP)
    far_out = send(pair_mid, perm=OUTWARD)
    hg_near, last = [], (low_in,)
    for span in spans:
        hg_near.append(hidden_grad(meta, (cotangent, y0, pair, y1), down_matrix, down_other, span, last))
        last = (hg_near[-1],)
    slot3 = jnp.where(at_end, tied(far_out, hg_near[0]), pair_mid)
    y3 = send(tied(slot3, y2), perm=Y_SWAP)

    far = (slot2, y2, slot3, y3)
    near = (cotangent, y0, pair, y1)
    columns, low_sum, low = low_parts(meta, near + far, adapter_output_factor, low_in, last)
    hg_far = []
    for perm, span in zip((Y_SWAP, PAIR, FAR), spans):
        got = send(low, perm=perm)
        hg_far.append(hidden_grad(meta, far, down_matrix, down_other, span, (low,)))
        low_sum, low = add_after(meta, (low_sum, got), (hg_far[-1],), (F32, BF16))

    def grads(slot, after):
        hgs = hg_far if slot >= 2 else hg_near
        return act_grad(meta, slot, spans, hgs, gate_act, up_act, low, a_t, after)

    def parts(mine, other, after):
        keep, give = input_grad_parts(meta, mine, other, gate_matrix, up_matrix, after)
        return keep, send(give, perm=Y_SWAP), give

    mine3 = grads(3, ())
    other3 = swap_cores(mine3)
    mine2 = grads(2, (mine3,))
    other2 = swap_cores(tied(mine2, other3))
    keep3, got3, give3 = parts(mine3, other3, (mine2,))
    mine1 = grads(1, (give3,))
    keep2, got2, give2 = parts(mine2, other2, (mine1,))
    other1 = swap_cores(tied(mine1, other2))
    sum3 = add_after(meta, (keep3, got3), (give2,))
    far_in = send(sum3, perm=INWARD)
    mine0 = grads(0, (sum3,))
    keep1, got1, give1 = parts(mine1, other1, (mine0,))
    other0 = swap_cores(tied(mine0, other1))
    sum2 = add_after(meta, (keep2, got2), (give1,))
    mid_in = send(sum2, perm=INWARD)
    sum3 = add_after(meta, (sum3, far_in), (sum2,))
    far_mid = send(sum3, perm=MID)
    keep0, got0, give0 = parts(mine0, other0, (sum3,))
    sum1 = add_after(meta, (keep1, got1, far_mid), (give0,))
    from_pair = send(sum1, perm=PAIR)
    sum2 = add_after(meta, (sum2, mid_in), (sum1,))
    from_mid = send(sum2, perm=MID)
    owned = adapters // 2
    keep_a, give_a = owner_grads(meta, low, 0, hidden, owned, (sum2,))
    keep_b, give_b = owner_grads(meta, low, 1, columns, owned, (keep_a,))
    own, give = final_sum(meta, (keep0, got0, from_pair, from_mid), (keep_b,))
    grad_b = add(keep_b, swap_cores(give_b))
    shape = keep_a.shape
    flat = (shape[0] * shape[1], shape[2])
    grad_a = add_after(
        meta, (keep_a.reshape(flat), swap_cores(give_a).reshape(flat)), (give,), steps=2
    )
    got = swap_cores(give)
    input_grad = jnp.where(
        d == 0, jnp.concatenate([own, got], axis=1), jnp.concatenate([got, own], axis=1)
    )
    grad_a = jnp.swapaxes(grad_a.reshape(shape), 1, 2)
    return (input_grad, grad_a, grad_b)


def body(
    cotangent,
    gate_activation_stored,
    up_activation_stored,
    gate_matrix,
    up_matrix,
    down_matrix,
    adapter_input_factor,
    adapter_output_factor,
    padded_block_segment,
    segment_adapter_index,
    adapter_grad_slot,
):
    local_token_rows = gate_activation_stored.shape[0]
    local_hidden_units = gate_activation_stored.shape[1]
    adapter_list = adapter_input_factor.shape[0]
    local_columns = adapter_output_factor.shape[2]
    seg_count = segment_adapter_index.shape[0]
    block_count = local_token_rows // BLOCK
    dp_index = lax.axis_index("dp")
    tensor_index = lax.axis_index("tensor")
    grad_all = lax.all_gather(cotangent, "tensor", axis=0, tiled=True)
    segments_here = lax.dynamic_slice_in_dim(
        padded_block_segment, dp_index * block_count, block_count
    )
    seg_onehot = (segments_here[:, None] == jnp.arange(seg_count, dtype=jnp.int32)[None, :]).astype(
        jnp.float32
    )
    adapter_onehot = (
        segment_adapter_index[:, 0][:, None] == jnp.arange(adapter_list, dtype=jnp.int32)[None, :]
    ).astype(jnp.float32)
    block_onehot = jnp.dot(seg_onehot, adapter_onehot)
    block_selector = block_onehot.astype(jnp.bfloat16)
    gate = gate_activation_stored.astype(jnp.float32)
    upper = up_activation_stored.astype(jnp.float32)
    sigmoid_gate = jax.nn.sigmoid(gate)
    silu_gate = gate * sigmoid_gate
    hidden_state = (silu_gate * upper).astype(jnp.bfloat16)
    hidden_blocks = hidden_state.reshape(block_count, BLOCK, local_hidden_units)
    cols_mine = lax.dynamic_slice_in_dim(grad_all, tensor_index * local_columns, local_columns, 1)
    cols_blocks = cols_mine.reshape(block_count, BLOCK, local_columns)
    a_blocks = jnp.einsum(
        "yz,zuo->yuo", block_selector, adapter_input_factor, preferred_element_type=jnp.float32
    ).astype(jnp.bfloat16)
    b_blocks = jnp.einsum(
        "vl,lyt->vyt", block_selector, adapter_output_factor, preferred_element_type=jnp.float32
    ).astype(jnp.bfloat16)
    part_in = jnp.einsum(
        "btf,bfr->btr", hidden_blocks, a_blocks, preferred_element_type=jnp.float32
    )
    part_out = jnp.einsum("btc,brc->btr", cols_blocks, b_blocks, preferred_element_type=jnp.float32)
    lowrank_input, lowrank_output = lax.psum((part_in, part_out), "tensor")
    lowrank_input = lowrank_input.astype(jnp.bfloat16)
    lowrank_output = lowrank_output.astype(jnp.bfloat16)
    gate_full, up_full, down_full = (
        lax.all_gather(gate_matrix, "dp", axis=0, tiled=True),
        lax.all_gather(up_matrix, "dp", axis=0, tiled=True),
        lax.all_gather(down_matrix, "dp", axis=0, tiled=True),
    )
    hidden_gradient = jnp.dot(grad_all, down_full, preferred_element_type=jnp.float32)
    additional_term = jnp.einsum(
        "btr,bfr->btf", lowrank_output, a_blocks, preferred_element_type=jnp.float32
    )
    hidden_gradient = hidden_gradient + ADAPTER_SCALE * additional_term.reshape(
        local_token_rows, local_hidden_units
    )
    gate_grad = (
        hidden_gradient * upper * sigmoid_gate * (1.0 + gate * (1.0 - sigmoid_gate))
    ).astype(jnp.bfloat16)
    up_grad = (hidden_gradient * silu_gate).astype(jnp.bfloat16)
    outer_product_input = jnp.einsum(
        "btf,btr->bfr", hidden_blocks, lowrank_output, preferred_element_type=jnp.float32
    )
    outer_product_output = jnp.einsum(
        "btr,btc->brc", lowrank_input, cols_blocks, preferred_element_type=jnp.float32
    )
    slot_onehot = (
        jnp.arange(adapter_list, dtype=jnp.int32)[:, None] == adapter_grad_slot[None, :]
    ).astype(jnp.float32)
    slot_block_mask = jnp.dot(slot_onehot, block_onehot.T)
    input_factor_terms = ADAPTER_SCALE * jnp.einsum(
        "pc,cdw->pdw", slot_block_mask, outer_product_input
    )
    output_factor_terms = ADAPTER_SCALE * jnp.einsum(
        "fn,nlv->flv", slot_block_mask, outer_product_output
    )
    owned_a, owned_b = (
        lax.psum_scatter(input_factor_terms, "dp", scatter_dimension=0, tiled=True),
        lax.psum_scatter(output_factor_terms, "dp", scatter_dimension=0, tiled=True),
    )
    grad_a = owned_a.astype(jnp.bfloat16)
    grad_b = owned_b.astype(jnp.bfloat16)
    first = lax.dot_general(
        gate_grad, gate_full, (((1,), (1,)), ((), ())), preferred_element_type=jnp.float32
    )
    second = lax.dot_general(
        up_grad, up_full, (((1,), (1,)), ((), ())), preferred_element_type=jnp.float32
    )
    summed = lax.psum_scatter(first + second, "tensor", scatter_dimension=0, tiled=True)
    input_grad = summed.astype(jnp.bfloat16)
    return (input_grad, grad_a, grad_b)


def solution(mesh):
    return jax.shard_map(
        grid_body if mesh.shape["tensor"] == 8 and mesh.shape["dp"] == 2 else body,
        mesh=mesh,
        in_specs=(
            P(("groups", "dp", "tensor"), None),
            P(("groups", "dp"), "tensor"),
            P(("groups", "dp"), "tensor"),
            P("dp", "tensor"),
            P("dp", "tensor"),
            P("dp", "tensor"),
            P(None, "tensor", None),
            P(None, None, "tensor"),
            P("groups"),
            P("groups", None),
            P(),
        ),
        out_specs=(
            P(("groups", "dp", "tensor"), None),
            P(("groups", "dp"), "tensor", None),
            P(("groups", "dp"), None, "tensor"),
        ),
        check_vma=False,
    )
```

```python
import functools

import jax
import jax.numpy as jnp
from jax import lax
from jax.experimental import pallas as pl
from jax.experimental.pallas import tpu as pltpu
from jax.sharding import PartitionSpec as P

BLOCK = 128


ADAPTER_SCALE = 2.0

F32 = jnp.float32
BF16 = jnp.bfloat16
MIB = 1024 * 1024

Y_SWAP = [(t, t ^ 1) for t in range(8)]
PAIR = [(t, t ^ 2) for t in range(8)]
FAR = [(t, t ^ 4) for t in range(8)]
MID = [(2, 4), (3, 5), (4, 2), (5, 3)]
OUTWARD = [(2, 0), (3, 1), (4, 6), (5, 7)]
INWARD = [(0, 2), (1, 3), (6, 4), (7, 5)]
CORES = [(0, 1), (1, 0)]

M_T, M_Y, M_D, M_Z, M_SLOT_ADAPTER, M_ADAPTER, M_GRAD_SLOT = 0, 1, 2, 3, 7, 11, 15


def nt_dot(a, b):
    return lax.dot_general(a, b, (((1,), (1,)), ((), ())), preferred_element_type=F32)


def tn_dot(a, b):
    return lax.dot_general(a, b, (((0,), (0,)), ((), ())), preferred_element_type=F32)


def call(
    kernel, meta, args, grid, in_specs, out_specs, out_shape, scratch=(), vmem=24, after=(), cost=(1000, 1000)
):
    first, extra = len(args), len(after)

    def run(m, *refs):
        kernel(m, *refs[:first], *refs[first + extra :])

    return pl.pallas_call(
        run,
        grid_spec=pltpu.PrefetchScalarGridSpec(
            num_scalar_prefetch=1,
            grid=grid,
            in_specs=list(in_specs) + [pl.BlockSpec(memory_space=pl.ANY)] * extra,
            out_specs=out_specs,
            scratch_shapes=list(scratch),
        ),
        out_shape=out_shape,
        compiler_params=pltpu.CompilerParams(vmem_limit_bytes=vmem * MIB),
        cost_estimate=pl.CostEstimate(flops=cost[0], bytes_accessed=cost[1], transcendentals=0),
    )(meta, *args, *after)


def pack_halves(p):
    h = p.shape[0] // 2
    return jnp.concatenate([p[:h], p[h:]], axis=1)


def unpack_halves(p):
    h = p.shape[1] // 2
    return jnp.concatenate([p[:, :h], p[:, h:]], axis=0)


def hidden_kernel(m, gate_ref, up_ref, a_ref, hidden_ref, low_ref):
    g = gate_ref[...].astype(F32)
    hidden = (g * jax.nn.sigmoid(g) * up_ref[...].astype(F32)).astype(BF16)
    hidden_ref[...] = hidden
    low_ref[...] = pack_halves(nt_dot(hidden, a_ref[0]))


def hidden_and_low_in(meta, gate_act, up_act, a_t):
    rows, width = gate_act.shape
    rank = a_t.shape[1]
    blocks = rows // BLOCK
    return call(
        hidden_kernel,
        meta,
        (gate_act, up_act, a_t),
        (blocks,),
        [
            pl.BlockSpec((BLOCK, width), lambda b, m: (b, 0)),
            pl.BlockSpec((BLOCK, width), lambda b, m: (b, 0)),
            pl.BlockSpec((1, rank, width), lambda b, m: (m[M_ADAPTER + b], 0, 0)),
        ],
        [
            pl.BlockSpec((BLOCK, width), lambda b, m: (b, 0)),
            pl.BlockSpec((BLOCK // 2, 2 * rank), lambda b, m: (b, 0)),
        ],
        [
            jax.ShapeDtypeStruct((rows, width), BF16),
            jax.ShapeDtypeStruct((rows // 2, 2 * rank), F32),
        ],
        vmem=56,
    )


def low_out_kernel(m, *refs):
    shards, b_ref, low_in_ref = refs[:8], refs[8], refs[9]
    cols_ref, full_ref, short_ref = refs[10:]
    rows = shards[0].shape[0]
    y = m[M_Y]
    for s in range(4):
        z = m[M_Z + s]
        own, other = shards[2 * s][...], shards[2 * s + 1][...]
        first = jnp.where(y == 0, own, other)
        second = jnp.where(y == 0, other, own)
        tokens = jnp.concatenate([first, second], axis=0)
        cols_ref[pl.ds(pl.multiple_of(z * 2 * rows, 2 * rows), 2 * rows), :] = tokens
        part = pack_halves(nt_dot(tokens, b_ref[m[M_SLOT_ADAPTER + s]]))
        at = pl.ds(pl.multiple_of(z * rows, rows), rows)
        full_ref[at, :] = part
        short_ref[at, :] = part.astype(BF16)
    full_ref[4 * rows :] = low_in_ref[...]
    short_ref[4 * rows :] = low_in_ref[...].astype(BF16)


def low_parts(meta, shards, b, low_in, after):
    rows = shards[0].shape[0]
    adapters, rank, columns = b.shape
    out = (8 * rows, 2 * rank)
    return call(
        low_out_kernel,
        meta,
        (*shards, b, low_in),
        (1,),
        [pl.BlockSpec((rows, columns), lambda i, m: (0, m[M_T]))] * 8
        + [pl.BlockSpec((adapters, rank, columns), lambda i, m: (0, 0, 0))]
        + [pl.BlockSpec((4 * rows, 2 * rank), lambda i, m: (0, 0))],
        [pl.BlockSpec((8 * rows, columns), lambda i, m: (0, 0))]
        + [pl.BlockSpec(out, lambda i, m: (0, 0))] * 2,
        [
            jax.ShapeDtypeStruct((8 * rows, columns), BF16),
            jax.ShapeDtypeStruct(out, F32),
            jax.ShapeDtypeStruct(out, BF16),
        ],
        after=after,
    )


def hidden_grad_kernel(count, m, *refs):
    mine, other = refs[:count], refs[count : 2 * count]
    down_mine, down_other, out_ref, lhs = refs[2 * count :]
    rows = mine[0].shape[0]

    @pl.when(pl.program_id(0) == 0)
    def _():
        for s in range(count):
            lhs[0, s * rows : (s + 1) * rows] = mine[s][...]
            lhs[1, s * rows : (s + 1) * rows] = other[s][...]

    total = jnp.dot(lhs[0], down_mine[...], preferred_element_type=F32)
    out_ref[...] = total + jnp.dot(lhs[1], down_other[...], preferred_element_type=F32)


def hidden_grad(meta, shards, mine, other, span, after=()):
    rows = shards[0].shape[0]
    half = mine.shape[0]
    start, width, step = span
    count = len(shards)
    total = rows * count
    return call(
        functools.partial(hidden_grad_kernel, count),
        meta,
        (*shards, *shards, mine, other),
        (width // step,),
        [pl.BlockSpec((rows, half), lambda n, m: (0, m[M_D]))] * count
        + [pl.BlockSpec((rows, half), lambda n, m: (0, 1 - m[M_D]))] * count
        + [pl.BlockSpec((half, step), lambda n, m: (0, n + start // step))] * 2,
        pl.BlockSpec((total, step), lambda n, m: (0, n)),
        jax.ShapeDtypeStruct((total, width), F32),
        scratch=[pltpu.VMEM((2, total, half), BF16)],
        after=after,
    )


def act_grad_kernel(spans, m, *refs):
    hg_refs, (gate_ref, up_ref, low_ref, a_ref, out_ref) = refs[: len(spans)], refs[len(spans) :]
    j = pl.program_id(0)
    y = m[M_Y]
    rank = low_ref.shape[1] // 2
    second = jnp.where(j == 0, y, 1 - y) == 1
    low = jnp.where(second, low_ref[:, rank:], low_ref[:, :rank])
    for hg_ref, (start, width, _) in zip(hg_refs, spans):
        at = slice(start, start + width)
        hg = hg_ref[...] + ADAPTER_SCALE * jnp.dot(low, a_ref[0, :, at], preferred_element_type=F32)
        g = gate_ref[:, at].astype(F32)
        u = up_ref[:, at].astype(F32)
        sig = jax.nn.sigmoid(g)
        out_ref[0, :, at] = (hg * u * sig * (1.0 + g * (1.0 - sig))).astype(BF16)
        out_ref[1, :, at] = (hg * (g * sig)).astype(BF16)


def act_grad(meta, slot, spans, hgs, gate_act, up_act, low, a_t, after=()):
    rank, width = a_t.shape[1:]
    rows = BLOCK // 2

    def shard_of(j, m):
        y = m[M_Y]
        return (m[M_Z + slot] * 2 + y + j * (1 - 2 * y), 0)

    return call(
        functools.partial(act_grad_kernel, spans),
        meta,
        (*hgs, gate_act, up_act, low, a_t),
        (2,),
        [pl.BlockSpec((rows, w), lambda j, m: ((slot % 2) * 2 + j, 0)) for _, w, _ in spans]
        + [
            pl.BlockSpec((rows, width), shard_of),
            pl.BlockSpec((rows, width), shard_of),
            pl.BlockSpec((rows, 2 * rank), lambda j, m: (m[M_Z + slot], 0)),
            pl.BlockSpec((1, rank, width), lambda j, m: (m[M_SLOT_ADAPTER + slot], 0, 0)),
        ],
        pl.BlockSpec((2, rows, width), lambda j, m: (0, j, 0)),
        jax.ShapeDtypeStruct((2, 2 * rows, width), BF16),
        after=after,
    )


def input_grad_kernel(m, mine_ref, other_ref, gate_ref, up_ref, keep_ref, send_ref, lhs):
    rows = mine_ref.shape[1] // 2

    @pl.when(pl.program_id(0) == 0)
    def _():
        for i in range(2):
            for y in range(2):
                lhs[i, (2 * y) * rows : (2 * y + 1) * rows] = mine_ref[i, y * rows : (y + 1) * rows]
                lhs[i, (2 * y + 1) * rows : (2 * y + 2) * rows] = other_ref[i, y * rows : (y + 1) * rows]

    total = nt_dot(lhs[0], gate_ref[...]) + nt_dot(lhs[1], up_ref[...])
    keep_ref[...] = total[: 2 * rows].astype(BF16)
    send_ref[...] = total[2 * rows :].astype(BF16)


def input_grad_parts(meta, mine, other, gate, up, after=()):
    rows, width = mine.shape[1:]
    half = gate.shape[0]
    step = 512
    out = jax.ShapeDtypeStruct((rows, half), BF16)
    return call(
        input_grad_kernel,
        meta,
        (mine, other, gate, up),
        (half // step,),
        [pl.BlockSpec((2, rows, width), lambda n, m: (0, 0, 0))] * 2
        + [pl.BlockSpec((step, width), lambda n, m: (n, 0))] * 2,
        [pl.BlockSpec((rows, step), lambda n, m: (0, n))] * 2,
        [out, out],
        scratch=[pltpu.VMEM((2, 2 * rows, width), BF16)],
        after=after,
    )


def owner_kernel(m, low_ref, features_ref, keep_ref, send_ref, lhs):
    owned, rank = keep_ref.shape[:2]
    blocks = features_ref.shape[0] // BLOCK
    rows = low_ref.shape[0] // blocks
    d = m[M_D]

    @pl.when(pl.program_id(0) == 0)
    def _():
        for b in range(blocks):
            low = unpack_halves(low_ref[b * rows : (b + 1) * rows, :])
            masked = []
            for owner in (d, 1 - d):
                for i in range(owned):
                    hit = m[M_GRAD_SLOT + b] == owner * owned + i
                    masked.append(jnp.where(hit, low, jnp.zeros_like(low)))
            lhs[b * BLOCK : (b + 1) * BLOCK] = jnp.concatenate(masked, axis=1)

    total = (ADAPTER_SCALE * tn_dot(lhs[...], features_ref[...])).astype(BF16)
    for i in range(owned):
        keep_ref[i] = total[i * rank : (i + 1) * rank]
        send_ref[i] = total[(owned + i) * rank : (owned + i + 1) * rank]


def owner_grads(meta, low, which, features, owned, after=()):
    tokens, width = features.shape
    half_rows, double = low.shape[0] // 2, low.shape[1]
    rank = double // 2
    step = 640
    out = jax.ShapeDtypeStruct((owned, rank, width), BF16)
    return call(
        owner_kernel,
        meta,
        (low, features),
        (width // step,),
        [
            pl.BlockSpec((half_rows, double), lambda n, m: (which, 0)),
            pl.BlockSpec((tokens, step), lambda n, m: (0, n)),
        ],
        [pl.BlockSpec((owned, rank, step), lambda n, m: (0, 0, n))] * 2,
        [out, out],
        scratch=[pltpu.VMEM((tokens, 2 * owned * rank), BF16)],
        after=after,
    )


def add_kernel(count, m, *refs):
    total = refs[0][...].astype(F32)
    for r in refs[1:count]:
        total += r[...].astype(F32)
    for r in refs[count:]:
        r[...] = total.astype(r.dtype)


def add_after(meta, xs, after, kinds=(BF16,), steps=1):
    rows, width = xs[0].shape
    spec = pl.BlockSpec((rows // steps, width), lambda i, m: (i, 0))
    out = call(
        functools.partial(add_kernel, len(xs)),
        meta,
        xs,
        (steps,),
        [spec] * len(xs),
        [spec] * len(kinds),
        [jax.ShapeDtypeStruct((rows, width), k) for k in kinds],
        vmem=16,
        after=after,
    )
    return out if len(kinds) > 1 else out[0]


def final_kernel(m, *refs):
    total = refs[0][...].astype(F32)
    for r in refs[1:-2]:
        total += r[...].astype(F32)
    rows = refs[-1].shape[0]
    refs[-2][...] = total[:rows].astype(BF16)
    refs[-1][...] = total[rows:].astype(BF16)


def final_sum(meta, xs, after):
    rows, width = xs[0].shape
    return call(
        final_kernel,
        meta,
        xs,
        (1,),
        [pl.BlockSpec((rows, width), lambda i, m: (0, 0))] * len(xs),
        [pl.BlockSpec((rows // 2, width), lambda i, m: (0, 0))] * 2,
        [jax.ShapeDtypeStruct((rows // 2, width), BF16)] * 2,
        vmem=16,
        after=after,
    )


def add(*xs):
    return functools.reduce(jnp.add, [x.astype(F32) for x in xs]).astype(BF16)


def tied(x, *others):
    return lax.optimization_barrier((x, *others))[0]


def grid_body(
    cotangent,
    gate_act,
    up_act,
    gate_matrix,
    up_matrix,
    down_matrix,
    adapter_input_factor,
    adapter_output_factor,
    padded_block_segment,
    segment_adapter_index,
    adapter_grad_slot,
):
    adapters = adapter_input_factor.shape[0]
    blocks = gate_act.shape[0] // BLOCK
    d = lax.axis_index("dp")
    t = lax.axis_index("tensor")
    z, y = t // 2, t % 2
    low_side = z < 2
    slots_z = jnp.stack([z, z ^ 1, jnp.where(low_side, 2, 1), jnp.where(low_side, 3, 0)])
    segments_here = lax.dynamic_slice_in_dim(padded_block_segment, d * blocks, blocks)

    def pick(table, index):
        hit = index[:, None] == jnp.arange(table.shape[0], dtype=jnp.int32)[None, :]
        return jnp.sum(jnp.where(hit, table[None, :], 0), axis=1)

    block_adapter = pick(segment_adapter_index[:, 0], segments_here)
    meta = jnp.concatenate(
        [
            jnp.stack([t, y, d]),
            slots_z,
            pick(block_adapter, slots_z),
            block_adapter,
            pick(adapter_grad_slot, block_adapter),
        ]
    ).astype(jnp.int32)
    a_t = jnp.swapaxes(adapter_input_factor, 1, 2)
    send = functools.partial(lax.ppermute, axis_name="tensor")
    swap_cores = functools.partial(lax.ppermute, axis_name="dp", perm=CORES)
    at_end = (z == 0) | (z == 3)

    width = gate_act.shape[1]
    step = width * 2 // 5
    spans = ((0, step, step // 2), (step, step, step // 2), (2 * step, width - 2 * step, width - 2 * step))

    down_other = swap_cores(down_matrix)
    pair = send(cotangent, perm=PAIR)
    mid = send(cotangent, perm=MID)
    y0 = send(cotangent, perm=Y_SWAP)
    hidden, low_in = hidden_and_low_in(meta, gate_act, up_act, a_t)
    y1 = send(tied(pair, y0, low_in), perm=Y_SWAP)
    pair_mid = send(tied(pair, low_in), perm=MID)
    mid_out = send(tied(mid, low_in), perm=OUTWARD)
    slot2 = jnp.where(at_end, mid_out, mid)
    y2 = send(tied(slot2, y1), perm=Y_SWAP)
    far_out = send(pair_mid, perm=OUTWARD)
    hg_near, last = [], (low_in,)
    for span in spans:
        hg_near.append(hidden_grad(meta, (cotangent, y0, pair, y1), down_matrix, down_other, span, last))
        last = (hg_near[-1],)
    slot3 = jnp.where(at_end, tied(far_out, hg_near[0]), pair_mid)
    y3 = send(tied(slot3, y2), perm=Y_SWAP)

    far = (slot2, y2, slot3, y3)
    near = (cotangent, y0, pair, y1)
    columns, low_sum, low = low_parts(meta, near + far, adapter_output_factor, low_in, last)
    hg_far = []
    for perm, span in zip((Y_SWAP, PAIR, FAR), spans):
        got = send(low, perm=perm)
        hg_far.append(hidden_grad(meta, far, down_matrix, down_other, span, (low,)))
        low_sum, low = add_after(meta, (low_sum, got), (hg_far[-1],), (F32, BF16))

    def grads(slot, after):
        hgs = hg_far if slot >= 2 else hg_near
        return act_grad(meta, slot, spans, hgs, gate_act, up_act, low, a_t, after)

    def parts(mine, other, after):
        keep, give = input_grad_parts(meta, mine, other, gate_matrix, up_matrix, after)
        return keep, send(give, perm=Y_SWAP), give

    mine3 = grads(3, ())
    other3 = swap_cores(mine3)
    mine2 = grads(2, (mine3,))
    other2 = swap_cores(tied(mine2, other3))
    keep3, got3, give3 = parts(mine3, other3, (mine2,))
    mine1 = grads(1, (give3,))
    keep2, got2, give2 = parts(mine2, other2, (mine1,))
    other1 = swap_cores(tied(mine1, other2))
    sum3 = add_after(meta, (keep3, got3), (give2,))
    far_in = send(sum3, perm=INWARD)
    mine0 = grads(0, (sum3,))
    keep1, got1, give1 = parts(mine1, other1, (mine0,))
    other0 = swap_cores(tied(mine0, other1))
    sum2 = add_after(meta, (keep2, got2), (give1,))
    mid_in = send(sum2, perm=INWARD)
    sum3 = add_after(meta, (sum3, far_in), (sum2,))
    far_mid = send(sum3, perm=MID)
    keep0, got0, give0 = parts(mine0, other0, (sum3,))
    sum1 = add_after(meta, (keep1, got1, far_mid), (give0,))
    from_pair = send(sum1, perm=PAIR)
    sum2 = add_after(meta, (sum2, mid_in), (sum1,))
    from_mid = send(sum2, perm=MID)
    owned = adapters // 2
    keep_a, give_a = owner_grads(meta, low, 0, hidden, owned, (sum2,))
    keep_b, give_b = owner_grads(meta, low, 1, columns, owned, (keep_a,))
    own, give = final_sum(meta, (keep0, got0, from_pair, from_mid), (keep_b,))
    grad_b = add(keep_b, swap_cores(give_b))
    shape = keep_a.shape
    flat = (shape[0] * shape[1], shape[2])
    grad_a = add_after(
        meta, (keep_a.reshape(flat), swap_cores(give_a).reshape(flat)), (give,), steps=2
    )
    got = swap_cores(give)
    input_grad = jnp.where(
        d == 0, jnp.concatenate([own, got], axis=1), jnp.concatenate([got, own], axis=1)
    )
    grad_a = jnp.swapaxes(grad_a.reshape(shape), 1, 2)
    return (input_grad, grad_a, grad_b)


def body(
    cotangent,
    gate_activation_stored,
    up_activation_stored,
    gate_matrix,
    up_matrix,
    down_matrix,
    adapter_input_factor,
    adapter_output_factor,
    padded_block_segment,
    segment_adapter_index,
    adapter_grad_slot,
):
    local_token_rows = gate_activation_stored.shape[0]
    local_hidden_units = gate_activation_stored.shape[1]
    adapter_list = adapter_input_factor.shape[0]
    local_columns = adapter_output_factor.shape[2]
    seg_count = segment_adapter_index.shape[0]
    block_count = local_token_rows // BLOCK
    dp_index = lax.axis_index("dp")
    tensor_index = lax.axis_index("tensor")
    grad_all = lax.all_gather(cotangent, "tensor", axis=0, tiled=True)
    segments_here = lax.dynamic_slice_in_dim(
        padded_block_segment, dp_index * block_count, block_count
    )
    seg_onehot = (segments_here[:, None] == jnp.arange(seg_count, dtype=jnp.int32)[None, :]).astype(
        jnp.float32
    )
    adapter_onehot = (
        segment_adapter_index[:, 0][:, None] == jnp.arange(adapter_list, dtype=jnp.int32)[None, :]
    ).astype(jnp.float32)
    block_onehot = jnp.dot(seg_onehot, adapter_onehot)
    block_selector = block_onehot.astype(jnp.bfloat16)
    gate = gate_activation_stored.astype(jnp.float32)
    upper = up_activation_stored.astype(jnp.float32)
    sigmoid_gate = jax.nn.sigmoid(gate)
    silu_gate = gate * sigmoid_gate
    hidden_state = (silu_gate * upper).astype(jnp.bfloat16)
    hidden_blocks = hidden_state.reshape(block_count, BLOCK, local_hidden_units)
    cols_mine = lax.dynamic_slice_in_dim(grad_all, tensor_index * local_columns, local_columns, 1)
    cols_blocks = cols_mine.reshape(block_count, BLOCK, local_columns)
    a_blocks = jnp.einsum(
        "yz,zuo->yuo", block_selector, adapter_input_factor, preferred_element_type=jnp.float32
    ).astype(jnp.bfloat16)
    b_blocks = jnp.einsum(
        "vl,lyt->vyt", block_selector, adapter_output_factor, preferred_element_type=jnp.float32
    ).astype(jnp.bfloat16)
    part_in = jnp.einsum(
        "btf,bfr->btr", hidden_blocks, a_blocks, preferred_element_type=jnp.float32
    )
    part_out = jnp.einsum("btc,brc->btr", cols_blocks, b_blocks, preferred_element_type=jnp.float32)
    lowrank_input, lowrank_output = lax.psum((part_in, part_out), "tensor")
    lowrank_input = lowrank_input.astype(jnp.bfloat16)
    lowrank_output = lowrank_output.astype(jnp.bfloat16)
    gate_full, up_full, down_full = (
        lax.all_gather(gate_matrix, "dp", axis=0, tiled=True),
        lax.all_gather(up_matrix, "dp", axis=0, tiled=True),
        lax.all_gather(down_matrix, "dp", axis=0, tiled=True),
    )
    hidden_gradient = jnp.dot(grad_all, down_full, preferred_element_type=jnp.float32)
    additional_term = jnp.einsum(
        "btr,bfr->btf", lowrank_output, a_blocks, preferred_element_type=jnp.float32
    )
    hidden_gradient = hidden_gradient + ADAPTER_SCALE * additional_term.reshape(
        local_token_rows, local_hidden_units
    )
    gate_grad = (
        hidden_gradient * upper * sigmoid_gate * (1.0 + gate * (1.0 - sigmoid_gate))
    ).astype(jnp.bfloat16)
    up_grad = (hidden_gradient * silu_gate).astype(jnp.bfloat16)
    outer_product_input = jnp.einsum(
        "btf,btr->bfr", hidden_blocks, lowrank_output, preferred_element_type=jnp.float32
    )
    outer_product_output = jnp.einsum(
        "btr,btc->brc", lowrank_input, cols_blocks, preferred_element_type=jnp.float32
    )
    slot_onehot = (
        jnp.arange(adapter_list, dtype=jnp.int32)[:, None] == adapter_grad_slot[None, :]
    ).astype(jnp.float32)
    slot_block_mask = jnp.dot(slot_onehot, block_onehot.T)
    input_factor_terms = ADAPTER_SCALE * jnp.einsum(
        "pc,cdw->pdw", slot_block_mask, outer_product_input
    )
    output_factor_terms = ADAPTER_SCALE * jnp.einsum(
        "fn,nlv->flv", slot_block_mask, outer_product_output
    )
    owned_a, owned_b = (
        lax.psum_scatter(input_factor_terms, "dp", scatter_dimension=0, tiled=True),
        lax.psum_scatter(output_factor_terms, "dp", scatter_dimension=0, tiled=True),
    )
    grad_a = owned_a.astype(jnp.bfloat16)
    grad_b = owned_b.astype(jnp.bfloat16)
    first = lax.dot_general(
        gate_grad, gate_full, (((1,), (1,)), ((), ())), preferred_element_type=jnp.float32
    )
    second = lax.dot_general(
        up_grad, up_full, (((1,), (1,)), ((), ())), preferred_element_type=jnp.float32
    )
    summed = lax.psum_scatter(first + second, "tensor", scatter_dimension=0, tiled=True)
    input_grad = summed.astype(jnp.bfloat16)
    return (input_grad, grad_a, grad_b)


def solution(mesh):
    return jax.shard_map(
        grid_body if mesh.shape["tensor"] == 8 and mesh.shape["dp"] == 2 else body,
        mesh=mesh,
        in_specs=(
            P(("groups", "dp", "tensor"), None),
            P(("groups", "dp"), "tensor"),
            P(("groups", "dp"), "tensor"),
            P("dp", "tensor"),
            P("dp", "tensor"),
            P("dp", "tensor"),
            P(None, "tensor", None),
            P(None, None, "tensor"),
            P("groups"),
            P("groups", None),
            P(),
        ),
        out_specs=(
            P(("groups", "dp", "tensor"), None),
            P(("groups", "dp"), "tensor", None),
            P(("groups", "dp"), None, "tensor"),
        ),
        check_vma=False,
    )
```
